32 devices in a mesh: dp: 2 (over core), dq: 16 (over z, y, x).
Axes of the slice: x: 2, y: 2, z: 4, core: 2. Of those that a mesh axis runs over, the one named last changes fastest.
Arguments:
- tokens: bfloat16 [65536, 512], P(('dp', 'dq')), may hold values from -6 to 6
- out_grad: bfloat16 [65536, 512], P(('dp', 'dq')), may hold values from -6 to 6
- context_len: int32 [32, 8], P(('dp', 'dq')), may hold values from 0 to 1000, as said below
- query_count: int32 [32, 8], P(('dp', 'dq')), may hold values from 0 to 100, as said below
- w_query: bfloat16 [512, 512], replicated, may hold values from -0.25 to 0.25
- w_key: bfloat16 [512, 512], replicated, may hold values from -0.25 to 0.25
- w_value: bfloat16 [512, 512], replicated, may hold values from -0.25 to 0.25
- b_query: float32 [512], replicated, may hold values from -3 to 3
- b_value: float32 [512], replicated, may hold values from -3 to 3
- w_out: bfloat16 [512, 512], replicated, may hold values from -2.5 to 2.5
- b_out: float32 [512], replicated, may hold values from -2 to 2
- norm1_gain: float32 [512], replicated, may hold values from 0.5 to 1.5
- norm1_bias: float32 [512], replicated, may hold values from -2 to 2
- w_hidden: bfloat16 [512, 1024], replicated, may hold values from -0.25 to 0.25
- b_hidden: float32 [1024], replicated, may hold values from -3 to 3
- w_back: bfloat16 [1024, 512], replicated, may hold values from -0.1875 to 0.1875
- b_back: float32 [512], replicated, may hold values from -2 to 2
- norm2_gain: float32 [512], replicated, may hold values from 0.5 to 1.5
- norm2_bias: float32 [512], replicated, may hold values from -2 to 2
Outputs:
- output: bfloat16 [65536, 512], P(('dp', 'dq'))
- input_grad: bfloat16 [65536, 512], P(('dp', 'dq'))
- grad_w_query: float32 [512, 512], replicated
- grad_w_key: float32 [512, 512], replicated
- grad_w_value: float32 [512, 512], replicated
- grad_b_query: float32 [512], replicated
- grad_b_value: float32 [512], replicated
- grad_w_out: float32 [512, 512], replicated
- grad_b_out: float32 [512], replicated
- grad_norm1_gain: float32 [512], replicated
- grad_norm1_bias: float32 [512], replicated
- grad_w_hidden: float32 [512, 1024], replicated
- grad_b_hidden: float32 [1024], replicated
- grad_w_back: float32 [1024, 512], replicated
- grad_b_back: float32 [512], replicated
- grad_norm2_gain: float32 [512], replicated
- grad_norm2_bias: float32 [512], replicated
The draws below stay inside these ranges and needn't reach their ends.
Inputs may be any that keep to these rules, and one draw needn't show every extreme that they name: `context_len`: row r describes device r's slots in the order in which their rows lie; a slot with 0 context rows has 0 query rows, and so have all later slots of that row; a non-empty slot has 100 or more context rows and 1 or more query rows; slot 0 is never empty; the context and query rows of one device add up to at most 2048; some slot has exactly 1000 context rows. `query_count`: A slot has 0 query rows exactly when it has 0 context rows; some slot has exactly 100 query rows.
All inputs are finite; a program needn't handle non-finite values.
Results may differ from the reference program's by a relative error of at most 0.014.
The reference program's roundings to bfloat16 on the way count: a program that leaves them out, or rounds other values in their place, can miss the bound.
Values sent between devices are 32-bit elements; how exact they have to be, the bound alone decides.
No kernel may reach another device: no remote copies, remote signals or barrier semaphores. Data moves between devices by JAX's collectives and lax.ppermute only.
A program may use at most 192 MiB of HBM per device.

```python
import math
import jax
import jax.numpy as jnp
from jax import lax

D = 512
HEADS = 4
HEAD_DIM = 128
FF = 1024
TOK_DEV = 2048
SLOTS = 8
CTX_LEAST = 100
CTX_MOST = 1000
QRY_MOST = 100
SHARDS = 32
TOKENS = 65536


def slot_lengths(key):
    key_roll, key_query, key_device = jax.random.split(key, 3)
    roll = jax.random.randint(key_roll, (SHARDS, SLOTS), 0, 1000)
    span = CTX_MOST - CTX_LEAST
    context = CTX_LEAST + roll * roll // 1000 * roll // 1000 * span // 1000
    queries = jax.random.randint(key_query, (SHARDS, SLOTS), 1, QRY_MOST + 1)
    chosen = jax.random.randint(key_device, (), 0, SHARDS)
    device_rows = lax.broadcasted_iota(jnp.int32, (SHARDS, SLOTS), 0)
    slot_cols = lax.broadcasted_iota(jnp.int32, (SHARDS, SLOTS), 1)
    forced = (device_rows == chosen) & (slot_cols == 0)
    context = jnp.where(forced, CTX_MOST, context).astype(jnp.int32)
    queries = jnp.where(forced, QRY_MOST, queries).astype(jnp.int32)
    slot_ends = jnp.cumsum(context + queries, axis=1).astype(jnp.int32)
    fitting = slot_ends <= TOK_DEV
    return (jnp.where(fitting, context, 0).astype(jnp.int32), jnp.where(fitting, queries, 0).astype(jnp.int32))


def draw_context_len(key, part):
    return slot_lengths(key)[0]


def draw_query_count(key, part):
    return slot_lengths(key)[1]


def levels(stream_key, extent, shards, smallest, top_value):
    def one(dim, blocks):
        steps = jax.random.uniform(jax.random.fold_in(jax.random.fold_in(stream_key, 6), dim), (blocks,), jnp.float32, smallest / len(shards), top_value / len(shards))
        return jnp.repeat(jnp.exp(steps), extent[dim] // blocks).reshape((-1,) + (1,) * (len(extent) - dim - 1))

    gain = one(*shards[0])
    for cut in shards[1:]:
        gain = gain * one(*cut)
    return gain


def scatter_about(rng, shape, scale, limit, cuts=(), kind=jnp.bfloat16):
    result = jax.random.normal(rng, shape, jnp.float32) * scale
    if len(cuts) > 0:
        result = levels(rng, shape, cuts, -0.22, 0.18) * result
    return jnp.clip(result, min=-limit, max=limit).astype(kind)


def setup_inputs(seed: int = 0) -> dict:
    seeds = jax.random.split(jax.random.key(seed), 20)
    return {
        "tokens": scatter_about(seeds[0], (TOKENS, D), 1.0, 6.0, ((0, 32),)),
        "out_grad": scatter_about(seeds[1], (TOKENS, D), 1.0, 6.0, ((0, 32),)),
        "context_len": draw_context_len(jax.random.fold_in(seeds[19], 71), 0),
        "query_count": draw_query_count(jax.random.fold_in(seeds[19], 71), 0),
        "w_query": scatter_about(seeds[4], (D, D), D ** -0.5, 0.25),
        "w_key": scatter_about(seeds[5], (D, D), D ** -0.5, 0.25),
        "w_value": scatter_about(seeds[6], (D, D), D ** -0.5, 0.25),
        "b_query": scatter_about(seeds[7], (D,), 0.5, 3.0, (), jnp.float32),
        "b_value": scatter_about(seeds[8], (D,), 0.5, 3.0, (), jnp.float32),
        "w_out": scatter_about(seeds[9], (D, D), (D * 16 // (CTX_MOST + 4 * CTX_LEAST)) ** -0.5, 2.5),
        "b_out": scatter_about(seeds[10], (D,), 0.3, 2.0, (), jnp.float32),
        "norm1_gain": jnp.clip(1.0 + 0.1 * jax.random.normal(seeds[11], (D,), jnp.float32), 0.5, 1.5),
        "norm1_bias": scatter_about(seeds[12], (D,), 0.3, 2.0, (), jnp.float32),
        "w_hidden": scatter_about(seeds[13], (D, FF), D ** -0.5, 0.25),
        "b_hidden": scatter_about(seeds[14], (FF,), 0.5, 3.0, (), jnp.float32),
        "w_back": scatter_about(seeds[15], (FF, D), FF ** -0.5, 0.1875),
        "b_back": scatter_about(seeds[16], (D,), 0.3, 2.0, (), jnp.float32),
        "norm2_gain": jnp.clip(1.0 + 0.1 * jax.random.normal(seeds[17], (D,), jnp.float32), 0.5, 1.5),
        "norm2_bias": scatter_about(seeds[18], (D,), 0.3, 2.0, (), jnp.float32),
    }


epsilon = 1e-05
precise = lax.Precision.HIGHEST

@jax.custom_vjp
def low(v):
    return lax.optimization_barrier(v.astype(jnp.bfloat16)).astype(jnp.float32)

@jax.custom_vjp
def low_back(v):
    return v

def low_keep(v):
    return (low(v), None)

def low_pass(kept, grad):
    return (grad,)

def back_keep(v):
    return (v, None)

def back_low(kept, grad):
    return (low(grad),)
low.defvjp(low_keep, low_pass)
low_back.defvjp(back_keep, back_low)

def token_layout(context_row, query_row, row_count):
    lengths = (context_row + query_row).astype(jnp.int32)
    slot_ends = jnp.cumsum(lengths).astype(jnp.int32)
    starts = slot_ends - lengths
    position = jnp.arange(row_count, dtype=jnp.int32)
    segment = lax.optimization_barrier(jnp.sum((position[:, None] >= slot_ends[None, :]).astype(jnp.int32), axis=1, dtype=jnp.int32))
    is_valid = position < slot_ends[-1]
    slot_index = jnp.arange(context_row.shape[0], dtype=jnp.int32)
    context_end = lax.optimization_barrier(jnp.sum(jnp.where(segment[:, None] == slot_index[None, :], (starts + context_row.astype(jnp.int32))[None, :], 0), axis=1, dtype=jnp.int32))
    is_context = is_valid & (position < context_end)
    segment = jnp.where(is_valid, segment, -1)
    return (position, segment, is_context, is_valid)

def allowed_pairs(position, segment, is_context, is_valid, query_pos, query_seg, query_valid):
    same_slot = (query_seg[:, None] == segment[None, :]) & is_context[None, :] & query_valid[:, None]
    padding_self = (query_pos[:, None] == position[None, :]) & jnp.logical_not(query_valid)[:, None]
    return same_slot | padding_self

def normalize(hidden, norm_gain, norm_shift):
    average = lax.optimization_barrier(jnp.mean(hidden, axis=-1, keepdims=True))
    centered = hidden - average
    variance = lax.optimization_barrier(jnp.mean(centered * centered, axis=-1, keepdims=True))
    return centered * lax.rsqrt(variance + epsilon) * norm_gain + norm_shift

def layer_forward(values, context_row, query_row, weights):
    w_query, w_key, w_value, b_query, b_value, w_out, b_out, norm1_gain, norm1_bias, w_hidden, b_hidden, w_back, b_back, norm2_gain, norm2_bias = weights
    row_count = values.shape[0]
    position, segment, is_context, is_valid = token_layout(context_row, query_row, row_count)
    allowed = allowed_pairs(position, segment, is_context, is_valid, position, segment, is_valid)
    queries = low(low_back(jnp.dot(values, w_query, precision=precise) + b_query))
    key_rows = low(low_back(jnp.dot(values, w_key, precision=precise)))
    value_rows = low(low_back(jnp.dot(values, w_value, precision=precise) + b_value))
    query_heads = queries.reshape(row_count, HEADS, HEAD_DIM)
    key_heads = key_rows.reshape(row_count, HEADS, HEAD_DIM)
    value_heads = value_rows.reshape(row_count, HEADS, HEAD_DIM)
    scores = jnp.einsum('qhd,khd->hqk', query_heads, key_heads, precision=precise) * (1.0 / math.sqrt(HEAD_DIM))
    scores = low_back(scores)
    scores = jnp.where(allowed[None], scores, -1e+30)
    row_max = lax.optimization_barrier(jnp.max(scores, axis=-1, keepdims=True))
    exp_scores = jnp.exp(scores - row_max)
    attn_probs = exp_scores / lax.optimization_barrier(jnp.sum(exp_scores, axis=-1, keepdims=True))
    attended = jnp.einsum('hqk,khd->qhd', low(attn_probs), value_heads, precision=precise).reshape(row_count, D)
    attended = low(low_back(attended))
    branch = low_back(jnp.dot(attended, w_out, precision=precise) + b_out)
    normed_one = normalize(values + branch, norm1_gain, norm1_bias)
    hidden_pre = low_back(jnp.dot(low(normed_one), w_hidden, precision=precise) + b_hidden)
    activated = low(jax.nn.gelu(hidden_pre, approximate=False))
    ffn_out = low_back(jnp.dot(activated, w_back, precision=precise) + b_back)
    normed_two = normalize(normed_one + ffn_out, norm2_gain, norm2_bias)
    return normed_two * is_valid.astype(jnp.float32)[:, None]

def reference(tokens, out_grad, context_len, query_count, w_query, w_key, w_value, b_query, b_value, w_out, b_out, norm1_gain, norm1_bias, w_hidden, b_hidden, w_back, b_back, norm2_gain, norm2_bias):
    weights = tuple((weight.astype(jnp.float32) for weight in (w_query, w_key, w_value, b_query, b_value, w_out, b_out, norm1_gain, norm1_bias, w_hidden, b_hidden, w_back, b_back, norm2_gain, norm2_bias)))
    inputs = tokens.astype(jnp.float32).reshape(SHARDS, TOK_DEV, D)

    def forward(inputs, weights):

        def device_layer(pieces):
            return layer_forward(pieces[0], pieces[1], pieces[2], weights)
        return lax.map(jax.checkpoint(device_layer), (inputs, context_len, query_count))
    output, pullback = jax.vjp(forward, inputs, weights)
    grad_in, grads = pullback(out_grad.astype(jnp.float32).reshape(SHARDS, TOK_DEV, D))
    return (output.reshape(TOKENS, D).astype(jnp.bfloat16), grad_in.reshape(TOKENS, D).astype(jnp.bfloat16), grads[0], grads[1], grads[2], grads[3], grads[4], grads[5], grads[6], grads[7], grads[8], grads[9], grads[10], grads[11], grads[12], grads[13], grads[14])
```

```python
import functools
import math

import jax
import jax.experimental.pallas as pl
import jax.experimental.pallas.tpu as pltpu
import jax.numpy as jnp
from jax import lax
from jax.sharding import PartitionSpec as P

HEADS = 4
HD = 128
SLOTS = 8
EPS = 1e-5
SCALE = 1.0 / math.sqrt(HD)
SCALE2 = SCALE * math.log2(math.e)
NEG = -1e30
F32 = jnp.float32
BF = jnp.bfloat16
ROWS = 512
QB = 256
KB = 512


def mm(a, b):
    return jnp.dot(a, b, preferred_element_type=F32)


def mm_t(a, b):
    return lax.dot_general(a, b, (((1,), (1,)), ((), ())), preferred_element_type=F32)


def t_mm(a, b):
    return lax.dot_general(a, b, (((0,), (0,)), ((), ())), preferred_element_type=F32)


def slot_bounds(ctx, qry):
    out = []
    start = jnp.int32(0)
    for t in range(SLOTS):
        c = ctx[0, t]
        end = start + c + qry[0, t]
        out.append((start, start + c, end))
        start = end
    return out


def key_range(bounds, first, rows):
    lo = jnp.int32(1 << 30)
    hi = jnp.int32(0)
    for start, ctx_end, end in bounds:
        hit = (start < first + rows) & (end > first) & (end > start)
        lo = jnp.where(hit, jnp.minimum(lo, start), lo)
        hi = jnp.where(hit, jnp.maximum(hi, ctx_end), hi)
    return lo, hi


def row_bounds(bounds, pos):
    lo = jnp.zeros(pos.shape, jnp.int32)
    hi = jnp.zeros(pos.shape, jnp.int32)
    for start, ctx_end, end in bounds:
        inside = (pos >= start) & (pos < end)
        lo = jnp.where(inside, start, lo)
        hi = jnp.where(inside, ctx_end, hi)
    return lo, hi


def full(shape):
    return pl.BlockSpec(shape, lambda i, *_: (0,) * len(shape))


def forward_kernel(
    rows, ctx, qry, tok, wq, wk, wv, bq, bv, q_o, k_o, v_o, kt_o, att_o, lse_o, qs, ks, vt, mx, sm, acc, sc
):
    i = pl.program_id(0)
    proj_steps = rows // ROWS

    @pl.when(i < proj_steps)
    def _():
        t = tok[...]
        r = pl.ds(pl.multiple_of(i * ROWS, ROWS), ROWS)
        q = (mm(t, wq[...]) + bq[...]).astype(BF)
        qs[r, :] = q
        q_o[...] = q
        k = mm(t, wk[...]).astype(BF)
        ks[r, :] = k
        k_o[...] = k
        kt_o[...] = k.T
        v = (mm(t, wv[...]) + bv[...]).astype(BF)
        v_o[...] = v
        vt[:, r] = v.T

    @pl.when(i >= proj_steps)
    def _():
        first = (i - proj_steps) * QB
        bounds = slot_bounds(ctx, qry)
        lo, hi = key_range(bounds, first, QB)
        key_lo, key_hi = row_bounds(bounds, first + lax.broadcasted_iota(jnp.int32, (1, QB), 1))
        rq = pl.ds(pl.multiple_of(first, QB), QB)
        mx[...] = jnp.full(mx.shape, NEG, F32)
        sm[...] = jnp.zeros(sm.shape, F32)
        acc[...] = jnp.zeros(acc.shape, F32)
        j0 = lo // KB
        j1 = (hi + KB - 1) // KB
        cols = [slice(h * HD, (h + 1) * HD) for h in range(HEADS)]
        parts = [slice(h * 8, (h + 1) * 8) for h in range(HEADS)]

        def score_pass(j, carry):
            rk = pl.ds(pl.multiple_of(j * KB, KB), KB)
            key_pos = j * KB + lax.broadcasted_iota(jnp.int32, (KB, QB), 0)
            allowed = (key_pos >= key_lo) & (key_pos < key_hi)
            raw = [mm_t(ks[rk, c], qs[rq, c]) for c in cols]
            for h, part in enumerate(parts):
                s = jnp.where(allowed, raw[h], NEG)
                sc[h, rk, :] = s
                mx[part, :] = jnp.maximum(mx[part, :], jnp.max(s.reshape(KB // 8, 8, QB), axis=0))
            return carry

        lax.fori_loop(j0, j1, score_pass, 0)
        peak = [jnp.max(mx[part, :], axis=0, keepdims=True) * SCALE2 for part in parts]

        def value_pass(j, carry):
            rk = pl.ds(pl.multiple_of(j * KB, KB), KB)
            probs = []
            for h, part in enumerate(parts):
                p = jnp.exp2(sc[h, rk, :] * SCALE2 - peak[h])
                sm[part, :] = sm[part, :] + jnp.sum(p.reshape(KB // 8, 8, QB), axis=0)
                probs.append(p.astype(BF))
            for h, c in enumerate(cols):
                acc[c, :] = acc[c, :] + mm(vt[c, rk], probs[h])
            return carry

        lax.fori_loop(j0, j1, value_pass, 0)
        padding = key_hi == 0
        own_values = vt[:, rq]
        for h, (c, part) in enumerate(zip(cols, parts)):
            total = jnp.sum(sm[part, :], axis=0, keepdims=True)
            o = jnp.where(padding, own_values[c, :].astype(F32), acc[c, :] * (1.0 / total))
            att_o[:, c] = o.T.astype(BF)
            lse_o[h : h + 1, :] = peak[h] + jnp.log2(total)


def forward(ctx, qry, tok, wq, wk, wv, bq, bv):
    rows, width = tok.shape
    ps, qn = rows // ROWS, rows // QB
    struct = jax.ShapeDtypeStruct
    proj = pl.BlockSpec((ROWS, width), lambda i, *_: (jnp.minimum(i, ps - 1), 0))
    proj_t = pl.BlockSpec((width, ROWS), lambda i, *_: (0, jnp.minimum(i, ps - 1)))
    att = pl.BlockSpec((QB, width), lambda i, *_: (jnp.maximum(i - ps, 0), 0))
    att_t = pl.BlockSpec((8, QB), lambda i, *_: (0, jnp.maximum(i - ps, 0)))
    spec = pltpu.PrefetchScalarGridSpec(
        num_scalar_prefetch=2,
        grid=(ps + qn,),
        in_specs=[proj] + [full((width, width))] * 3 + [full((1, width))] * 2,
        out_specs=[proj] * 3 + [proj_t, att, att_t],
        scratch_shapes=[
            pltpu.VMEM((rows, width), BF),
            pltpu.VMEM((rows, width), BF),
            pltpu.VMEM((width, rows), BF),
            pltpu.VMEM((8 * HEADS, QB), F32),
            pltpu.VMEM((8 * HEADS, QB), F32),
            pltpu.VMEM((width, QB), F32),
            pltpu.VMEM((HEADS, rows, QB), F32),
        ],
    )
    return pl.pallas_call(
        functools.partial(forward_kernel, rows),
        grid_spec=spec,
        out_shape=[struct((rows, width), BF)] * 3
        + [struct((width, rows), BF), struct((rows, width), BF), struct((8, rows), F32)],
        compiler_params=pltpu.CompilerParams(vmem_limit_bytes=56 << 20),
        name="attention_forward",
    )(ctx, qry, tok, wq, wk, wv, bq[None], bv[None])


def middle_kernel(
    ctx, qry, tok, og, att, w_out, b_out, g1, b1, w_h, b_h, w_b, b_b, g2, b2,
    out_o, dsum_o, datt_o, delta_o, gwb, gwh, gwo, vec,
):
    i = pl.program_id(0)
    total = slot_bounds(ctx, qry)[-1][2]
    row = i * ROWS + lax.broadcasted_iota(jnp.int32, (ROWS, 1), 0)
    valid = (row < total).astype(F32)
    a = att[...]
    x1 = tok[...].astype(F32) + (mm(a, w_out[...]) + b_out[...])
    xc1 = x1 - jnp.mean(x1, axis=1, keepdims=True)
    r1 = lax.rsqrt(jnp.mean(xc1 * xc1, axis=1, keepdims=True) + EPS)
    xh1 = xc1 * r1
    n1 = xh1 * g1[...] + b1[...]
    nl = n1.astype(BF)
    hp = mm(nl, w_h[...]) + b_h[...]
    cdf = 0.5 * (1.0 + lax.erf(hp * (1.0 / math.sqrt(2.0))))
    act = (hp * cdf).astype(BF)
    slope = cdf + hp * (jnp.exp(-0.5 * hp * hp) * (1.0 / math.sqrt(2.0 * math.pi)))
    x2 = n1 + (mm(act, w_b[...]) + b_b[...])
    xc2 = x2 - jnp.mean(x2, axis=1, keepdims=True)
    r2 = lax.rsqrt(jnp.mean(xc2 * xc2, axis=1, keepdims=True) + EPS)
    xh2 = xc2 * r2
    out_o[...] = ((xh2 * g2[...] + b2[...]) * valid).astype(BF)
    dy = og[...].astype(F32) * valid
    dg2 = jnp.sum(dy * xh2, axis=0, keepdims=True)
    db2 = jnp.sum(dy, axis=0, keepdims=True)
    dx = dy * g2[...]
    d2 = r2 * (dx - jnp.mean(dx, axis=1, keepdims=True) - xh2 * jnp.mean(dx * xh2, axis=1, keepdims=True))
    df = d2.astype(BF)
    dbb = jnp.sum(df.astype(F32), axis=0, keepdims=True)
    dh = (mm_t(df, w_b[...]) * slope).astype(BF)
    dbh = jnp.sum(dh.astype(F32), axis=0, keepdims=True)
    dn = d2 + mm_t(dh, w_h[...])
    dg1 = jnp.sum(dn * xh1, axis=0, keepdims=True)
    db1 = jnp.sum(dn, axis=0, keepdims=True)
    dx1 = dn * g1[...]
    ds = r1 * (dx1 - jnp.mean(dx1, axis=1, keepdims=True) - xh1 * jnp.mean(dx1 * xh1, axis=1, keepdims=True))
    dsum_o[...] = ds
    dbr = ds.astype(BF)
    dbo = jnp.sum(dbr.astype(F32), axis=0, keepdims=True)
    da = mm_t(dbr, w_out[...]).astype(BF)
    datt_o[...] = da
    prod = a.astype(F32) * da.astype(F32)
    prod_hi = prod.astype(BF)
    prod_lo = (prod - prod_hi.astype(F32)).astype(BF)
    width = prod.shape[1]
    head_of = lax.broadcasted_iota(jnp.int32, (8, width), 1) // HD
    pick = (head_of == lax.broadcasted_iota(jnp.int32, (8, width), 0)).astype(BF)
    delta_o[...] = mm_t(pick, prod_hi) + mm_t(pick, prod_lo)

    @pl.when(i == 0)
    def _():
        gwb[...] = t_mm(act, df)
        gwh[...] = t_mm(nl, dh)
        gwo[...] = t_mm(a, dbr)
        vec[...] = jnp.zeros(vec.shape, F32)

    @pl.when(i > 0)
    def _():
        gwb[...] += t_mm(act, df)
        gwh[...] += t_mm(nl, dh)
        gwo[...] += t_mm(a, dbr)

    for n, v in enumerate((dbo, dg1, db1, dbh[:, :width], dbh[:, width:], dbb, dg2, db2)):
        vec[n : n + 1, :] += v


def middle(ctx, qry, tok, og, att, w_out, b_out, g1, b1, w_h, b_h, w_b, b_b, g2, b2):
    rows, width = tok.shape
    ff = w_h.shape[1]
    struct = jax.ShapeDtypeStruct
    row = pl.BlockSpec((ROWS, width), lambda i, *_: (i, 0))
    vec = full((1, width))
    spec = pltpu.PrefetchScalarGridSpec(
        num_scalar_prefetch=2,
        grid=(rows // ROWS,),
        in_specs=[row] * 3
        + [full((width, width)), vec, vec, vec, full((width, ff)), full((1, ff)), full((ff, width)), vec, vec, vec],
        out_specs=[row] * 3
        + [pl.BlockSpec((8, ROWS), lambda i, *_: (0, i)), full((ff, width)), full((width, ff))]
        + [full((width, width)), full((8, width))],
    )
    return pl.pallas_call(
        middle_kernel,
        grid_spec=spec,
        out_shape=[
            struct((rows, width), BF),
            struct((rows, width), F32),
            struct((rows, width), BF),
            struct((8, rows), F32),
            struct((ff, width), F32),
            struct((width, ff), F32),
            struct((width, width), F32),
            struct((8, width), F32),
        ],
        compiler_params=pltpu.CompilerParams(vmem_limit_bytes=56 << 20),
        name="ffn_and_norms",
    )(
        ctx, qry, tok, og, att, w_out, b_out[None], g1[None], b1[None], w_h, b_h[None], w_b, b_b[None],
        g2[None], b2[None],
    )


def backward_kernel(
    rows, heads, ctx, qry, tok, q, k, kt, v, do, lse, delta, dq_o, dk_o, dv_o, gw_o, vec_o, dqt, dka, dva
):
    i = pl.program_id(0)
    steps = rows // QB
    width = heads * HD
    bounds = slot_bounds(ctx, qry)

    @pl.when(i == 0)
    def _():
        dka[...] = jnp.zeros(dka.shape, F32)
        dva[...] = jnp.zeros(dva.shape, F32)

    @pl.when(i < steps)
    def _():
        first = i * QB
        lo, hi = key_range(bounds, first, QB)
        key_lo, key_hi = row_bounds(bounds, first + lax.broadcasted_iota(jnp.int32, (1, QB), 1))
        rq = pl.ds(pl.multiple_of(first, QB), QB)
        dqt[...] = jnp.zeros(dqt.shape, F32)
        cols = [slice(h * HD, (h + 1) * HD) for h in range(heads)]

        def body(j, carry):
            rk = pl.ds(pl.multiple_of(j * KB, KB), KB)
            key_pos = j * KB + lax.broadcasted_iota(jnp.int32, (KB, QB), 0)
            allowed = (key_pos >= key_lo) & (key_pos < key_hi)
            scores = [mm_t(k[rk, c], q[rq, c]) for c in cols]
            dprobs = [mm_t(v[rk, c], do[rq, c]) for c in cols]
            probs = []
            dscores = []
            for h in range(heads):
                p = jnp.where(allowed, jnp.exp2(scores[h] * SCALE2 - lse[h : h + 1, rq]), 0.0)
                probs.append(p.astype(BF))
                dscores.append((p * (dprobs[h] - delta[h : h + 1, rq])).astype(BF))
            for h, c in enumerate(cols):
                dva[rk, c] += mm(probs[h], do[rq, c])
                dka[rk, c] += mm(dscores[h], q[rq, c])
                dqt[c, :] += mm(kt[c, rk], dscores[h])
            return carry

        lax.fori_loop(lo // KB, (hi + KB - 1) // KB, body, 0)
        dq_o[rq, :] = (dqt[...] * SCALE).T.astype(BF)

    @pl.when(i == steps)
    def _():
        padding = lax.broadcasted_iota(jnp.int32, (rows, 1), 0) >= bounds[-1][2]
        dk_o[...] = (dka[...] * SCALE).astype(BF)
        dv_o[...] = (dva[...] + jnp.where(padding, do[...].astype(F32), 0.0)).astype(BF)
        gw_o[:, :width] = t_mm(tok[...], dq_o[...])
        gw_o[:, width : 2 * width] = t_mm(tok[...], dk_o[...])
        gw_o[:, 2 * width :] = t_mm(tok[...], dv_o[...])
        vec_o[0:1, :] = jnp.sum(dq_o[...].astype(F32), axis=0, keepdims=True)
        vec_o[1:2, :] = jnp.sum(dv_o[...].astype(F32), axis=0, keepdims=True)


def backward(ctx, qry, tok, q, k, kt, v, do, lse, delta):
    rows, width = tok.shape
    struct = jax.ShapeDtypeStruct
    whole = full((rows, width))
    spec = pltpu.PrefetchScalarGridSpec(
        num_scalar_prefetch=2,
        grid=(rows // QB + 1,),
        in_specs=[whole, whole, whole, full((width, rows)), whole, whole, full((8, rows)), full((8, rows))],
        out_specs=[whole] * 3 + [full((width, 3 * width)), full((8, width))],
        scratch_shapes=[
            pltpu.VMEM((width, QB), F32),
            pltpu.VMEM((rows, width), F32),
            pltpu.VMEM((rows, width), F32),
        ],
    )
    return pl.pallas_call(
        functools.partial(backward_kernel, rows, HEADS),
        grid_spec=spec,
        out_shape=[struct((rows, width), BF)] * 3 + [struct((width, 3 * width), F32), struct((8, width), F32)],
        compiler_params=pltpu.CompilerParams(vmem_limit_bytes=60 << 20),
        name="attention_backward",
    )(ctx, qry, tok, q, k, kt, v, do, lse, delta)


def input_grad_kernel(ds, dq, dk, dv, wq, wk, wv, o):
    total = ds[...] + mm_t(dq[...], wq[...]) + mm_t(dk[...], wk[...]) + mm_t(dv[...], wv[...])
    o[...] = total.astype(BF)


def input_gradient(ds, dq, dk, dv, wq, wk, wv):
    rows, width = ds.shape
    row = pl.BlockSpec((ROWS, width), lambda i: (i, 0))
    square = pl.BlockSpec((width, width), lambda i: (0, 0))
    return pl.pallas_call(
        input_grad_kernel,
        grid=(rows // ROWS,),
        in_specs=[row] * 4 + [square] * 3,
        out_specs=row,
        out_shape=jax.ShapeDtypeStruct((rows, width), BF),
        compiler_params=pltpu.CompilerParams(vmem_limit_bytes=48 << 20),
        name="input_gradient",
    )(ds, dq, dk, dv, wq, wk, wv)


def local(
    tokens, out_grad, context_len, query_count, w_query, w_key, w_value, b_query, b_value, w_out, b_out,
    norm1_gain, norm1_bias, w_hidden, b_hidden, w_back, b_back, norm2_gain, norm2_bias,
):
    width = tokens.shape[1]
    q, k, v, kt, att, lse = forward(
        context_len, query_count, tokens, w_query, w_key, w_value, b_query, b_value
    )
    output, ds, datt, delta, gwb, gwh, gwo, vec = middle(
        context_len, query_count, tokens, out_grad, att, w_out, b_out, norm1_gain, norm1_bias,
        w_hidden, b_hidden, w_back, b_back, norm2_gain, norm2_bias,
    )
    dq, dk, dv, gw, vec2 = backward(context_len, query_count, tokens, q, k, kt, v, datt, lse, delta)
    input_grad = input_gradient(ds, dq, dk, dv, w_query, w_key, w_value)
    gwb, gwh, gwo, gw, vec, vec2 = lax.psum((gwb, gwh, gwo, gw, vec, vec2), ("dp", "dq"))
    return (
        output,
        input_grad,
        gw[:, :width],
        gw[:, width : 2 * width],
        gw[:, 2 * width :],
        vec2[0],
        vec2[1],
        gwo,
        vec[0],
        vec[1],
        vec[2],
        gwh,
        vec[3:5].reshape(-1),
        gwb,
        vec[5],
        vec[6],
        vec[7],
    )


def solution(mesh):
    return jax.shard_map(
        local,
        mesh=mesh,
        in_specs=(
            P(("dp", "dq"), None),
            P(("dp", "dq"), None),
            P(("dp", "dq"), None),
            P(("dp", "dq"), None),
            P(),
            P(),
            P(),
            P(),
            P(),
            P(),
            P(),
            P(),
            P(),
            P(),
            P(),
            P(),
            P(),
            P(),
            P(),
        ),
        out_specs=(
            P(("dp", "dq"), None),
            P(("dp", "dq"), None),
            P(),
            P(),
            P(),
            P(),
            P(),
            P(),
            P(),
            P(),
            P(),
            P(),
            P(),
            P(),
            P(),
            P(),
            P(),
        ),
        check_vma=False,
    )
```

```python
import functools
import math

import jax
import jax.experimental.pallas as pl
import jax.experimental.pallas.tpu as pltpu
import jax.numpy as jnp
from jax import lax
from jax.sharding import PartitionSpec as P

HEADS = 4
HD = 128
SLOTS = 8
EPS = 1e-5
SCALE = 1.0 / math.sqrt(HD)
SCALE2 = SCALE * math.log2(math.e)
NEG = -1e30
F32 = jnp.float32
BF = jnp.bfloat16
ROWS = 512
QB = 256
KB = 512
PIECE = 256
SMALL = 16


def mm(a, b):
    return jnp.dot(a, b, preferred_element_type=F32)


def mm_t(a, b):
    return lax.dot_general(a, b, (((1,), (1,)), ((), ())), preferred_element_type=F32)


def t_mm(a, b):
    return lax.dot_general(a, b, (((0,), (0,)), ((), ())), preferred_element_type=F32)


def slot_bounds(ctx, qry):
    out = []
    start = jnp.int32(0)
    for t in range(SLOTS):
        c = ctx[0, t]
        end = start + c + qry[0, t]
        out.append((start, start + c, end))
        start = end
    return out


def key_range(bounds, first, rows):
    lo = jnp.int32(1 << 30)
    hi = jnp.int32(0)
    for start, ctx_end, end in bounds:
        hit = (start < first + rows) & (end > first) & (end > start)
        lo = jnp.where(hit, jnp.minimum(lo, start), lo)
        hi = jnp.where(hit, jnp.maximum(hi, ctx_end), hi)
    return lo, hi


def row_bounds(bounds, pos):
    lo = jnp.zeros(pos.shape, jnp.int32)
    hi = jnp.zeros(pos.shape, jnp.int32)
    for start, ctx_end, end in bounds:
        inside = (pos >= start) & (pos < end)
        lo = jnp.where(inside, start, lo)
        hi = jnp.where(inside, ctx_end, hi)
    return lo, hi


def full(shape):
    return pl.BlockSpec(shape, lambda i, *_: (0,) * len(shape))


def forward_kernel(
    rows, ctx, qry, tok, wq, wk, wv, bq, bv, q_o, k_o, v_o, kt_o, att_o, lse_o, qs, ks, vt, mx, sm, acc, sc
):
    i = pl.program_id(0)
    proj_steps = rows // ROWS

    @pl.when(i < proj_steps)
    def _():
        t = tok[...]
        r = pl.ds(pl.multiple_of(i * ROWS, ROWS), ROWS)
        q = (mm(t, wq[...]) + bq[...]).astype(BF)
        qs[r, :] = q
        q_o[...] = q
        k = mm(t, wk[...]).astype(BF)
        ks[r, :] = k
        k_o[...] = k
        kt_o[...] = k.T
        v = (mm(t, wv[...]) + bv[...]).astype(BF)
        v_o[...] = v
        vt[:, r] = v.T

    @pl.when(i >= proj_steps)
    def _():
        first = (i - proj_steps) * QB
        bounds = slot_bounds(ctx, qry)
        lo, hi = key_range(bounds, first, QB)
        key_lo, key_hi = row_bounds(bounds, first + lax.broadcasted_iota(jnp.int32, (1, QB), 1))
        rq = pl.ds(pl.multiple_of(first, QB), QB)
        mx[...] = jnp.full(mx.shape, NEG, F32)
        sm[...] = jnp.zeros(sm.shape, F32)
        acc[...] = jnp.zeros(acc.shape, F32)
        j0 = lo // KB
        j1 = (hi + KB - 1) // KB
        cols = [slice(h * HD, (h + 1) * HD) for h in range(HEADS)]
        parts = [slice(h * 8, (h + 1) * 8) for h in range(HEADS)]

        def score_pass(j, carry):
            rk = pl.ds(pl.multiple_of(j * KB, KB), KB)
            key_pos = j * KB + lax.broadcasted_iota(jnp.int32, (KB, QB), 0)
            allowed = (key_pos >= key_lo) & (key_pos < key_hi)
            raw = [mm_t(ks[rk, c], qs[rq, c]) for c in cols]
            for h, part in enumerate(parts):
                s = jnp.where(allowed, raw[h], NEG)
                sc[h, rk, :] = s
                mx[part, :] = jnp.maximum(mx[part, :], jnp.max(s.reshape(KB // 8, 8, QB), axis=0))
            return carry

        lax.fori_loop(j0, j1, score_pass, 0)
        peak = [jnp.max(mx[part, :], axis=0, keepdims=True) * SCALE2 for part in parts]

        def value_pass(j, carry):
            rk = pl.ds(pl.multiple_of(j * KB, KB), KB)
            probs = []
            for h, part in enumerate(parts):
                p = jnp.exp2(sc[h, rk, :] * SCALE2 - peak[h])
                sm[part, :] = sm[part, :] + jnp.sum(p.reshape(KB // 8, 8, QB), axis=0)
                probs.append(p.astype(BF))
            for h, c in enumerate(cols):
                acc[c, :] = acc[c, :] + mm(vt[c, rk], probs[h])
            return carry

        lax.fori_loop(j0, j1, value_pass, 0)
        padding = key_hi == 0
        own_values = vt[:, rq]
        for h, (c, part) in enumerate(zip(cols, parts)):
            total = jnp.sum(sm[part, :], axis=0, keepdims=True)
            o = jnp.where(padding, own_values[c, :].astype(F32), acc[c, :] * (1.0 / total))
            att_o[:, c] = o.T.astype(BF)
            lse_o[h : h + 1, :] = peak[h] + jnp.log2(total)


def forward(ctx, qry, tok, wq, wk, wv, bq, bv):
    rows, width = tok.shape
    ps, qn = rows // ROWS, rows // QB
    struct = jax.ShapeDtypeStruct
    proj = pl.BlockSpec((ROWS, width), lambda i, *_: (jnp.minimum(i, ps - 1), 0))
    proj_t = pl.BlockSpec((width, ROWS), lambda i, *_: (0, jnp.minimum(i, ps - 1)))
    att = pl.BlockSpec((QB, width), lambda i, *_: (jnp.maximum(i - ps, 0), 0))
    att_t = pl.BlockSpec((8, QB), lambda i, *_: (0, jnp.maximum(i - ps, 0)))
    spec = pltpu.PrefetchScalarGridSpec(
        num_scalar_prefetch=2,
        grid=(ps + qn,),
        in_specs=[proj] + [full((width, width))] * 3 + [full((1, width))] * 2,
        out_specs=[proj] * 3 + [proj_t, att, att_t],
        scratch_shapes=[
            pltpu.VMEM((rows, width), BF),
            pltpu.VMEM((rows, width), BF),
            pltpu.VMEM((width, rows), BF),
            pltpu.VMEM((8 * HEADS, QB), F32),
            pltpu.VMEM((8 * HEADS, QB), F32),
            pltpu.VMEM((width, QB), F32),
            pltpu.VMEM((HEADS, rows, QB), F32),
        ],
    )
    return pl.pallas_call(
        functools.partial(forward_kernel, rows),
        grid_spec=spec,
        out_shape=[struct((rows, width), BF)] * 3
        + [struct((width, rows), BF), struct((rows, width), BF), struct((8, rows), F32)],
        compiler_params=pltpu.CompilerParams(vmem_limit_bytes=56 << 20),
        name="attention_forward",
    )(ctx, qry, tok, wq, wk, wv, bq[None], bv[None])


def middle_kernel(
    core, ctx, qry, tok, og, att, w_out, b_out, g1, b1, w_h, b_h, w_b, b_b, g2, b2,
    out_o, dsum_o, dbr_o, keep_o, send_o, vec, pack,
):
    i = pl.program_id(0)
    total = slot_bounds(ctx, qry)[-1][2]
    row = i * ROWS + lax.broadcasted_iota(jnp.int32, (ROWS, 1), 0)
    valid = (row < total).astype(F32)
    a = att[...]
    x1 = tok[...].astype(F32) + (mm(a, w_out[...]) + b_out[...])
    xc1 = x1 - jnp.mean(x1, axis=1, keepdims=True)
    r1 = lax.rsqrt(jnp.mean(xc1 * xc1, axis=1, keepdims=True) + EPS)
    xh1 = xc1 * r1
    n1 = xh1 * g1[...] + b1[...]
    nl = n1.astype(BF)
    hp = mm(nl, w_h[...]) + b_h[...]
    cdf = 0.5 * (1.0 + lax.erf(hp * (1.0 / math.sqrt(2.0))))
    act = (hp * cdf).astype(BF)
    slope = cdf + hp * (jnp.exp(-0.5 * hp * hp) * (1.0 / math.sqrt(2.0 * math.pi)))
    x2 = n1 + (mm(act, w_b[...]) + b_b[...])
    xc2 = x2 - jnp.mean(x2, axis=1, keepdims=True)
    r2 = lax.rsqrt(jnp.mean(xc2 * xc2, axis=1, keepdims=True) + EPS)
    xh2 = xc2 * r2
    out_o[...] = ((xh2 * g2[...] + b2[...]) * valid).astype(BF)
    dy = og[...].astype(F32) * valid
    dg2 = jnp.sum(dy * xh2, axis=0, keepdims=True)
    db2 = jnp.sum(dy, axis=0, keepdims=True)
    dx = dy * g2[...]
    d2 = r2 * (dx - jnp.mean(dx, axis=1, keepdims=True) - xh2 * jnp.mean(dx * xh2, axis=1, keepdims=True))
    df = d2.astype(BF)
    dbb = jnp.sum(df.astype(F32), axis=0, keepdims=True)
    dh = (mm_t(df, w_b[...]) * slope).astype(BF)
    dbh = jnp.sum(dh.astype(F32), axis=0, keepdims=True)
    dn = d2 + mm_t(dh, w_h[...])
    dg1 = jnp.sum(dn * xh1, axis=0, keepdims=True)
    db1 = jnp.sum(dn, axis=0, keepdims=True)
    dx1 = dn * g1[...]
    ds = r1 * (dx1 - jnp.mean(dx1, axis=1, keepdims=True) - xh1 * jnp.mean(dx1 * xh1, axis=1, keepdims=True))
    dsum_o[...] = ds
    dbr = ds.astype(BF)
    dbo = jnp.sum(dbr.astype(F32), axis=0, keepdims=True)
    dbr_o[...] = dbr
    width = dbr.shape[1]

    @pl.when(i == 0)
    def _():
        pack[...] = jnp.zeros(pack.shape, F32)
        vec[...] = jnp.zeros(vec.shape, F32)

    def add(row, value):
        for r in range(0, value.shape[0], PIECE):
            half, at = divmod(row + r, pack.shape[1])
            pack[half, at : at + PIECE, :] += value[r : r + PIECE]

    ff = act.shape[1]
    add(0, t_mm(act, df))
    for n in range(ff // width):
        add(ff + n * width, t_mm(nl, dh[:, n * width : (n + 1) * width]))
    add(2 * ff, t_mm(a, dbr))
    for n, v in enumerate((dbo, dg1, db1, dbh[:, :width], dbh[:, width:], dbb, dg2, db2)):
        vec[n : n + 1, :] += v

    @pl.when(i == pl.num_programs(0) - 1)
    def _():
        keep_o[...] = pack[core[0]]
        send_o[...] = pack[1 - core[0]]


def middle(core, ctx, qry, tok, og, att, w_out, b_out, g1, b1, w_h, b_h, w_b, b_b, g2, b2):
    rows, width = tok.shape
    ff = w_h.shape[1]
    half = ff + width // 2
    struct = jax.ShapeDtypeStruct
    row = pl.BlockSpec((ROWS, width), lambda i, *_: (i, 0))
    vec = full((1, width))
    spec = pltpu.PrefetchScalarGridSpec(
        num_scalar_prefetch=3,
        grid=(rows // ROWS,),
        in_specs=[row] * 3
        + [full((width, width)), vec, vec, vec, full((width, ff)), full((1, ff)), full((ff, width)), vec, vec, vec],
        out_specs=[row] * 3
        + [full((half, width)), full((half, width)), full((8, width))],
        scratch_shapes=[pltpu.VMEM((2, half, width), F32)],
    )
    return pl.pallas_call(
        middle_kernel,
        grid_spec=spec,
        out_shape=[
            struct((rows, width), BF),
            struct((rows, width), F32),
            struct((rows, width), BF),
            struct((half, width), F32),
            struct((half, width), F32),
            struct((8, width), F32),
        ],
        compiler_params=pltpu.CompilerParams(vmem_limit_bytes=56 << 20),
        name="ffn_and_norms",
    )(
        core, ctx, qry, tok, og, att, w_out, b_out[None], g1[None], b1[None], w_h, b_h[None], w_b, b_b[None],
        g2[None], b2[None],
    )


def attended_grad_kernel(att, dbr, w_out, datt_o, delta_o):
    da = mm_t(dbr[...], w_out[...]).astype(BF)
    datt_o[...] = da
    prod = att[...].astype(F32) * da.astype(F32)
    prod_hi = prod.astype(BF)
    prod_lo = (prod - prod_hi.astype(F32)).astype(BF)
    width = prod.shape[1]
    head_of = lax.broadcasted_iota(jnp.int32, (8, width), 1) // HD
    pick = (head_of == lax.broadcasted_iota(jnp.int32, (8, width), 0)).astype(BF)
    delta_o[...] = mm_t(pick, prod_hi) + mm_t(pick, prod_lo)


def attended_grad(att, dbr, w_out):
    rows, width = att.shape
    row = pl.BlockSpec((ROWS, width), lambda i: (i, 0))
    return pl.pallas_call(
        attended_grad_kernel,
        grid=(rows // ROWS,),
        in_specs=[row, row, full((width, width))],
        out_specs=[row, pl.BlockSpec((8, ROWS), lambda i: (0, i))],
        out_shape=[jax.ShapeDtypeStruct((rows, width), BF), jax.ShapeDtypeStruct((8, rows), F32)],
        compiler_params=pltpu.CompilerParams(vmem_limit_bytes=32 << 20),
        cost_estimate=pl.CostEstimate(flops=2 * 10**9, bytes_accessed=7 << 20, transcendentals=0),
        name="attended_gradient",
    )(att, dbr, w_out)


def backward_kernel(
    rows, heads, ctx, qry, tok, q, k, kt, v, do, lse, delta, dq_o, dk_o, dv_o, dqt, dka, dva
):
    i = pl.program_id(0)
    steps = rows // QB
    width = heads * HD
    bounds = slot_bounds(ctx, qry)

    @pl.when(i == 0)
    def _():
        dka[...] = jnp.zeros(dka.shape, F32)
        dva[...] = jnp.zeros(dva.shape, F32)

    @pl.when(i < steps)
    def _():
        first = i * QB
        lo, hi = key_range(bounds, first, QB)
        key_lo, key_hi = row_bounds(bounds, first + lax.broadcasted_iota(jnp.int32, (1, QB), 1))
        rq = pl.ds(pl.multiple_of(first, QB), QB)
        dqt[...] = jnp.zeros(dqt.shape, F32)
        cols = [slice(h * HD, (h + 1) * HD) for h in range(heads)]

        def body(j, carry):
            rk = pl.ds(pl.multiple_of(j * KB, KB), KB)
            key_pos = j * KB + lax.broadcasted_iota(jnp.int32, (KB, QB), 0)
            allowed = (key_pos >= key_lo) & (key_pos < key_hi)
            scores = [mm_t(k[rk, c], q[rq, c]) for c in cols]
            dprobs = [mm_t(v[rk, c], do[rq, c]) for c in cols]
            probs = []
            dscores = []
            for h in range(heads):
                p = jnp.where(allowed, jnp.exp2(scores[h] * SCALE2 - lse[h : h + 1, rq]), 0.0)
                probs.append(p.astype(BF))
                dscores.append((p * (dprobs[h] - delta[h : h + 1, rq])).astype(BF))
            for h, c in enumerate(cols):
                dva[rk, c] += mm(probs[h], do[rq, c])
                dka[rk, c] += mm(dscores[h], q[rq, c])
                dqt[c, :] += mm(kt[c, rk], dscores[h])
            return carry

        lax.fori_loop(lo // KB, (hi + KB - 1) // KB, body, 0)
        dq_o[rq, :] = (dqt[...] * SCALE).T.astype(BF)

    @pl.when(i == steps)
    def _():
        padding = lax.broadcasted_iota(jnp.int32, (rows, 1), 0) >= bounds[-1][2]
        dk_o[...] = (dka[...] * SCALE).astype(BF)
        dv_o[...] = (dva[...] + jnp.where(padding, do[...].astype(F32), 0.0)).astype(BF)


def backward(ctx, qry, tok, q, k, kt, v, do, lse, delta):
    rows, width = tok.shape
    struct = jax.ShapeDtypeStruct
    whole = full((rows, width))
    spec = pltpu.PrefetchScalarGridSpec(
        num_scalar_prefetch=2,
        grid=(rows // QB + 1,),
        in_specs=[whole, whole, whole, full((width, rows)), whole, whole, full((8, rows)), full((8, rows))],
        out_specs=[whole] * 3,
        scratch_shapes=[
            pltpu.VMEM((width, QB), F32),
            pltpu.VMEM((rows, width), F32),
            pltpu.VMEM((rows, width), F32),
        ],
    )
    return pl.pallas_call(
        functools.partial(backward_kernel, rows, HEADS),
        grid_spec=spec,
        out_shape=[struct((rows, width), BF)] * 3,
        compiler_params=pltpu.CompilerParams(vmem_limit_bytes=60 << 20),
        cost_estimate=pl.CostEstimate(flops=30 * 10**9, bytes_accessed=20 << 20, transcendentals=8 << 20),
        name="attention_backward",
    )(ctx, qry, tok, q, k, kt, v, do, lse, delta)


def input_grad_kernel(ds, dq, dk, dv, wq, wk, wv, o):
    total = ds[...] + mm_t(dq[...], wq[...]) + mm_t(dk[...], wk[...]) + mm_t(dv[...], wv[...])
    o[...] = total.astype(BF)


def input_gradient(ds, dq, dk, dv, wq, wk, wv):
    rows, width = ds.shape
    row = pl.BlockSpec((ROWS, width), lambda i: (i, 0))
    square = pl.BlockSpec((width, width), lambda i: (0, 0))
    return pl.pallas_call(
        input_grad_kernel,
        grid=(rows // ROWS,),
        in_specs=[row] * 4 + [square] * 3,
        out_specs=row,
        out_shape=jax.ShapeDtypeStruct((rows, width), BF),
        compiler_params=pltpu.CompilerParams(vmem_limit_bytes=48 << 20),
        name="input_gradient",
    )(ds, dq, dk, dv, wq, wk, wv)


def projection_kernel(core, tok, dq, dk, dv, vec, keep_o, send_o, small, acc):
    i = pl.program_id(0)

    @pl.when(i == 0)
    def _():
        acc[...] = jnp.zeros(acc.shape, F32)
        small[0:8, :] = vec[...]
        small[8:, :] = jnp.zeros((small.shape[0] - 8, small.shape[1]), F32)

    t = tok[...]
    width = t.shape[1]
    for n, g in enumerate((dq, dk, dv)):
        value = t_mm(t, g[...])
        for r in range(0, width, PIECE):
            half, at = divmod(n * width + r, acc.shape[1])
            acc[half, at : at + PIECE, :] += value[r : r + PIECE]
    small[8:9, :] += jnp.sum(dq[...].astype(F32), axis=0, keepdims=True)
    small[9:10, :] += jnp.sum(dv[...].astype(F32), axis=0, keepdims=True)

    @pl.when(i == pl.num_programs(0) - 1)
    def _():
        keep_o[...] = acc[core[0]]
        send_o[: acc.shape[1], :] = acc[1 - core[0]]
        send_o[acc.shape[1] :, :] = small[...]


def projection_gradients(core, tok, dq, dk, dv, vec):
    rows, width = tok.shape
    half = 3 * width // 2
    struct = jax.ShapeDtypeStruct
    row = pl.BlockSpec((2 * ROWS, width), lambda i, *_: (i, 0))
    spec = pltpu.PrefetchScalarGridSpec(
        num_scalar_prefetch=1,
        grid=(rows // (2 * ROWS),),
        in_specs=[row] * 4 + [full((8, width))],
        out_specs=[full((half, width)), full((half + SMALL, width)), full((SMALL, width))],
        scratch_shapes=[pltpu.VMEM((2, half, width), F32)],
    )
    return pl.pallas_call(
        projection_kernel,
        grid_spec=spec,
        out_shape=[
            struct((half, width), F32),
            struct((half + SMALL, width), F32),
            struct((SMALL, width), F32),
        ],
        compiler_params=pltpu.CompilerParams(vmem_limit_bytes=48 << 20),
        cost_estimate=pl.CostEstimate(flops=4 * 10**9, bytes_accessed=12 << 20, transcendentals=0),
        name="projection_gradients",
    )(core, tok, dq, dk, dv, vec)


def split_kernel(where, *refs):
    for n in range(4):
        refs[8 + n][...] = refs[n][0] + refs[4 + n][0]


def add_and_split(where, x, got):
    rows, cols = x.shape[0] // 4, x.shape[1]
    step = rows // 2 if rows % 16 == 0 else rows
    ins = [pl.BlockSpec((1, step, cols), lambda i, w, n=n: (w[n], i, 0)) for n in range(4)]
    spec = pltpu.PrefetchScalarGridSpec(
        num_scalar_prefetch=1,
        grid=(rows // step,),
        in_specs=ins + ins,
        out_specs=[pl.BlockSpec((step, cols), lambda i, w: (i, 0))] * 4,
    )
    return pl.pallas_call(
        split_kernel,
        grid_spec=spec,
        out_shape=[jax.ShapeDtypeStruct((rows, cols), F32)] * 4,
        compiler_params=pltpu.CompilerParams(vmem_limit_bytes=32 << 20),
        name="add_and_split",
    )(where, *[x.reshape(4, rows, cols)] * 4, *[got.reshape(4, rows, cols)] * 4)


def split_small_kernel(where, x, got, small, *outs):
    rows = x.shape[0] // 4
    total = small[...] + got[4 * rows :, :]
    for n in range(4):
        at = pl.ds(pl.multiple_of(where[n] * rows, 8), rows)
        outs[n][:rows, :] = x[at, :] + got[at, :]
        outs[n][rows:, :] = total


def add_and_split_small(where, x, got, small):
    rows, cols = x.shape[0] // 4, x.shape[1]
    whole = pl.BlockSpec(memory_space=pltpu.VMEM)
    return pl.pallas_call(
        split_small_kernel,
        in_specs=[pl.BlockSpec(memory_space=pltpu.SMEM)] + [whole] * 3,
        out_specs=[whole] * 4,
        out_shape=[jax.ShapeDtypeStruct((rows + small.shape[0], cols), F32)] * 4,
        compiler_params=pltpu.CompilerParams(vmem_limit_bytes=16 << 20),
        name="add_and_split_small",
    )(where, x, got, small)


def unpack_kernel(places, piece, order, *refs):
    sources, outs, held, in_sem, out_sem = refs[:4], refs[4:-3], refs[-3], refs[-2], refs[-1]

    def loads(n):
        return pltpu.make_async_copy(sources[n], held.at[n], in_sem.at[n])

    def copies(n, p):
        made = []
        for start, count, out, row, col in places:
            if start // piece == p:
                to = outs[out].at[pl.ds(row, count), pl.ds(col, held.shape[2])]
                from_ = held.at[n, pl.ds(start % piece, count)]
                made.append(pltpu.make_async_copy(from_, to, out_sem.at[n, len(made)]))
        return made

    for n in range(4):
        loads(n).start()
    for action in ("start", "wait"):
        for n in range(4):
            if action == "start":
                loads(n).wait()
            for p in range(4):

                @pl.when(order[n] == p)
                def _(n=n, p=p):
                    for c in copies(n, p):
                        c.start() if action == "start" else c.wait()


def unpack(places, shapes, order, sources):
    anywhere = pl.BlockSpec(memory_space=pl.ANY)
    piece = sources[0].shape[0]
    places = cut(places, piece)
    most = max(sum(p[0] // piece == n for p in places) for n in range(4))
    return pl.pallas_call(
        functools.partial(unpack_kernel, places, piece),
        in_specs=[pl.BlockSpec(memory_space=pltpu.SMEM)] + [anywhere] * 4,
        out_specs=[anywhere] * len(shapes),
        out_shape=[jax.ShapeDtypeStruct(s, F32) for s in shapes],
        scratch_shapes=[
            pltpu.VMEM((4,) + sources[0].shape, F32),
            pltpu.SemaphoreType.DMA((4,)),
            pltpu.SemaphoreType.DMA((4, most)),
        ],
        compiler_params=pltpu.CompilerParams(vmem_limit_bytes=24 << 20),
        name="unpack",
    )(order, *sources)


def swap_pairs(sizes, mask):
    dp, dq = sizes
    return [(p * dq + q, p * dq + (q ^ mask[p % 2])) for p in range(dp) for q in range(dq)]


class Ring:
    def __init__(self, sizes):
        dp, dq = sizes
        self.sizes = sizes
        self.core = lax.axis_index("dp") & 1
        me = lax.axis_index("dq")
        first, second = me & 1, (me >> 1) & 1
        self.low = jnp.where(self.core == 0, first, second)
        self.high = jnp.where(self.core == 0, second, first)
        place = 2 * self.high + self.low
        turned = [place ^ jnp.where(self.core == 0, a, b) for a, b in ((0, 0), (1, 2), (2, 1), (3, 3))]
        self.where = jnp.stack(turned).astype(jnp.int32)
        mine, other = 2 * self.core, 2 - 2 * self.core
        high = jnp.where(self.core == 0, first, second)
        self.order = jnp.stack(
            [mine + self.high, mine + 1 - self.high, other + high, other + 1 - high]
        ).astype(jnp.int32)
        bits = list(range(2, dq.bit_length() - 1))
        swapped = bits[1::-1] + bits[2:]
        self.far = [swap_pairs(sizes, (1 << a, 1 << b)) for a, b in zip(bits, swapped)]
        self.outer = [[(p, p ^ (1 << b)) for p in range(dp)] for b in range(1, dp.bit_length() - 1)]

    def core_start(self, send):
        return lax.ppermute(send, "dp", [(p, p ^ 1) for p in range(self.sizes[0])])

    def plane_start(self, sends):
        return [
            lax.ppermute(s, ("dp", "dq"), swap_pairs(self.sizes, (m, m))) for m, s in zip((1, 2, 3), sends)
        ]

    def plane_end(self, own, got):
        return (own + got[0]) + (got[1] + got[2])

    def far_start(self, x, n):
        return lax.ppermute(x, ("dp", "dq"), self.far[n])

    def rest(self, x):
        for pairs in self.far[2:]:
            x = x + lax.ppermute(x, ("dp", "dq"), pairs)
        for pairs in self.outer:
            x = x + lax.ppermute(x, "dp", pairs)
        return x

    def back_start(self, x, n):
        return lax.ppermute(x, ("dp", "dq"), swap_pairs(self.sizes, ((1, 2), (2, 1))[n]))

    def back_end(self, x, got, n):
        bit = (self.low, self.high)[n]
        return jnp.where(bit == 0, jnp.concatenate([x, got]), jnp.concatenate([got, x]))


def tie(*groups):
    return lax.optimization_barrier(groups)


def local(
    sizes, tokens, out_grad, context_len, query_count, w_query, w_key, w_value, b_query, b_value, w_out, b_out,
    norm1_gain, norm1_bias, w_hidden, b_hidden, w_back, b_back, norm2_gain, norm2_bias,
):
    width = tokens.shape[1]
    ff = w_hidden.shape[1]
    ring = Ring(sizes)
    core = ring.core.reshape(1).astype(jnp.int32)
    q, k, v, kt, att, lse = forward(
        context_len, query_count, tokens, w_query, w_key, w_value, b_query, b_value
    )
    output, ds, dbr, keep, send, vec = middle(
        core, context_len, query_count, tokens, out_grad, att, w_out, b_out, norm1_gain, norm1_bias,
        w_hidden, b_hidden, w_back, b_back, norm2_gain, norm2_bias,
    )
    got = ring.core_start(send)
    send, att, dbr = tie(send, att, dbr)
    datt, delta = attended_grad(att, dbr, w_out)
    got, datt, delta = tie(got, datt, delta)
    one, *sends = add_and_split(ring.where, keep, got)
    got_one = ring.plane_start(sends)
    one, ins = tie(one, (context_len, query_count, tokens, q, k, kt, v, datt, lse, delta))
    dq, dk, dv = backward(*ins)
    one, got_one, dq, dk, dv = tie(one, got_one, dq, dk, dv)
    one = ring.plane_end(one, got_one)
    got_one = ring.far_start(one, 0)
    one, dq, dk, dv = tie(one, dq, dk, dv)
    keep, send, small = projection_gradients(core, tokens, dq, dk, dv, vec)
    two, *sends = add_and_split_small(ring.where, keep, ring.core_start(send), small)
    got_two = ring.plane_start(sends)
    one, got_one, two, sends = tie(one, got_one, two, sends)
    one = one + got_one
    got_one = ring.far_start(one, 1)
    one, dq, dk, dv, ds = tie(one, dq, dk, dv, ds)
    input_grad = input_gradient(ds, dq, dk, dv, w_query, w_key, w_value)
    one, got_one, two, got_two, input_grad = tie(one, got_one, two, got_two, input_grad)
    one = ring.rest(one + got_one)
    got_one = ring.back_start(one, 0)
    two = ring.plane_end(two, got_two)
    got_two = ring.far_start(two, 0)
    one, got_one, two, got_two = tie(one, got_one, two, got_two)
    one = ring.back_end(one, got_one, 0)
    got_one = ring.back_start(one, 1)
    home_one = ring.core_start(one)
    two = two + got_two
    got_two = ring.far_start(two, 1)
    one, two, got_two = tie(one, two, got_two)
    two = ring.rest(two + got_two)
    small = two[-SMALL:]
    two = two[:-SMALL]
    got_two = ring.back_start(two, 0)
    one, got_one, home_one, two, got_two = tie(one, got_one, home_one, two, got_two)
    two = ring.back_end(two, got_two, 0)
    got_two = ring.back_start(two, 1)
    home_two = ring.core_start(two)
    last_one = ring.core_start(got_one)
    places = [(0, ff, 0, 0, 0)]
    places += [(ff + n * width, width, 1, 0, n * width) for n in range(ff // width)]
    places += [(2 * ff, width, 2, 0, 0)]
    shapes = [(ff, width), (width, ff), (width, width)]
    gwb, gwh, gwo = unpack(places, shapes, ring.order, (one, got_one, home_one, last_one))
    two, got_two, home_two, gwb, gwh, gwo = tie(two, got_two, home_two, gwb, gwh, gwo)
    places = [(n * width, width, n, 0, 0) for n in range(3)]
    last_two = ring.core_start(got_two)
    gq, gk, gv = unpack(places, [(width, width)] * 3, ring.order, (two, got_two, home_two, last_two))
    return (
        output,
        input_grad,
        gq,
        gk,
        gv,
        small[8],
        small[9],
        gwo,
        small[0],
        small[1],
        small[2],
        gwh,
        small[3:5].reshape(-1),
        gwb,
        small[5],
        small[6],
        small[7],
    )


def cut(places, piece):
    out = []
    for start, rows, to, row, col in places:
        at = start
        while at < start + rows:
            end = min((at // piece + 1) * piece, start + rows)
            out.append((at, end - at, to, row + at - start, col))
            at = end
    return out


def solution(mesh):
    sizes = (mesh.shape["dp"], mesh.shape["dq"])
    return jax.shard_map(
        functools.partial(local, sizes),
        mesh=mesh,
        in_specs=(
            P(("dp", "dq"), None),
            P(("dp", "dq"), None),
            P(("dp", "dq"), None),
            P(("dp", "dq"), None),
            P(),
            P(),
            P(),
            P(),
            P(),
            P(),
            P(),
            P(),
            P(),
            P(),
            P(),
            P(),
            P(),
            P(),
            P(),
        ),
        out_specs=(
            P(("dp", "dq"), None),
            P(("dp", "dq"), None),
            P(),
            P(),
            P(),
            P(),
            P(),
            P(),
            P(),
            P(),
            P(),
            P(),
            P(),
            P(),
            P(),
            P(),
            P(),
        ),
        check_vma=False,
    )
```

```python
import functools
import math

import jax
import jax.experimental.pallas as pl
import jax.experimental.pallas.tpu as pltpu
import jax.numpy as jnp
from jax import lax
from jax.sharding import PartitionSpec as P

HEADS = 4
HD = 128
SLOTS = 8
EPS = 1e-5
SCALE = 1.0 / math.sqrt(HD)
SCALE2 = SCALE * math.log2(math.e)
NEG = -1e30
F32 = jnp.float32
BF = jnp.bfloat16
ROWS = 512
QB = 256
KB = 512
UNIT = 128
PIECE = 256
LIGHT = pl.CostEstimate(flops=1, bytes_accessed=1, transcendentals=0)
SMALL = 16
SEND = 128


def mm(a, b):
    return jnp.dot(a, b, preferred_element_type=F32)


def mm_t(a, b):
    return lax.dot_general(a, b, (((1,), (1,)), ((), ())), preferred_element_type=F32)


def t_mm(a, b):
    return lax.dot_general(a, b, (((0,), (0,)), ((), ())), preferred_element_type=F32)


def slot_bounds(ctx, qry):
    out = []
    start = jnp.int32(0)
    for t in range(SLOTS):
        c = ctx[0, t]
        end = start + c + qry[0, t]
        out.append((start, start + c, end))
        start = end
    return out


def key_range(bounds, first, rows):
    lo = jnp.int32(1 << 30)
    hi = jnp.int32(0)
    for start, ctx_end, end in bounds:
        hit = (start < first + rows) & (end > first) & (end > start)
        lo = jnp.where(hit, jnp.minimum(lo, start), lo)
        hi = jnp.where(hit, jnp.maximum(hi, ctx_end), hi)
    return lo, hi


def row_bounds(bounds, pos):
    lo = jnp.zeros(pos.shape, jnp.int32)
    hi = jnp.zeros(pos.shape, jnp.int32)
    for start, ctx_end, end in bounds:
        inside = (pos >= start) & (pos < end)
        lo = jnp.where(inside, start, lo)
        hi = jnp.where(inside, ctx_end, hi)
    return lo, hi


def over_keys(lo, hi, body):
    first = lo // UNIT * UNIT
    units = jnp.maximum((hi - first + UNIT - 1) // UNIT, 0)
    whole = units // (KB // UNIT)

    def step(j, carry):
        body(first + j * KB, KB)
        return carry

    lax.fori_loop(0, whole, step, 0)
    rest = units - whole * (KB // UNIT)
    start = first + whole * KB

    @pl.when(rest >= 2)
    def _():
        body(start, 2 * UNIT)

    @pl.when(rest % 2 == 1)
    def _():
        body(start + (rest - 1) * UNIT, UNIT)


def full(shape):
    return pl.BlockSpec(shape, lambda i, *_: (0,) * len(shape), pipeline_mode=pl.Buffered(1))


def forward_kernel(
    rows, ctx, qry, tok, wq, wk, wv, bq, bv, q_o, k_o, v_o, kt_o, att_o, lse_o, qs, ks, vt, mx, sm, acc, sc
):
    i = pl.program_id(0)
    proj_steps = rows // ROWS

    @pl.when(i < proj_steps)
    def _():
        t = tok[...]
        r = pl.ds(pl.multiple_of(i * ROWS, ROWS), ROWS)
        q = (mm(t, wq[...]) + bq[...]).astype(BF)
        qs[r, :] = q
        q_o[...] = q
        k = mm(t, wk[...]).astype(BF)
        ks[r, :] = k
        k_o[...] = k
        kt_o[...] = k.T
        v = (mm(t, wv[...]) + bv[...]).astype(BF)
        v_o[...] = v
        vt[:, r] = v.T

    @pl.when(i >= proj_steps)
    def _():
        first = (i - proj_steps) * QB
        bounds = slot_bounds(ctx, qry)
        lo, hi = key_range(bounds, first, QB)
        key_lo, key_hi = row_bounds(bounds, first + lax.broadcasted_iota(jnp.int32, (1, QB), 1))
        rq = pl.ds(pl.multiple_of(first, QB), QB)
        mx[...] = jnp.full(mx.shape, NEG, F32)
        sm[...] = jnp.zeros(sm.shape, F32)
        acc[...] = jnp.zeros(acc.shape, F32)
        cols = [slice(h * HD, (h + 1) * HD) for h in range(HEADS)]
        parts = [slice(h * 8, (h + 1) * 8) for h in range(HEADS)]

        def score_pass(start, size):
            rk = pl.ds(pl.multiple_of(start, UNIT), size)
            key_pos = start + lax.broadcasted_iota(jnp.int32, (size, QB), 0)
            allowed = (key_pos >= key_lo) & (key_pos < key_hi)
            raw = [mm_t(ks[rk, c], qs[rq, c]) for c in cols]
            for h, part in enumerate(parts):
                s = jnp.where(allowed, raw[h], NEG)
                sc[h, rk, :] = s
                mx[part, :] = jnp.maximum(mx[part, :], jnp.max(s.reshape(size // 8, 8, QB), axis=0))

        over_keys(lo, hi, score_pass)
        peak = [jnp.max(mx[part, :], axis=0, keepdims=True) * SCALE2 for part in parts]

        def value_pass(start, size):
            rk = pl.ds(pl.multiple_of(start, UNIT), size)
            probs = []
            for h, part in enumerate(parts):
                p = jnp.exp2(sc[h, rk, :] * SCALE2 - peak[h])
                sm[part, :] = sm[part, :] + jnp.sum(p.reshape(size // 8, 8, QB), axis=0)
                probs.append(p.astype(BF))
            for h, c in enumerate(cols):
                acc[c, :] = acc[c, :] + mm(vt[c, rk], probs[h])

        over_keys(lo, hi, value_pass)
        padding = key_hi == 0
        own_values = vt[:, rq]
        for h, (c, part) in enumerate(zip(cols, parts)):
            total = jnp.sum(sm[part, :], axis=0, keepdims=True)
            o = jnp.where(padding, own_values[c, :].astype(F32), acc[c, :] * (1.0 / total))
            att_o[:, c] = o.T.astype(BF)
            lse_o[h : h + 1, :] = peak[h] + jnp.log2(total)


def forward(ctx, qry, tok, wq, wk, wv, bq, bv):
    rows, width = tok.shape
    ps, qn = rows // ROWS, rows // QB
    struct = jax.ShapeDtypeStruct
    proj = pl.BlockSpec((ROWS, width), lambda i, *_: (jnp.minimum(i, ps - 1), 0))
    proj_t = pl.BlockSpec((width, ROWS), lambda i, *_: (0, jnp.minimum(i, ps - 1)))
    att = pl.BlockSpec((QB, width), lambda i, *_: (jnp.maximum(i - ps, 0), 0))
    att_t = pl.BlockSpec((8, QB), lambda i, *_: (0, jnp.maximum(i - ps, 0)))
    spec = pltpu.PrefetchScalarGridSpec(
        num_scalar_prefetch=2,
        grid=(ps + qn,),
        in_specs=[proj] + [full((width, width))] * 3 + [full((1, width))] * 2,
        out_specs=[proj] * 3 + [proj_t, att, att_t],
        scratch_shapes=[
            pltpu.VMEM((rows, width), BF),
            pltpu.VMEM((rows, width), BF),
            pltpu.VMEM((width, rows), BF),
            pltpu.VMEM((8 * HEADS, QB), F32),
            pltpu.VMEM((8 * HEADS, QB), F32),
            pltpu.VMEM((width, QB), F32),
            pltpu.VMEM((HEADS, rows, QB), F32),
        ],
    )
    return pl.pallas_call(
        functools.partial(forward_kernel, rows),
        grid_spec=spec,
        out_shape=[pltpu.HBM((rows, width), BF)] * 3
        + [pltpu.HBM((width, rows), BF), pltpu.HBM((rows, width), BF), pltpu.HBM((8, rows), F32)],
        compiler_params=pltpu.CompilerParams(vmem_limit_bytes=58 << 20),
        name="attention_forward",
    )(ctx, qry, tok, wq, wk, wv, bq[None], bv[None])


def middle_kernel(
    core, ctx, qry, tok, og, att, w_out, b_out, g1, b1, w_h, b_h, w_b, b_b, g2, b2,
    out_o, dsum_o, dbr_o, keep_o, send_o, vec, pack,
):
    i = pl.program_id(0)
    total = slot_bounds(ctx, qry)[-1][2]
    row = i * ROWS + lax.broadcasted_iota(jnp.int32, (ROWS, 1), 0)
    valid = (row < total).astype(F32)
    a = att[...]
    x1 = tok[...].astype(F32) + (mm(a, w_out[...]) + b_out[...])
    xc1 = x1 - jnp.mean(x1, axis=1, keepdims=True)
    r1 = lax.rsqrt(jnp.mean(xc1 * xc1, axis=1, keepdims=True) + EPS)
    xh1 = xc1 * r1
    n1 = xh1 * g1[...] + b1[...]
    nl = n1.astype(BF)
    hp = mm(nl, w_h[...]) + b_h[...]
    cdf = 0.5 * (1.0 + lax.erf(hp * (1.0 / math.sqrt(2.0))))
    act = (hp * cdf).astype(BF)
    slope = cdf + hp * (jnp.exp(-0.5 * hp * hp) * (1.0 / math.sqrt(2.0 * math.pi)))
    x2 = n1 + (mm(act, w_b[...]) + b_b[...])
    xc2 = x2 - jnp.mean(x2, axis=1, keepdims=True)
    r2 = lax.rsqrt(jnp.mean(xc2 * xc2, axis=1, keepdims=True) + EPS)
    xh2 = xc2 * r2
    out_o[...] = ((xh2 * g2[...] + b2[...]) * valid).astype(BF)
    dy = og[...].astype(F32) * valid
    dg2 = jnp.sum(dy * xh2, axis=0, keepdims=True)
    db2 = jnp.sum(dy, axis=0, keepdims=True)
    dx = dy * g2[...]
    d2 = r2 * (dx - jnp.mean(dx, axis=1, keepdims=True) - xh2 * jnp.mean(dx * xh2, axis=1, keepdims=True))
    df = d2.astype(BF)
    dbb = jnp.sum(df.astype(F32), axis=0, keepdims=True)
    dh = (mm_t(df, w_b[...]) * slope).astype(BF)
    dbh = jnp.sum(dh.astype(F32), axis=0, keepdims=True)
    dn = d2 + mm_t(dh, w_h[...])
    dg1 = jnp.sum(dn * xh1, axis=0, keepdims=True)
    db1 = jnp.sum(dn, axis=0, keepdims=True)
    dx1 = dn * g1[...]
    ds = r1 * (dx1 - jnp.mean(dx1, axis=1, keepdims=True) - xh1 * jnp.mean(dx1 * xh1, axis=1, keepdims=True))
    dsum_o[...] = ds
    dbr = ds.astype(BF)
    dbo = jnp.sum(dbr.astype(F32), axis=0, keepdims=True)
    dbr_o[...] = dbr
    width = dbr.shape[1]

    @pl.when(i == 0)
    def _():
        pack[...] = jnp.zeros(pack.shape, F32)
        vec[...] = jnp.zeros(vec.shape, F32)

    def add(row, value):
        for r in range(0, value.shape[0], PIECE):
            half, at = divmod(row + r, pack.shape[1])
            pack[half, at : at + PIECE, :] += value[r : r + PIECE]

    ff = act.shape[1]
    add(0, t_mm(act, df))
    for n in range(ff // width):
        add(ff + n * width, t_mm(nl, dh[:, n * width : (n + 1) * width]))
    add(2 * ff, t_mm(a, dbr))
    for n, v in enumerate((dbo, dg1, db1, dbh[:, :width], dbh[:, width:], dbb, dg2, db2)):
        vec[n : n + 1, :] += v

    @pl.when(i == pl.num_programs(0) - 1)
    def _():
        keep_o[...] = pack[core[0]]
        send_o[...] = pack[1 - core[0]]


def middle(core, ctx, qry, tok, og, att, w_out, b_out, g1, b1, w_h, b_h, w_b, b_b, g2, b2):
    rows, width = tok.shape
    ff = w_h.shape[1]
    half = ff + width // 2
    struct = jax.ShapeDtypeStruct
    row = pl.BlockSpec((ROWS, width), lambda i, *_: (i, 0))
    vec = full((1, width))
    spec = pltpu.PrefetchScalarGridSpec(
        num_scalar_prefetch=3,
        grid=(rows // ROWS,),
        in_specs=[row] * 3
        + [full((width, width)), vec, vec, vec, full((width, ff)), full((1, ff)), full((ff, width)), vec, vec, vec],
        out_specs=[row] * 3
        + [full((half, width)), full((half, width)), full((8, width))],
        scratch_shapes=[pltpu.VMEM((2, half, width), F32)],
    )
    return pl.pallas_call(
        middle_kernel,
        grid_spec=spec,
        out_shape=[
            pltpu.HBM((rows, width), BF),
            pltpu.HBM((rows, width), F32),
            struct((rows, width), BF),
            struct((half, width), F32),
            struct((half, width), F32),
            struct((8, width), F32),
        ],
        compiler_params=pltpu.CompilerParams(vmem_limit_bytes=40 << 20),
        name="ffn_and_norms",
    )(
        core, ctx, qry, tok, og, att, w_out, b_out[None], g1[None], b1[None], w_h, b_h[None], w_b, b_b[None],
        g2[None], b2[None],
    )


def attended_grad_kernel(att, dbr, w_out, datt_o, delta_o):
    da = mm_t(dbr[...], w_out[...]).astype(BF)
    datt_o[...] = da
    prod = att[...].astype(F32) * da.astype(F32)
    prod_hi = prod.astype(BF)
    prod_lo = (prod - prod_hi.astype(F32)).astype(BF)
    width = prod.shape[1]
    head_of = lax.broadcasted_iota(jnp.int32, (8, width), 1) // HD
    pick = (head_of == lax.broadcasted_iota(jnp.int32, (8, width), 0)).astype(BF)
    delta_o[...] = mm_t(pick, prod_hi) + mm_t(pick, prod_lo)


def attended_grad(att, dbr, w_out):
    rows, width = att.shape
    row = pl.BlockSpec((ROWS, width), lambda i: (i, 0))
    return pl.pallas_call(
        attended_grad_kernel,
        grid=(rows // ROWS,),
        in_specs=[row, row, full((width, width))],
        out_specs=[row, pl.BlockSpec((8, ROWS), lambda i: (0, i))],
        out_shape=[pltpu.HBM((rows, width), BF), pltpu.HBM((8, rows), F32)],
        compiler_params=pltpu.CompilerParams(vmem_limit_bytes=20 << 20),
        cost_estimate=LIGHT,
        name="attended_gradient",
    )(att, dbr, w_out)


def backward_kernel(
    rows, heads, ctx, qry, tok, q, k, kt, v, do, lse, delta, dq_o, dk_o, dv_o, dqt, dka, dva
):
    i = pl.program_id(0)
    steps = rows // QB
    width = heads * HD
    bounds = slot_bounds(ctx, qry)

    @pl.when(i == 0)
    def _():
        dka[...] = jnp.zeros(dka.shape, F32)
        dva[...] = jnp.zeros(dva.shape, F32)

    @pl.when(i < steps)
    def _():
        first = i * QB
        lo, hi = key_range(bounds, first, QB)
        key_lo, key_hi = row_bounds(bounds, first + lax.broadcasted_iota(jnp.int32, (1, QB), 1))
        rq = pl.ds(pl.multiple_of(first, QB), QB)
        dqt[...] = jnp.zeros(dqt.shape, F32)
        cols = [slice(h * HD, (h + 1) * HD) for h in range(heads)]

        def body(start, size):
            rk = pl.ds(pl.multiple_of(start, UNIT), size)
            key_pos = start + lax.broadcasted_iota(jnp.int32, (size, QB), 0)
            allowed = (key_pos >= key_lo) & (key_pos < key_hi)
            scores = [mm_t(k[rk, c], q[rq, c]) for c in cols]
            dprobs = [mm_t(v[rk, c], do[rq, c]) for c in cols]
            probs = []
            dscores = []
            for h in range(heads):
                p = jnp.where(allowed, jnp.exp2(scores[h] * SCALE2 - lse[h : h + 1, rq]), 0.0)
                probs.append(p.astype(BF))
                dscores.append((p * (dprobs[h] - delta[h : h + 1, rq])).astype(BF))
            for h, c in enumerate(cols):
                dva[rk, c] += mm(probs[h], do[rq, c])
                dka[rk, c] += mm(dscores[h], q[rq, c])
                dqt[c, :] += mm(kt[c, rk], dscores[h])

        over_keys(lo, hi, body)
        dq_o[rq, :] = (dqt[...] * SCALE).T.astype(BF)

    @pl.when(i == steps)
    def _():
        padding = lax.broadcasted_iota(jnp.int32, (rows, 1), 0) >= bounds[-1][2]
        dk_o[...] = (dka[...] * SCALE).astype(BF)
        dv_o[...] = (dva[...] + jnp.where(padding, do[...].astype(F32), 0.0)).astype(BF)


def backward(ctx, qry, tok, q, k, kt, v, do, lse, delta):
    rows, width = tok.shape
    struct = jax.ShapeDtypeStruct
    whole = full((rows, width))
    spec = pltpu.PrefetchScalarGridSpec(
        num_scalar_prefetch=2,
        grid=(rows // QB + 1,),
        in_specs=[whole, whole, whole, full((width, rows)), whole, whole, full((8, rows)), full((8, rows))],
        out_specs=[whole] * 3,
        scratch_shapes=[
            pltpu.VMEM((width, QB), F32),
            pltpu.VMEM((rows, width), F32),
            pltpu.VMEM((rows, width), F32),
        ],
    )
    return pl.pallas_call(
        functools.partial(backward_kernel, rows, HEADS),
        grid_spec=spec,
        out_shape=[struct((rows, width), BF)] * 3,
        compiler_params=pltpu.CompilerParams(vmem_limit_bytes=34 << 20),
        cost_estimate=pl.CostEstimate(flops=30 * 10**9, bytes_accessed=20 << 20, transcendentals=8 << 20),
        name="attention_backward",
    )(ctx, qry, tok, q, k, kt, v, do, lse, delta)


def input_grad_kernel(ds, dq, dk, dv, wq, wk, wv, o):
    total = ds[...] + mm_t(dq[...], wq[...]) + mm_t(dk[...], wk[...]) + mm_t(dv[...], wv[...])
    o[...] = total.astype(BF)


def input_gradient(ds, dq, dk, dv, wq, wk, wv):
    rows, width = ds.shape
    row = pl.BlockSpec((ROWS, width), lambda i: (i, 0))
    square = pl.BlockSpec((width, width), lambda i: (0, 0))
    return pl.pallas_call(
        input_grad_kernel,
        grid=(rows // ROWS,),
        in_specs=[row] * 4 + [square] * 3,
        out_specs=row,
        out_shape=jax.ShapeDtypeStruct((rows, width), BF),
        compiler_params=pltpu.CompilerParams(vmem_limit_bytes=48 << 20),
        cost_estimate=LIGHT,
        name="input_gradient",
    )(ds, dq, dk, dv, wq, wk, wv)


def projection_kernel(core, tok, dq, dk, dv, vec, keep_o, small, *rest):
    sends, acc = rest[:-1], rest[-1]
    i = pl.program_id(0)

    @pl.when(i == 0)
    def _():
        acc[...] = jnp.zeros(acc.shape, F32)
        small[0:8, :] = vec[...]
        small[8:, :] = jnp.zeros((small.shape[0] - 8, small.shape[1]), F32)

    t = tok[...]
    width = t.shape[1]
    for n, g in enumerate((dq, dk, dv)):
        value = t_mm(t, g[...])
        for r in range(0, width, PIECE):
            half, at = divmod(n * width + r, acc.shape[1])
            acc[half, at : at + PIECE, :] += value[r : r + PIECE]
    small[8:9, :] += jnp.sum(dq[...].astype(F32), axis=0, keepdims=True)
    small[9:10, :] += jnp.sum(dv[...].astype(F32), axis=0, keepdims=True)

    @pl.when(i == pl.num_programs(0) - 1)
    def _():
        keep_o[...] = acc[core[0]]
        for n, send in enumerate(sends):
            send[...] = acc[1 - core[0], n * SEND : (n + 1) * SEND, :]


def projection_gradients(core, tok, dq, dk, dv, vec):
    rows, width = tok.shape
    half = 3 * width // 2
    struct = jax.ShapeDtypeStruct
    row = pl.BlockSpec((2 * ROWS, width), lambda i, *_: (i, 0))
    spec = pltpu.PrefetchScalarGridSpec(
        num_scalar_prefetch=1,
        grid=(rows // (2 * ROWS),),
        in_specs=[row] * 4 + [full((8, width))],
        out_specs=[full((half, width)), full((SMALL, width))] + [full((SEND, width))] * (half // SEND),
        scratch_shapes=[pltpu.VMEM((2, half, width), F32)],
    )
    return pl.pallas_call(
        projection_kernel,
        grid_spec=spec,
        out_shape=[
            struct((half, width), F32),
            struct((SMALL, width), F32),
        ]
        + [struct((SEND, width), F32)] * (half // SEND),
        compiler_params=pltpu.CompilerParams(vmem_limit_bytes=32 << 20),
        cost_estimate=LIGHT,
        name="projection_gradients",
    )(core, tok, dq, dk, dv, vec)


def split_kernel(where, *refs):
    for n in range(4):
        refs[8 + n][...] = refs[n][0] + refs[4 + n][0]


def add_and_split(where, x, got):
    rows, cols = x.shape[0] // 4, x.shape[1]
    step = rows // 2 if rows % 16 == 0 else rows
    ins = [pl.BlockSpec((1, step, cols), lambda i, w, n=n: (w[n], i, 0)) for n in range(4)]
    spec = pltpu.PrefetchScalarGridSpec(
        num_scalar_prefetch=1,
        grid=(rows // step,),
        in_specs=ins + ins,
        out_specs=[pl.BlockSpec((step, cols), lambda i, w: (i, 0))] * 4,
    )
    return pl.pallas_call(
        split_kernel,
        grid_spec=spec,
        out_shape=[jax.ShapeDtypeStruct((rows, cols), F32)] * 4,
        compiler_params=pltpu.CompilerParams(vmem_limit_bytes=32 << 20),
        name="add_and_split",
    )(where, *[x.reshape(4, rows, cols)] * 4, *[got.reshape(4, rows, cols)] * 4)


def split_small_kernel(where, x, small, got_small, *rest):
    gots, outs, total = rest[:-5], rest[-5:-1], rest[-1]
    rows = x.shape[0] // 4
    for n, got in enumerate(gots):
        at = slice(n * SEND, (n + 1) * SEND)
        total[at, :] = x[at, :] + got[...]
    for n in range(4):
        outs[n][:rows, :] = total[pl.ds(pl.multiple_of(where[n] * rows, 8), rows), :]
        outs[n][rows:, :] = small[...] + got_small[...]


def add_and_split_small(where, x, small, got_small, *gots):
    rows, cols = x.shape[0] // 4, x.shape[1]
    whole = pl.BlockSpec(memory_space=pltpu.VMEM)
    return pl.pallas_call(
        split_small_kernel,
        in_specs=[pl.BlockSpec(memory_space=pltpu.SMEM)] + [whole] * (3 + len(gots)),
        out_specs=[whole] * 4,
        out_shape=[jax.ShapeDtypeStruct((rows + small.shape[0], cols), F32)] * 4,
        scratch_shapes=[pltpu.VMEM(x.shape, F32)],
        compiler_params=pltpu.CompilerParams(vmem_limit_bytes=16 << 20),
        name="add_and_split_small",
    )(where, x, small, got_small, *gots)


def unpack_kernel(places, piece, order, *refs):
    sources, outs, held, in_sem, out_sem = refs[:4], refs[4:-3], refs[-3], refs[-2], refs[-1]

    def loads(n):
        return pltpu.make_async_copy(sources[n], held.at[n], in_sem.at[n])

    def copies(n, p):
        made = []
        for start, count, out, row, col in places:
            if start // piece == p:
                to = outs[out].at[pl.ds(row, count), pl.ds(col, held.shape[2])]
                from_ = held.at[n, pl.ds(start % piece, count)]
                made.append(pltpu.make_async_copy(from_, to, out_sem.at[n, len(made)]))
        return made

    for n in range(4):
        loads(n).start()
    for action in ("start", "wait"):
        for n in range(4):
            if action == "start":
                loads(n).wait()
            for p in range(4):

                @pl.when(order[n] == p)
                def _(n=n, p=p):
                    for c in copies(n, p):
                        c.start() if action == "start" else c.wait()


def unpack(places, shapes, order, sources):
    anywhere = pl.BlockSpec(memory_space=pl.ANY)
    piece = sources[0].shape[0]
    places = cut(places, piece)
    most = max(sum(p[0] // piece == n for p in places) for n in range(4))
    return pl.pallas_call(
        functools.partial(unpack_kernel, places, piece),
        in_specs=[pl.BlockSpec(memory_space=pltpu.SMEM)] + [anywhere] * 4,
        out_specs=[anywhere] * len(shapes),
        out_shape=[jax.ShapeDtypeStruct(s, F32) for s in shapes],
        scratch_shapes=[
            pltpu.VMEM((4,) + sources[0].shape, F32),
            pltpu.SemaphoreType.DMA((4,)),
            pltpu.SemaphoreType.DMA((4, most)),
        ],
        compiler_params=pltpu.CompilerParams(vmem_limit_bytes=24 << 20),
        name="unpack",
    )(order, *sources)


def swap_pairs(sizes, mask):
    dp, dq = sizes
    return [(p * dq + q, p * dq + (q ^ mask[p % 2])) for p in range(dp) for q in range(dq)]


class Ring:
    def __init__(self, sizes):
        dp, dq = sizes
        self.sizes = sizes
        self.core = lax.axis_index("dp") & 1
        me = lax.axis_index("dq")
        first, second = me & 1, (me >> 1) & 1
        self.low = jnp.where(self.core == 0, first, second)
        self.high = jnp.where(self.core == 0, second, first)
        place = 2 * self.high + self.low
        turned = [place ^ jnp.where(self.core == 0, a, b) for a, b in ((0, 0), (1, 2), (2, 1), (3, 3))]
        self.where = jnp.stack(turned).astype(jnp.int32)
        mine, other = 2 * self.core, 2 - 2 * self.core
        high = jnp.where(self.core == 0, first, second)
        self.order = jnp.stack(
            [mine + self.high, mine + 1 - self.high, other + high, other + 1 - high]
        ).astype(jnp.int32)
        bits = list(range(2, dq.bit_length() - 1))
        swapped = bits[1::-1] + bits[2:]
        self.far = [swap_pairs(sizes, (1 << a, 1 << b)) for a, b in zip(bits, swapped)]
        self.outer = [[(p, p ^ (1 << b)) for p in range(dp)] for b in range(1, dp.bit_length() - 1)]

    def core_start(self, send):
        return lax.ppermute(send, "dp", [(p, p ^ 1) for p in range(self.sizes[0])])

    def plane_start(self, sends):
        return [
            lax.ppermute(s, ("dp", "dq"), swap_pairs(self.sizes, (m, m))) for m, s in zip((1, 2, 3), sends)
        ]

    def plane_end(self, own, got):
        return (own + got[0]) + (got[1] + got[2])

    def far_start(self, x, n):
        return lax.ppermute(x, ("dp", "dq"), self.far[n])

    def rest(self, x):
        for pairs in self.far[2:]:
            x = x + lax.ppermute(x, ("dp", "dq"), pairs)
        for pairs in self.outer:
            x = x + lax.ppermute(x, "dp", pairs)
        return x

    def back_start(self, x, n):
        return lax.ppermute(x, ("dp", "dq"), swap_pairs(self.sizes, ((1, 2), (2, 1))[n]))

    def back_end(self, x, got, n):
        bit = (self.low, self.high)[n]
        return jnp.where(bit == 0, jnp.concatenate([x, got]), jnp.concatenate([got, x]))


def tie(*groups):
    return lax.optimization_barrier(groups)


def local(
    sizes, tokens, out_grad, context_len, query_count, w_query, w_key, w_value, b_query, b_value, w_out, b_out,
    norm1_gain, norm1_bias, w_hidden, b_hidden, w_back, b_back, norm2_gain, norm2_bias,
):
    width = tokens.shape[1]
    ff = w_hidden.shape[1]
    ring = Ring(sizes)
    tokens, out_grad, w_query, w_key, w_value, w_out, w_hidden, w_back = [
        pltpu.with_memory_space_constraint(x, pltpu.HBM)
        for x in (tokens, out_grad, w_query, w_key, w_value, w_out, w_hidden, w_back)
    ]
    core = ring.core.reshape(1).astype(jnp.int32)
    q, k, v, kt, att, lse = forward(
        context_len, query_count, tokens, w_query, w_key, w_value, b_query, b_value
    )
    output, ds, dbr, keep, send, vec = middle(
        core, context_len, query_count, tokens, out_grad, att, w_out, b_out, norm1_gain, norm1_bias,
        w_hidden, b_hidden, w_back, b_back, norm2_gain, norm2_bias,
    )
    got = ring.core_start(send)
    send, att, dbr = tie(send, att, dbr)
    datt, delta = attended_grad(att, dbr, w_out)
    got, datt, delta = tie(got, datt, delta)
    one, *sends = add_and_split(ring.where, keep, got)
    got_one = ring.plane_start(sends)
    one, ins = tie(one, (context_len, query_count, tokens, q, k, kt, v, datt, lse, delta))
    dq, dk, dv = backward(*ins)
    one, got_one, dq, dk, dv = tie(one, got_one, dq, dk, dv)
    one = ring.plane_end(one, got_one)
    got_one = ring.far_start(one, 0)
    one, dq, dk, dv = tie(one, dq, dk, dv)
    keep, small, *sends = projection_gradients(core, tokens, dq, dk, dv, vec)
    got = [ring.core_start(s) for s in [small] + sends]
    one = one + got_one
    middle_row = one.shape[0] // 2
    got_one = [ring.far_start(x, 1) for x in (one[:middle_row], one[middle_row:])]
    two, *sends = add_and_split_small(ring.where, keep, small, *got)
    got_two = ring.plane_start(sends)
    one, two, sends, dq, dk, dv, ds = tie(one, two, sends, dq, dk, dv, ds)
    input_grad = input_gradient(ds, dq, dk, dv, w_query, w_key, w_value)
    one, got_one, two, got_two, input_grad = tie(one, got_one, two, got_two, input_grad)
    one = ring.rest(one + jnp.concatenate(got_one))
    got_one = ring.back_start(one, 0)
    two = ring.plane_end(two, got_two)
    got_two = ring.far_start(two, 0)
    one, got_one, two, got_two = tie(one, got_one, two, got_two)
    one = ring.back_end(one, got_one, 0)
    got_one = ring.back_start(one, 1)
    home_one = ring.core_start(one)
    two = two + got_two
    got_two = ring.far_start(two, 1)
    one, two, got_two = tie(one, two, got_two)
    two = ring.rest(two + got_two)
    small = two[-SMALL:]
    two = two[:-SMALL]
    vectors = [small[n] for n in (8, 9, 0, 1, 2)] + [small[3:5].reshape(-1)] + [small[n] for n in (5, 6, 7)]
    got_two = ring.back_start(two, 0)
    one, got_one, home_one, two, got_two = tie(one, got_one, home_one, two, got_two)
    two = ring.back_end(two, got_two, 0)
    got_two = ring.back_start(two, 1)
    home_two = ring.core_start(two)
    last_one = ring.core_start(got_one)
    places = [(0, ff, 0, 0, 0)]
    places += [(ff + n * width, width, 1, 0, n * width) for n in range(ff // width)]
    places += [(2 * ff, width, 2, 0, 0)]
    shapes = [(ff, width), (width, ff), (width, width)]
    gwb, gwh, gwo = unpack(places, shapes, ring.order, (one, got_one, home_one, last_one))
    two, got_two, home_two, gwb, gwh, gwo, vectors = tie(two, got_two, home_two, gwb, gwh, gwo, vectors)
    places = [(n * width, width, n, 0, 0) for n in range(3)]
    last_two = ring.core_start(got_two)
    gq, gk, gv = unpack(places, [(width, width)] * 3, ring.order, (two, got_two, home_two, last_two))
    return (
        output,
        input_grad,
        gq,
        gk,
        gv,
        vectors[0],
        vectors[1],
        gwo,
        vectors[2],
        vectors[3],
        vectors[4],
        gwh,
        vectors[5],
        gwb,
        vectors[6],
        vectors[7],
        vectors[8],
    )


def cut(places, piece):
    out = []
    for start, rows, to, row, col in places:
        at = start
        while at < start + rows:
            end = min((at // piece + 1) * piece, start + rows)
            out.append((at, end - at, to, row + at - start, col))
            at = end
    return out


def solution(mesh):
    sizes = (mesh.shape["dp"], mesh.shape["dq"])
    return jax.shard_map(
        functools.partial(local, sizes),
        mesh=mesh,
        in_specs=(
            P(("dp", "dq"), None),
            P(("dp", "dq"), None),
            P(("dp", "dq"), None),
            P(("dp", "dq"), None),
            P(),
            P(),
            P(),
            P(),
            P(),
            P(),
            P(),
            P(),
            P(),
            P(),
            P(),
            P(),
            P(),
            P(),
            P(),
        ),
        out_specs=(
            P(("dp", "dq"), None),
            P(("dp", "dq"), None),
            P(),
            P(),
            P(),
            P(),
            P(),
            P(),
            P(),
            P(),
            P(),
            P(),
            P(),
            P(),
            P(),
            P(),
            P(),
        ),
        check_vma=False,
    )
```

```python
import functools
import math

import jax
import jax.experimental.pallas as pl
import jax.experimental.pallas.tpu as pltpu
import jax.numpy as jnp
from jax import lax
from jax.sharding import PartitionSpec as P

HEADS = 4
HD = 128
SLOTS = 8
EPS = 1e-5
SCALE = 1.0 / math.sqrt(HD)
SCALE2 = SCALE * math.log2(math.e)
NEG = -1e30
F32 = jnp.float32
BF = jnp.bfloat16
ROWS = 512
QF = 512
QB = 256
KB = 1024
KB_BACK = 1024
UNIT = 128
PROJ = 1024
ATT = 2
PIECE = 256
LIGHT = pl.CostEstimate(flops=1, bytes_accessed=1, transcendentals=0)
SMALL = 16
SEND = 128


def mm(a, b):
    return jnp.dot(a, b, preferred_element_type=F32)


def mm_t(a, b):
    return lax.dot_general(a, b, (((1,), (1,)), ((), ())), preferred_element_type=F32)


def t_mm(a, b):
    return lax.dot_general(a, b, (((0,), (0,)), ((), ())), preferred_element_type=F32)


def slot_bounds(ctx, qry):
    out = []
    start = jnp.int32(0)
    for t in range(SLOTS):
        c = ctx[0, t]
        end = start + c + qry[0, t]
        out.append((start, start + c, end))
        start = end
    return out


def key_range(bounds, first, rows):
    lo = jnp.int32(1 << 30)
    hi = jnp.int32(0)
    for start, ctx_end, end in bounds:
        hit = (start < first + rows) & (end > first) & (end > start)
        lo = jnp.where(hit, jnp.minimum(lo, start), lo)
        hi = jnp.where(hit, jnp.maximum(hi, ctx_end), hi)
    return lo, hi


def row_bounds(bounds, pos):
    lo = jnp.zeros(pos.shape, jnp.int32)
    hi = jnp.zeros(pos.shape, jnp.int32)
    for start, ctx_end, end in bounds:
        inside = (pos >= start) & (pos < end)
        lo = jnp.where(inside, start, lo)
        hi = jnp.where(inside, ctx_end, hi)
    return lo, hi


def over_keys(lo, hi, most, body):
    start = lo // UNIT * UNIT
    units = jnp.maximum((hi - start + UNIT - 1) // UNIT, 0)
    whole = units // (most // UNIT)

    def step(j, carry):
        body(start + j * most, most)
        return carry

    lax.fori_loop(0, whole, step, 0)
    done = whole * (most // UNIT)
    size = most // 2
    while size >= UNIT:
        take = (units - done) // (size // UNIT)
        pl.when(take > 0)(functools.partial(body, start + done * UNIT, size))
        done = done + take * (size // UNIT)
        size //= 2


def full(shape):
    return pl.BlockSpec(shape, lambda i, *_: (0,) * len(shape), pipeline_mode=pl.Buffered(1))


def forward_kernel(
    rows, ctx, qry, tok, wq, wk, wv, bq, bv, q_o, k_o, v_o, kt_o, att_o, lse_o, qs, ks, vt, mx, sm, acc, sc
):
    i = pl.program_id(0)
    proj_steps = rows // PROJ

    @pl.when(i < proj_steps)
    def _():
        t = tok[...]
        r = pl.ds(pl.multiple_of(i * PROJ, PROJ), PROJ)
        q = (mm(t, wq[...]) + bq[...]).astype(BF)
        qs[r, :] = q
        q_o[...] = q
        k = mm(t, wk[...]).astype(BF)
        ks[r, :] = k
        k_o[...] = k
        kt_o[...] = k.T
        v = (mm(t, wv[...]) + bv[...]).astype(BF)
        v_o[...] = v
        vt[:, r] = v.T

    def attend(n, carry):
        first = (i - proj_steps) * (ATT * QF) + n * QF
        bounds = slot_bounds(ctx, qry)
        lo, hi = key_range(bounds, first, QF)
        key_lo, key_hi = row_bounds(bounds, first + lax.broadcasted_iota(jnp.int32, (1, QF), 1))
        rq = pl.ds(pl.multiple_of(first, QF), QF)
        mx[...] = jnp.full(mx.shape, NEG, F32)
        sm[...] = jnp.zeros(sm.shape, F32)
        acc[...] = jnp.zeros(acc.shape, F32)
        cols = [slice(h * HD, (h + 1) * HD) for h in range(HEADS)]
        parts = [slice(h * 8, (h + 1) * 8) for h in range(HEADS)]

        def score_pass(start, size):
            rk = pl.ds(pl.multiple_of(start, UNIT), size)
            key_pos = start + lax.broadcasted_iota(jnp.int32, (size, QF), 0)
            allowed = (key_pos >= key_lo) & (key_pos < key_hi)
            raw = [mm_t(ks[rk, c], qs[rq, c]) for c in cols]
            for h, part in enumerate(parts):
                s = jnp.where(allowed, raw[h], NEG)
                sc[h, rk, :] = s
                mx[part, :] = jnp.maximum(mx[part, :], jnp.max(s.reshape(size // 8, 8, QF), axis=0))

        over_keys(lo, hi, KB, score_pass)
        peak = [jnp.max(mx[part, :], axis=0, keepdims=True) * SCALE2 for part in parts]

        def value_pass(start, size):
            rk = pl.ds(pl.multiple_of(start, UNIT), size)
            probs = []
            for h, part in enumerate(parts):
                p = jnp.exp2(sc[h, rk, :] * SCALE2 - peak[h])
                sm[part, :] = sm[part, :] + jnp.sum(p.reshape(size // 8, 8, QF), axis=0)
                probs.append(p.astype(BF))
            for h, c in enumerate(cols):
                acc[c, :] = acc[c, :] + mm(vt[c, rk], probs[h])

        over_keys(lo, hi, KB, value_pass)
        here = pl.ds(pl.multiple_of(n * QF, QF), QF)
        padding = key_hi == 0
        own_values = vt[:, rq]
        for h, (c, part) in enumerate(zip(cols, parts)):
            total = jnp.sum(sm[part, :], axis=0, keepdims=True)
            o = jnp.where(padding, own_values[c, :].astype(F32), acc[c, :] * (1.0 / total))
            att_o[here, c] = o.T.astype(BF)
            lse_o[h : h + 1, here] = peak[h] + jnp.log2(total)
        return carry

    @pl.when(i >= proj_steps)
    def _():
        lax.fori_loop(0, ATT, attend, 0)


def forward(ctx, qry, tok, wq, wk, wv, bq, bv):
    rows, width = tok.shape
    ps, qn = rows // PROJ, rows // (ATT * QF)
    struct = jax.ShapeDtypeStruct
    proj = pl.BlockSpec((PROJ, width), lambda i, *_: (jnp.minimum(i, ps - 1), 0))
    proj_t = pl.BlockSpec((width, PROJ), lambda i, *_: (0, jnp.minimum(i, ps - 1)))
    att = pl.BlockSpec((ATT * QF, width), lambda i, *_: (jnp.maximum(i - ps, 0), 0))
    att_t = pl.BlockSpec((8, ATT * QF), lambda i, *_: (0, jnp.maximum(i - ps, 0)))
    spec = pltpu.PrefetchScalarGridSpec(
        num_scalar_prefetch=2,
        grid=(ps + qn,),
        in_specs=[proj] + [full((width, width))] * 3 + [full((1, width))] * 2,
        out_specs=[proj] * 3 + [proj_t, att, att_t],
        scratch_shapes=[
            pltpu.VMEM((rows, width), BF),
            pltpu.VMEM((rows, width), BF),
            pltpu.VMEM((width, rows), BF),
            pltpu.VMEM((8 * HEADS, QF), F32),
            pltpu.VMEM((8 * HEADS, QF), F32),
            pltpu.VMEM((width, QF), F32),
            pltpu.VMEM((HEADS, rows, QF), F32),
        ],
    )
    return pl.pallas_call(
        functools.partial(forward_kernel, rows),
        grid_spec=spec,
        out_shape=[pltpu.HBM((rows, width), BF)] * 3
        + [pltpu.HBM((width, rows), BF), pltpu.HBM((rows, width), BF), pltpu.HBM((8, rows), F32)],
        compiler_params=pltpu.CompilerParams(vmem_limit_bytes=58 << 20),
        name="attention_forward",
    )(ctx, qry, tok, wq, wk, wv, bq[None], bv[None])


def middle_kernel(
    core, ctx, qry, tok, og, att, w_out, b_out, g1, b1, w_h, b_h, w_b, b_b, g2, b2,
    out_o, dsum_o, dbr_o, keep_o, send_o, vec, pack,
):
    i = pl.program_id(0)
    total = slot_bounds(ctx, qry)[-1][2]
    width = tok.shape[1]
    ff = w_h.shape[1]
    count = 2
    sub = ROWS // count
    rows = [slice(n * sub, (n + 1) * sub) for n in range(count)]

    @pl.when(i == 0)
    def _():
        pack[...] = jnp.zeros(pack.shape, F32)
        vec[...] = jnp.zeros(vec.shape, F32)

    def add(row, value):
        for r in range(0, value.shape[0], PIECE):
            half, at = divmod(row + r, pack.shape[1])
            pack[half, at : at + PIECE, :] += value[r : r + PIECE]

    def mean(x):
        return jnp.mean(x, axis=1, keepdims=True)

    def each(f, *lists):
        return [f(*xs) for xs in zip(*lists)]

    def split(pairs):
        return [list(xs) for xs in zip(*pairs)]

    def cols(lists):
        return sum(jnp.sum(x.astype(F32), axis=0, keepdims=True) for x in lists)

    def first_norm(r, branch):
        x1 = tok[r, :].astype(F32) + (branch + b_out[...])
        xc1 = x1 - mean(x1)
        r1 = lax.rsqrt(mean(xc1 * xc1) + EPS)
        xh1 = xc1 * r1
        n1 = xh1 * g1[...] + b1[...]
        return r1, xh1, n1, n1.astype(BF)

    def gelu(hp):
        hp = hp + b_h[...]
        cdf = 0.5 * (1.0 + lax.erf(hp * (1.0 / math.sqrt(2.0))))
        slope = cdf + hp * (jnp.exp(-0.5 * hp * hp) * (1.0 / math.sqrt(2.0 * math.pi)))
        return (hp * cdf).astype(BF), slope

    def second_norm(r, n1, ffn):
        row = i * ROWS + r.start + lax.broadcasted_iota(jnp.int32, (sub, 1), 0)
        valid = (row < total).astype(F32)
        x2 = n1 + (ffn + b_b[...])
        xc2 = x2 - mean(x2)
        r2 = lax.rsqrt(mean(xc2 * xc2) + EPS)
        xh2 = xc2 * r2
        out_o[r, :] = ((xh2 * g2[...] + b2[...]) * valid).astype(BF)
        dy = og[r, :].astype(F32) * valid
        dx = dy * g2[...]
        d2 = r2 * (dx - mean(dx) - xh2 * mean(dx * xh2))
        dg2 = jnp.sum(dy * xh2, axis=0, keepdims=True)
        return d2, d2.astype(BF), dg2, jnp.sum(dy, axis=0, keepdims=True)

    def first_norm_back(r, r1, xh1, d2, dhn):
        dn = d2 + dhn
        dx1 = dn * g1[...]
        ds = r1 * (dx1 - mean(dx1) - xh1 * mean(dx1 * xh1))
        dsum_o[r, :] = ds
        dbr = ds.astype(BF)
        dbr_o[r, :] = dbr
        dg1 = jnp.sum(dn * xh1, axis=0, keepdims=True)
        return dbr, dg1, jnp.sum(dn, axis=0, keepdims=True)

    branch = [mm(att[r, :], w_out[...]) for r in rows]
    r1, xh1, n1, nl = split(each(first_norm, rows, branch))
    act, slope = split(each(gelu, [mm(x, w_h[...]) for x in nl]))
    ffn = [mm(x, w_b[...]) for x in act]
    d2, df, dg2, db2 = split(each(second_norm, rows, n1, ffn))
    dact = [mm_t(x, w_b[...]) for x in df]
    add(0, t_mm(jnp.concatenate(act), jnp.concatenate(df)))
    dh = each(lambda x, s: (x * s).astype(BF), dact, slope)
    dhn = [mm_t(x, w_h[...]) for x in dh]
    nl, dh_all = jnp.concatenate(nl), jnp.concatenate(dh)
    for n in range(ff // width):
        add(ff + n * width, t_mm(nl, dh_all[:, n * width : (n + 1) * width]))
    dbr, dg1, db1 = split(each(first_norm_back, rows, r1, xh1, d2, dhn))
    add(2 * ff, t_mm(att[...], jnp.concatenate(dbr)))
    dbo, dbh, dbb = cols(dbr), cols(dh), cols(df)
    dg1, db1, dg2, db2 = cols(dg1), cols(db1), cols(dg2), cols(db2)
    for n, v in enumerate((dbo, dg1, db1, dbh[:, :width], dbh[:, width:], dbb, dg2, db2)):
        vec[n : n + 1, :] += v

    @pl.when(i == pl.num_programs(0) - 1)
    def _():
        keep_o[...] = pack[core[0]]
        send_o[...] = pack[1 - core[0]]


def middle(core, ctx, qry, tok, og, att, w_out, b_out, g1, b1, w_h, b_h, w_b, b_b, g2, b2):
    rows, width = tok.shape
    ff = w_h.shape[1]
    half = ff + width // 2
    struct = jax.ShapeDtypeStruct
    row = pl.BlockSpec((ROWS, width), lambda i, *_: (i, 0))
    vec = full((1, width))
    spec = pltpu.PrefetchScalarGridSpec(
        num_scalar_prefetch=3,
        grid=(rows // ROWS,),
        in_specs=[row] * 3
        + [full((width, width)), vec, vec, vec, full((width, ff)), full((1, ff)), full((ff, width)), vec, vec, vec],
        out_specs=[row] * 3
        + [full((half, width)), full((half, width)), full((8, width))],
        scratch_shapes=[pltpu.VMEM((2, half, width), F32)],
    )
    return pl.pallas_call(
        middle_kernel,
        grid_spec=spec,
        out_shape=[
            pltpu.HBM((rows, width), BF),
            pltpu.HBM((rows, width), F32),
            struct((rows, width), BF),
            struct((half, width), F32),
            struct((half, width), F32),
            struct((8, width), F32),
        ],
        compiler_params=pltpu.CompilerParams(vmem_limit_bytes=40 << 20),
        name="ffn_and_norms",
    )(
        core, ctx, qry, tok, og, att, w_out, b_out[None], g1[None], b1[None], w_h, b_h[None], w_b, b_b[None],
        g2[None], b2[None],
    )


def attended_grad_kernel(att, dbr, w_out, datt_o, delta_o):
    da = mm_t(dbr[...], w_out[...]).astype(BF)
    datt_o[...] = da
    prod = att[...].astype(F32) * da.astype(F32)
    heads = [jnp.sum(prod[:, h * HD : (h + 1) * HD], axis=1, keepdims=True) for h in range(HEADS)]
    rest = jnp.zeros((prod.shape[0], HD - HEADS), F32)
    delta_o[...] = jnp.concatenate(heads + [rest], axis=1).T[:8]


def attended_grad(att, dbr, w_out):
    rows, width = att.shape
    row = pl.BlockSpec((2 * ROWS, width), lambda i: (i, 0))
    return pl.pallas_call(
        attended_grad_kernel,
        grid=(rows // (2 * ROWS),),
        in_specs=[row, row, full((width, width))],
        out_specs=[row, pl.BlockSpec((8, 2 * ROWS), lambda i: (0, i))],
        out_shape=[pltpu.HBM((rows, width), BF), pltpu.HBM((8, rows), F32)],
        compiler_params=pltpu.CompilerParams(vmem_limit_bytes=20 << 20),
        cost_estimate=LIGHT,
        name="attended_gradient",
    )(att, dbr, w_out)


def backward_kernel(
    rows, heads, ctx, qry, tok, q, k, kt, v, do, lse, delta, dq_o, dk_o, dv_o, dqt, dka, dva
):
    width = heads * HD
    bounds = slot_bounds(ctx, qry)

    dka[...] = jnp.zeros(dka.shape, F32)
    dva[...] = jnp.zeros(dva.shape, F32)

    def block(i, carry):
        first = i * QB
        lo, hi = key_range(bounds, first, QB)
        key_lo, key_hi = row_bounds(bounds, first + lax.broadcasted_iota(jnp.int32, (1, QB), 1))
        rq = pl.ds(pl.multiple_of(first, QB), QB)
        dqt[...] = jnp.zeros(dqt.shape, F32)
        cols = [slice(h * HD, (h + 1) * HD) for h in range(heads)]

        def body(start, size):
            rk = pl.ds(pl.multiple_of(start, UNIT), size)
            key_pos = start + lax.broadcasted_iota(jnp.int32, (size, QB), 0)
            allowed = (key_pos >= key_lo) & (key_pos < key_hi)
            scores = [mm_t(k[rk, c], q[rq, c]) for c in cols]
            dprobs = [mm_t(v[rk, c], do[rq, c]) for c in cols]
            probs = []
            dscores = []
            for h in range(heads):
                p = jnp.where(allowed, jnp.exp2(scores[h] * SCALE2 - lse[h : h + 1, rq]), 0.0)
                probs.append(p.astype(BF))
                dscores.append((p * (dprobs[h] - delta[h : h + 1, rq])).astype(BF))
            for h, c in enumerate(cols):
                dva[rk, c] += mm(probs[h], do[rq, c])
                dka[rk, c] += mm(dscores[h], q[rq, c])
                dqt[c, :] += mm(kt[c, rk], dscores[h])

        over_keys(lo, hi, KB_BACK, body)
        dq_o[rq, :] = (dqt[...] * SCALE).T.astype(BF)
        return carry

    lax.fori_loop(0, rows // QB, block, 0)
    padding = lax.broadcasted_iota(jnp.int32, (rows, 1), 0) >= bounds[-1][2]
    dk_o[...] = (dka[...] * SCALE).astype(BF)
    dv_o[...] = (dva[...] + jnp.where(padding, do[...].astype(F32), 0.0)).astype(BF)


def backward(ctx, qry, tok, q, k, kt, v, do, lse, delta):
    rows, width = tok.shape
    struct = jax.ShapeDtypeStruct
    whole = full((rows, width))
    spec = pltpu.PrefetchScalarGridSpec(
        num_scalar_prefetch=2,
        grid=(1,),
        in_specs=[whole, whole, whole, full((width, rows)), whole, whole, full((8, rows)), full((8, rows))],
        out_specs=[whole] * 3,
        scratch_shapes=[
            pltpu.VMEM((width, QB), F32),
            pltpu.VMEM((rows, width), F32),
            pltpu.VMEM((rows, width), F32),
        ],
    )
    return pl.pallas_call(
        functools.partial(backward_kernel, rows, HEADS),
        grid_spec=spec,
        out_shape=[struct((rows, width), BF)] * 3,
        compiler_params=pltpu.CompilerParams(vmem_limit_bytes=34 << 20),
        cost_estimate=pl.CostEstimate(flops=30 * 10**9, bytes_accessed=20 << 20, transcendentals=8 << 20),
        name="attention_backward",
    )(ctx, qry, tok, q, k, kt, v, do, lse, delta)


def input_grad_kernel(ds, dq, dk, dv, wq, wk, wv, o):
    total = ds[...] + mm_t(dq[...], wq[...]) + mm_t(dk[...], wk[...]) + mm_t(dv[...], wv[...])
    o[...] = total.astype(BF)


def input_gradient(ds, dq, dk, dv, wq, wk, wv):
    rows, width = ds.shape
    row = pl.BlockSpec((ROWS, width), lambda i: (i, 0))
    square = pl.BlockSpec((width, width), lambda i: (0, 0))
    return pl.pallas_call(
        input_grad_kernel,
        grid=(rows // ROWS,),
        in_specs=[row] * 4 + [square] * 3,
        out_specs=row,
        out_shape=jax.ShapeDtypeStruct((rows, width), BF),
        compiler_params=pltpu.CompilerParams(vmem_limit_bytes=48 << 20),
        cost_estimate=LIGHT,
        name="input_gradient",
    )(ds, dq, dk, dv, wq, wk, wv)


def projection_kernel(core, tok, dq, dk, dv, vec, keep_o, small, *rest):
    sends, acc = rest[:-1], rest[-1]
    i = pl.program_id(0)

    @pl.when(i == 0)
    def _():
        acc[...] = jnp.zeros(acc.shape, F32)
        small[0:8, :] = vec[...]
        small[8:, :] = jnp.zeros((small.shape[0] - 8, small.shape[1]), F32)

    t = tok[...]
    width = t.shape[1]
    for n, g in enumerate((dq, dk, dv)):
        value = t_mm(t, g[...])
        for r in range(0, width, PIECE):
            half, at = divmod(n * width + r, acc.shape[1])
            acc[half, at : at + PIECE, :] += value[r : r + PIECE]
    small[8:9, :] += jnp.sum(dq[...].astype(F32), axis=0, keepdims=True)
    small[9:10, :] += jnp.sum(dv[...].astype(F32), axis=0, keepdims=True)

    @pl.when(i == pl.num_programs(0) - 1)
    def _():
        keep_o[...] = acc[core[0]]
        for n, send in enumerate(sends):
            send[...] = acc[1 - core[0], n * SEND : (n + 1) * SEND, :]


def projection_gradients(core, tok, dq, dk, dv, vec):
    rows, width = tok.shape
    half = 3 * width // 2
    struct = jax.ShapeDtypeStruct
    row = pl.BlockSpec((2 * ROWS, width), lambda i, *_: (i, 0))
    spec = pltpu.PrefetchScalarGridSpec(
        num_scalar_prefetch=1,
        grid=(rows // (2 * ROWS),),
        in_specs=[row] * 4 + [full((8, width))],
        out_specs=[full((half, width)), full((SMALL, width))] + [full((SEND, width))] * (half // SEND),
        scratch_shapes=[pltpu.VMEM((2, half, width), F32)],
    )
    return pl.pallas_call(
        projection_kernel,
        grid_spec=spec,
        out_shape=[
            struct((half, width), F32),
            struct((SMALL, width), F32),
        ]
        + [struct((SEND, width), F32)] * (half // SEND),
        compiler_params=pltpu.CompilerParams(vmem_limit_bytes=32 << 20),
        cost_estimate=LIGHT,
        name="projection_gradients",
    )(core, tok, dq, dk, dv, vec)


def split_kernel(where, *refs):
    for n in range(4):
        refs[8 + n][...] = refs[n][0] + refs[4 + n][0]


def add_and_split(where, x, got):
    rows, cols = x.shape[0] // 4, x.shape[1]
    step = rows // 2 if rows % 16 == 0 else rows
    ins = [pl.BlockSpec((1, step, cols), lambda i, w, n=n: (w[n], i, 0)) for n in range(4)]
    spec = pltpu.PrefetchScalarGridSpec(
        num_scalar_prefetch=1,
        grid=(rows // step,),
        in_specs=ins + ins,
        out_specs=[pl.BlockSpec((step, cols), lambda i, w: (i, 0))] * 4,
    )
    return pl.pallas_call(
        split_kernel,
        grid_spec=spec,
        out_shape=[jax.ShapeDtypeStruct((rows, cols), F32)] * 4,
        compiler_params=pltpu.CompilerParams(vmem_limit_bytes=32 << 20),
        name="add_and_split",
    )(where, *[x.reshape(4, rows, cols)] * 4, *[got.reshape(4, rows, cols)] * 4)


def split_small_kernel(where, x, small, got_small, *rest):
    gots, outs, total = rest[:-5], rest[-5:-1], rest[-1]
    rows = x.shape[0] // 4
    for n, got in enumerate(gots):
        at = slice(n * SEND, (n + 1) * SEND)
        total[at, :] = x[at, :] + got[...]
    for n in range(4):
        outs[n][:rows, :] = total[pl.ds(pl.multiple_of(where[n] * rows, 8), rows), :]
        outs[n][rows:, :] = small[...] + got_small[...]


def add_and_split_small(where, x, small, got_small, *gots):
    rows, cols = x.shape[0] // 4, x.shape[1]
    whole = pl.BlockSpec(memory_space=pltpu.VMEM)
    return pl.pallas_call(
        split_small_kernel,
        in_specs=[pl.BlockSpec(memory_space=pltpu.SMEM)] + [whole] * (3 + len(gots)),
        out_specs=[whole] * 4,
        out_shape=[jax.ShapeDtypeStruct((rows + small.shape[0], cols), F32)] * 4,
        scratch_shapes=[pltpu.VMEM(x.shape, F32)],
        compiler_params=pltpu.CompilerParams(vmem_limit_bytes=16 << 20),
        name="add_and_split_small",
    )(where, x, small, got_small, *gots)


def unpack_kernel(places, piece, first, count, results, order, *refs):
    sources, outs = refs[:count], refs[count + results : -3]
    held, in_sem, out_sem = refs[-3:]

    def loads(n):
        return pltpu.make_async_copy(sources[n], held.at[n], in_sem.at[n])

    def copies(n, p):
        made = []
        for start, count, out, row, col in places:
            if start // piece == p:
                to = outs[out].at[pl.ds(row, count), pl.ds(col, held.shape[2])]
                from_ = held.at[n, pl.ds(start % piece, count)]
                made.append(pltpu.make_async_copy(from_, to, out_sem.at[n, len(made)]))
        return made

    for n in range(count):
        loads(n).start()
    for action in ("start", "wait"):
        for n in range(count):
            if action == "start":
                loads(n).wait()
            for p in range(4):

                @pl.when(order[first + n] == p)
                def _(n=n, p=p):
                    for c in copies(n, p):
                        c.start() if action == "start" else c.wait()


def unpack(places, shapes, order, sources, first=0, results=()):
    anywhere = pl.BlockSpec(memory_space=pl.ANY)
    count = len(sources)
    piece = sources[0].shape[0]
    places = cut(places, piece)
    most = max(sum(p[0] // piece == n for p in places) for n in range(4))
    return pl.pallas_call(
        functools.partial(unpack_kernel, places, piece, first, count, len(results)),
        in_specs=[pl.BlockSpec(memory_space=pltpu.SMEM)] + [anywhere] * (count + len(results)),
        out_specs=[anywhere] * len(shapes),
        out_shape=[jax.ShapeDtypeStruct(s, F32) for s in shapes],
        scratch_shapes=[
            pltpu.VMEM((count,) + sources[0].shape, F32),
            pltpu.SemaphoreType.DMA((count,)),
            pltpu.SemaphoreType.DMA((count, most)),
        ],
        input_output_aliases={1 + count + n: n for n in range(len(results))},
        compiler_params=pltpu.CompilerParams(vmem_limit_bytes=24 << 20),
        name="unpack",
    )(order, *sources, *results)


def swap_pairs(sizes, mask):
    dp, dq = sizes
    return [(p * dq + q, p * dq + (q ^ mask[p % 2])) for p in range(dp) for q in range(dq)]


class Ring:
    def __init__(self, sizes):
        dp, dq = sizes
        self.sizes = sizes
        self.core = lax.axis_index("dp") & 1
        me = lax.axis_index("dq")
        first, second = me & 1, (me >> 1) & 1
        self.low = jnp.where(self.core == 0, first, second)
        self.high = jnp.where(self.core == 0, second, first)
        place = 2 * self.high + self.low
        turned = [place ^ jnp.where(self.core == 0, a, b) for a, b in ((0, 0), (1, 2), (2, 1), (3, 3))]
        self.where = jnp.stack(turned).astype(jnp.int32)
        mine, other = 2 * self.core, 2 - 2 * self.core
        high = jnp.where(self.core == 0, first, second)
        self.order = jnp.stack(
            [mine + self.high, mine + 1 - self.high, other + high, other + 1 - high]
        ).astype(jnp.int32)
        bits = list(range(2, dq.bit_length() - 1))
        swapped = bits[1::-1] + bits[2:]
        self.far = [swap_pairs(sizes, (1 << a, 1 << b)) for a, b in zip(bits, swapped)]
        self.outer = [[(p, p ^ (1 << b)) for p in range(dp)] for b in range(1, dp.bit_length() - 1)]

    def core_start(self, send):
        return lax.ppermute(send, "dp", [(p, p ^ 1) for p in range(self.sizes[0])])

    def plane_start(self, sends):
        return [
            lax.ppermute(s, ("dp", "dq"), swap_pairs(self.sizes, (m, m))) for m, s in zip((1, 2, 3), sends)
        ]

    def plane_end(self, own, got):
        return (own + got[0]) + (got[1] + got[2])

    def far_start(self, x, n):
        return lax.ppermute(x, ("dp", "dq"), self.far[n])

    def rest(self, x):
        for pairs in self.far[2:]:
            x = x + lax.ppermute(x, ("dp", "dq"), pairs)
        for pairs in self.outer:
            x = x + lax.ppermute(x, "dp", pairs)
        return x

    def back_start(self, x, n):
        return lax.ppermute(x, ("dp", "dq"), swap_pairs(self.sizes, ((1, 2), (2, 1))[n]))

    def back_end(self, x, got, n):
        bit = (self.low, self.high)[n]
        return jnp.where(bit == 0, jnp.concatenate([x, got]), jnp.concatenate([got, x]))


def in_hbm(x):
    return pltpu.with_memory_space_constraint(x, pltpu.HBM)


def tie(*groups):
    return lax.optimization_barrier(groups)


def local(
    sizes, tokens, out_grad, context_len, query_count, w_query, w_key, w_value, b_query, b_value, w_out, b_out,
    norm1_gain, norm1_bias, w_hidden, b_hidden, w_back, b_back, norm2_gain, norm2_bias,
):
    width = tokens.shape[1]
    ff = w_hidden.shape[1]
    ring = Ring(sizes)
    tokens, out_grad, w_query, w_key, w_value, w_out, w_hidden, w_back = [
        pltpu.with_memory_space_constraint(x, pltpu.HBM)
        for x in (tokens, out_grad, w_query, w_key, w_value, w_out, w_hidden, w_back)
    ]
    core = ring.core.reshape(1).astype(jnp.int32)
    q, k, v, kt, att, lse = forward(
        context_len, query_count, tokens, w_query, w_key, w_value, b_query, b_value
    )
    output, ds, dbr, keep, send, vec = middle(
        core, context_len, query_count, tokens, out_grad, in_hbm(att), w_out, b_out, norm1_gain, norm1_bias,
        w_hidden, b_hidden, w_back, b_back, norm2_gain, norm2_bias,
    )
    got = ring.core_start(send)
    send, att, dbr = tie(send, att, dbr)
    datt, delta = attended_grad(att, dbr, w_out)
    got, datt, delta = tie(got, datt, delta)
    one, *sends = add_and_split(ring.where, keep, got)
    got_one = ring.plane_start(sends)
    one, ins = tie(one, (context_len, query_count, tokens, q, k, kt, v, datt, lse, delta))
    dq, dk, dv = backward(*ins)
    one, got_one, dq, dk, dv = tie(one, got_one, dq, dk, dv)
    one = ring.plane_end(one, got_one)
    got_one = ring.far_start(one, 0)
    one, dq, dk, dv = tie(one, dq, dk, dv)
    keep, small, *sends = projection_gradients(core, tokens, dq, dk, dv, vec)
    got = [ring.core_start(s) for s in [small] + sends]
    one = one + got_one
    middle_row = one.shape[0] // 2
    got_one = [ring.far_start(x, 1) for x in (one[:middle_row], one[middle_row:])]
    two, *sends = add_and_split_small(ring.where, keep, small, *got)
    got_two = ring.plane_start(sends)
    one, two, sends, dq, dk, dv, ds = tie(one, two, sends, dq, dk, dv, ds)
    input_grad = input_gradient(ds, dq, dk, dv, w_query, w_key, w_value)
    one, got_one, two, got_two, input_grad = tie(one, got_one, two, got_two, input_grad)
    one = ring.rest(one + jnp.concatenate(got_one))
    got_one = ring.back_start(one, 0)
    two = ring.plane_end(two, got_two)
    got_two = ring.far_start(two, 0)
    one, got_one, two, got_two = tie(one, got_one, two, got_two)
    one = ring.back_end(one, got_one, 0)
    got_one = ring.back_start(one, 1)
    home_one = ring.core_start(one)
    two = two + got_two
    got_two = ring.far_start(two, 1)
    one, two, got_two = tie(one, two, got_two)
    two = ring.rest(two + got_two)
    small = two[-SMALL:]
    two = two[:-SMALL]
    vectors = [small[n] for n in (8, 9, 0, 1, 2)] + [small[3:5].reshape(-1)] + [small[n] for n in (5, 6, 7)]
    got_two = ring.back_start(two, 0)
    one, got_one, home_one, two, got_two = tie(one, got_one, home_one, two, got_two)
    two = ring.back_end(two, got_two, 0)
    got_two = ring.back_start(two, 1)
    home_two = ring.core_start(two)
    last_one = ring.core_start(got_one)
    places = [(0, ff, 0, 0, 0)]
    places += [(ff + n * width, width, 1, 0, n * width) for n in range(ff // width)]
    places += [(2 * ff, width, 2, 0, 0)]
    shapes = [(ff, width), (width, ff), (width, width)]
    gwb, gwh, gwo = unpack(places, shapes, ring.order, (one, got_one, home_one, last_one))
    two, got_two, home_two, gwb, gwh, gwo, vectors = tie(two, got_two, home_two, gwb, gwh, gwo, vectors)
    places = [(n * width, width, n, 0, 0) for n in range(3)]
    last_two = ring.core_start(got_two)
    shapes = [(width, width)] * 3
    squares = unpack(places, shapes, ring.order, (two, got_two, home_two))
    gq, gk, gv = unpack(places, shapes, ring.order, (last_two,), 3, squares)
    return (
        output,
        input_grad,
        gq,
        gk,
        gv,
        vectors[0],
        vectors[1],
        gwo,
        vectors[2],
        vectors[3],
        vectors[4],
        gwh,
        vectors[5],
        gwb,
        vectors[6],
        vectors[7],
        vectors[8],
    )


def cut(places, piece):
    out = []
    for start, rows, to, row, col in places:
        at = start
        while at < start + rows:
            end = min((at // piece + 1) * piece, start + rows)
            out.append((at, end - at, to, row + at - start, col))
            at = end
    return out


def solution(mesh):
    sizes = (mesh.shape["dp"], mesh.shape["dq"])
    return jax.shard_map(
        functools.partial(local, sizes),
        mesh=mesh,
        in_specs=(
            P(("dp", "dq"), None),
            P(("dp", "dq"), None),
            P(("dp", "dq"), None),
            P(("dp", "dq"), None),
            P(),
            P(),
            P(),
            P(),
            P(),
            P(),
            P(),
            P(),
            P(),
            P(),
            P(),
            P(),
            P(),
            P(),
            P(),
        ),
        out_specs=(
            P(("dp", "dq"), None),
            P(("dp", "dq"), None),
            P(),
            P(),
            P(),
            P(),
            P(),
            P(),
            P(),
            P(),
            P(),
            P(),
            P(),
            P(),
            P(),
            P(),
            P(),
        ),
        check_vma=False,
    )
```

```python
import functools
import math

import jax
import jax.experimental.pallas as pl
import jax.experimental.pallas.tpu as pltpu
import jax.numpy as jnp
from jax import lax
from jax.sharding import PartitionSpec as P

HEADS = 4
HD = 128
SLOTS = 8
EPS = 1e-5
SCALE = 1.0 / math.sqrt(HD)
SCALE2 = SCALE * math.log2(math.e)
NEG = -1e30
F32 = jnp.float32
BF = jnp.bfloat16
ROWS = 512
QF = 512
QB = 256
KB = 1024
KB_BACK = 1024
UNIT = 128
PROJ = 1024
ATT = 2
PIECE = 256
LIGHT = pl.CostEstimate(flops=1, bytes_accessed=1, transcendentals=0)
SMALL = 16
SEND = 128


def mm(a, b):
    return jnp.dot(a, b, preferred_element_type=F32)


def mm_t(a, b):
    return lax.dot_general(a, b, (((1,), (1,)), ((), ())), preferred_element_type=F32)


def t_mm(a, b):
    return lax.dot_general(a, b, (((0,), (0,)), ((), ())), preferred_element_type=F32)


def slot_bounds(ctx, qry):
    out = []
    start = jnp.int32(0)
    for t in range(SLOTS):
        c = ctx[0, t]
        end = start + c + qry[0, t]
        out.append((start, start + c, end))
        start = end
    return out


def key_range(bounds, first, rows):
    lo = jnp.int32(1 << 30)
    hi = jnp.int32(0)
    for start, ctx_end, end in bounds:
        hit = (start < first + rows) & (end > first) & (end > start)
        lo = jnp.where(hit, jnp.minimum(lo, start), lo)
        hi = jnp.where(hit, jnp.maximum(hi, ctx_end), hi)
    return lo, hi


def row_bounds(bounds, pos):
    lo = jnp.zeros(pos.shape, jnp.int32)
    hi = jnp.zeros(pos.shape, jnp.int32)
    for start, ctx_end, end in bounds:
        inside = (pos >= start) & (pos < end)
        lo = jnp.where(inside, start, lo)
        hi = jnp.where(inside, ctx_end, hi)
    return lo, hi


def over_keys(lo, hi, most, body):
    start = lo // UNIT * UNIT
    units = jnp.maximum((hi - start + UNIT - 1) // UNIT, 0)
    whole = units // (most // UNIT)

    def step(j, carry):
        body(start + j * most, most)
        return carry

    lax.fori_loop(0, whole, step, 0)
    done = whole * (most // UNIT)
    size = most // 2
    while size >= UNIT:
        take = (units - done) // (size // UNIT)
        pl.when(take > 0)(functools.partial(body, start + done * UNIT, size))
        done = done + take * (size // UNIT)
        size //= 2


def full(shape):
    return pl.BlockSpec(shape, lambda i, *_: (0,) * len(shape), pipeline_mode=pl.Buffered(1))


def forward_kernel(
    rows, ctx, qry, tok, wq, wk, wv, bq, bv, q_o, k_o, v_o, kt_o, att_o, lse_o, qs, ks, vt, mx, sm, acc, sc
):
    i = pl.program_id(0)
    proj_steps = rows // PROJ

    @pl.when(i < proj_steps)
    def _():
        t = tok[...]
        r = pl.ds(pl.multiple_of(i * PROJ, PROJ), PROJ)
        q = (mm(t, wq[...]) + bq[...]).astype(BF)
        qs[r, :] = q
        q_o[...] = q
        k = mm(t, wk[...]).astype(BF)
        ks[r, :] = k
        k_o[...] = k
        kt_o[...] = k.T
        v = (mm(t, wv[...]) + bv[...]).astype(BF)
        v_o[...] = v
        vt[:, r] = v.T

    def attend(n, carry):
        first = (i - proj_steps) * (ATT * QF) + n * QF
        bounds = slot_bounds(ctx, qry)
        lo, hi = key_range(bounds, first, QF)
        key_lo, key_hi = row_bounds(bounds, first + lax.broadcasted_iota(jnp.int32, (1, QF), 1))
        rq = pl.ds(pl.multiple_of(first, QF), QF)
        mx[...] = jnp.full(mx.shape, NEG, F32)
        sm[...] = jnp.zeros(sm.shape, F32)
        acc[...] = jnp.zeros(acc.shape, F32)
        cols = [slice(h * HD, (h + 1) * HD) for h in range(HEADS)]
        parts = [slice(h * 8, (h + 1) * 8) for h in range(HEADS)]

        def score_pass(start, size):
            rk = pl.ds(pl.multiple_of(start, UNIT), size)
            key_pos = start + lax.broadcasted_iota(jnp.int32, (size, QF), 0)
            allowed = (key_pos >= key_lo) & (key_pos < key_hi)
            raw = [mm_t(ks[rk, c], qs[rq, c]) for c in cols]
            for h, part in enumerate(parts):
                s = jnp.where(allowed, raw[h], NEG)
                sc[h, rk, :] = s
                mx[part, :] = jnp.maximum(mx[part, :], jnp.max(s.reshape(size // 8, 8, QF), axis=0))

        over_keys(lo, hi, KB, score_pass)
        peak = [jnp.max(mx[part, :], axis=0, keepdims=True) * SCALE2 for part in parts]

        def value_pass(start, size):
            rk = pl.ds(pl.multiple_of(start, UNIT), size)
            probs = []
            for h, part in enumerate(parts):
                p = jnp.exp2(sc[h, rk, :] * SCALE2 - peak[h])
                sm[part, :] = sm[part, :] + jnp.sum(p.reshape(size // 8, 8, QF), axis=0)
                probs.append(p.astype(BF))
            for h, c in enumerate(cols):
                acc[c, :] = acc[c, :] + mm(vt[c, rk], probs[h])

        over_keys(lo, hi, KB, value_pass)
        here = pl.ds(pl.multiple_of(n * QF, QF), QF)
        padding = key_hi == 0
        own_values = vt[:, rq]
        for h, (c, part) in enumerate(zip(cols, parts)):
            total = jnp.sum(sm[part, :], axis=0, keepdims=True)
            o = jnp.where(padding, own_values[c, :].astype(F32), acc[c, :] * (1.0 / total))
            att_o[here, c] = o.T.astype(BF)
            lse_o[h : h + 1, here] = peak[h] + jnp.log2(total)
        return carry

    @pl.when(i >= proj_steps)
    def _():
        lax.fori_loop(0, ATT, attend, 0)


def forward(ctx, qry, tok, wq, wk, wv, bq, bv):
    rows, width = tok.shape
    ps, qn = rows // PROJ, rows // (ATT * QF)
    struct = jax.ShapeDtypeStruct
    proj = pl.BlockSpec((PROJ, width), lambda i, *_: (jnp.minimum(i, ps - 1), 0))
    proj_t = pl.BlockSpec((width, PROJ), lambda i, *_: (0, jnp.minimum(i, ps - 1)))
    att = pl.BlockSpec((ATT * QF, width), lambda i, *_: (jnp.maximum(i - ps, 0), 0))
    att_t = pl.BlockSpec((8, ATT * QF), lambda i, *_: (0, jnp.maximum(i - ps, 0)))
    spec = pltpu.PrefetchScalarGridSpec(
        num_scalar_prefetch=2,
        grid=(ps + qn,),
        in_specs=[proj] + [full((width, width))] * 3 + [full((1, width))] * 2,
        out_specs=[proj] * 3 + [proj_t, att, att_t],
        scratch_shapes=[
            pltpu.VMEM((rows, width), BF),
            pltpu.VMEM((rows, width), BF),
            pltpu.VMEM((width, rows), BF),
            pltpu.VMEM((8 * HEADS, QF), F32),
            pltpu.VMEM((8 * HEADS, QF), F32),
            pltpu.VMEM((width, QF), F32),
            pltpu.VMEM((HEADS, rows, QF), F32),
        ],
    )
    return pl.pallas_call(
        functools.partial(forward_kernel, rows),
        grid_spec=spec,
        out_shape=[pltpu.HBM((rows, width), BF)] * 3
        + [pltpu.HBM((width, rows), BF), pltpu.HBM((rows, width), BF), pltpu.HBM((8, rows), F32)],
        compiler_params=pltpu.CompilerParams(vmem_limit_bytes=58 << 20),
        name="attention_forward",
    )(ctx, qry, tok, wq, wk, wv, bq[None], bv[None])


def middle_kernel(
    core, ctx, qry, tok, og, att, w_out, b_out, g1, b1, w_h, b_h, w_b, b_b, g2, b2,
    out_o, dsum_o, dbr_o, keep_o, send_o, vec, pack,
):
    i = pl.program_id(0)
    total = slot_bounds(ctx, qry)[-1][2]
    width = tok.shape[1]
    ff = w_h.shape[1]
    count = 2
    sub = ROWS // count
    rows = [slice(n * sub, (n + 1) * sub) for n in range(count)]

    @pl.when(i == 0)
    def _():
        pack[...] = jnp.zeros(pack.shape, F32)
        vec[...] = jnp.zeros(vec.shape, F32)

    def add(row, value):
        for r in range(0, value.shape[0], PIECE):
            half, at = divmod(row + r, pack.shape[1])
            pack[half, at : at + PIECE, :] += value[r : r + PIECE]

    def mean(x):
        return jnp.mean(x, axis=1, keepdims=True)

    def each(f, *lists):
        return [f(*xs) for xs in zip(*lists)]

    def split(pairs):
        return [list(xs) for xs in zip(*pairs)]

    def cols(lists):
        return sum(jnp.sum(x.astype(F32), axis=0, keepdims=True) for x in lists)

    def first_norm(r, branch):
        x1 = tok[r, :].astype(F32) + (branch + b_out[...])
        xc1 = x1 - mean(x1)
        r1 = lax.rsqrt(mean(xc1 * xc1) + EPS)
        xh1 = xc1 * r1
        n1 = xh1 * g1[...] + b1[...]
        return r1, xh1, n1, n1.astype(BF)

    def gelu(hp):
        hp = hp + b_h[...]
        cdf = 0.5 * (1.0 + lax.erf(hp * (1.0 / math.sqrt(2.0))))
        slope = cdf + hp * (jnp.exp(-0.5 * hp * hp) * (1.0 / math.sqrt(2.0 * math.pi)))
        return (hp * cdf).astype(BF), slope

    def second_norm(r, n1, ffn):
        row = i * ROWS + r.start + lax.broadcasted_iota(jnp.int32, (sub, 1), 0)
        valid = (row < total).astype(F32)
        x2 = n1 + (ffn + b_b[...])
        xc2 = x2 - mean(x2)
        r2 = lax.rsqrt(mean(xc2 * xc2) + EPS)
        xh2 = xc2 * r2
        out_o[r, :] = ((xh2 * g2[...] + b2[...]) * valid).astype(BF)
        dy = og[r, :].astype(F32) * valid
        dx = dy * g2[...]
        d2 = r2 * (dx - mean(dx) - xh2 * mean(dx * xh2))
        dg2 = jnp.sum(dy * xh2, axis=0, keepdims=True)
        return d2, d2.astype(BF), dg2, jnp.sum(dy, axis=0, keepdims=True)

    def first_norm_back(r, r1, xh1, d2, dhn):
        dn = d2 + dhn
        dx1 = dn * g1[...]
        ds = r1 * (dx1 - mean(dx1) - xh1 * mean(dx1 * xh1))
        dsum_o[r, :] = ds
        dbr = ds.astype(BF)
        dbr_o[r, :] = dbr
        dg1 = jnp.sum(dn * xh1, axis=0, keepdims=True)
        return dbr, dg1, jnp.sum(dn, axis=0, keepdims=True)

    branch = [mm(att[r, :], w_out[...]) for r in rows]
    r1, xh1, n1, nl = split(each(first_norm, rows, branch))
    act, slope = split(each(gelu, [mm(x, w_h[...]) for x in nl]))
    ffn = [mm(x, w_b[...]) for x in act]
    d2, df, dg2, db2 = split(each(second_norm, rows, n1, ffn))
    dact = [mm_t(x, w_b[...]) for x in df]
    add(0, t_mm(jnp.concatenate(act), jnp.concatenate(df)))
    dh = each(lambda x, s: (x * s).astype(BF), dact, slope)
    dhn = [mm_t(x, w_h[...]) for x in dh]
    nl, dh_all = jnp.concatenate(nl), jnp.concatenate(dh)
    for n in range(ff // width):
        add(ff + n * width, t_mm(nl, dh_all[:, n * width : (n + 1) * width]))
    dbr, dg1, db1 = split(each(first_norm_back, rows, r1, xh1, d2, dhn))
    add(2 * ff, t_mm(att[...], jnp.concatenate(dbr)))
    dbo, dbh, dbb = cols(dbr), cols(dh), cols(df)
    dg1, db1, dg2, db2 = cols(dg1), cols(db1), cols(dg2), cols(db2)
    for n, v in enumerate((dbo, dg1, db1, dbh[:, :width], dbh[:, width:], dbb, dg2, db2)):
        vec[n : n + 1, :] += v

    @pl.when(i == pl.num_programs(0) - 1)
    def _():
        keep_o[...] = pack[core[0]]
        send_o[...] = pack[1 - core[0]]


def middle(core, ctx, qry, tok, og, att, w_out, b_out, g1, b1, w_h, b_h, w_b, b_b, g2, b2):
    rows, width = tok.shape
    ff = w_h.shape[1]
    half = ff + width // 2
    struct = jax.ShapeDtypeStruct
    row = pl.BlockSpec((ROWS, width), lambda i, *_: (i, 0))
    vec = full((1, width))
    spec = pltpu.PrefetchScalarGridSpec(
        num_scalar_prefetch=3,
        grid=(rows // ROWS,),
        in_specs=[row] * 3
        + [full((width, width)), vec, vec, vec, full((width, ff)), full((1, ff)), full((ff, width)), vec, vec, vec],
        out_specs=[row] * 3
        + [full((half, width)), full((half, width)), full((8, width))],
        scratch_shapes=[pltpu.VMEM((2, half, width), F32)],
    )
    return pl.pallas_call(
        middle_kernel,
        grid_spec=spec,
        out_shape=[
            pltpu.HBM((rows, width), BF),
            pltpu.HBM((rows, width), F32),
            struct((rows, width), BF),
            struct((half, width), F32),
            struct((half, width), F32),
            struct((8, width), F32),
        ],
        compiler_params=pltpu.CompilerParams(vmem_limit_bytes=40 << 20),
        name="ffn_and_norms",
    )(
        core, ctx, qry, tok, og, att, w_out, b_out[None], g1[None], b1[None], w_h, b_h[None], w_b, b_b[None],
        g2[None], b2[None],
    )


def attended_grad_kernel(att, dbr, w_out, datt_o, delta_o):
    da = mm_t(dbr[...], w_out[...]).astype(BF)
    datt_o[...] = da
    prod = att[...].astype(F32) * da.astype(F32)
    heads = [jnp.sum(prod[:, h * HD : (h + 1) * HD], axis=1, keepdims=True) for h in range(HEADS)]
    rest = jnp.zeros((prod.shape[0], HD - HEADS), F32)
    delta_o[...] = jnp.concatenate(heads + [rest], axis=1).T[:8]


def attended_grad(att, dbr, w_out):
    rows, width = att.shape
    row = pl.BlockSpec((2 * ROWS, width), lambda i: (i, 0))
    return pl.pallas_call(
        attended_grad_kernel,
        grid=(rows // (2 * ROWS),),
        in_specs=[row, row, full((width, width))],
        out_specs=[row, pl.BlockSpec((8, 2 * ROWS), lambda i: (0, i))],
        out_shape=[pltpu.HBM((rows, width), BF), pltpu.HBM((8, rows), F32)],
        compiler_params=pltpu.CompilerParams(vmem_limit_bytes=20 << 20),
        cost_estimate=LIGHT,
        name="attended_gradient",
    )(att, dbr, w_out)


def backward_kernel(
    rows, heads, ctx, qry, tok, q, k, kt, v, do, lse, delta, dq_o, dk_o, dv_o, dqt, dka, dva
):
    width = heads * HD
    bounds = slot_bounds(ctx, qry)

    dka[...] = jnp.zeros(dka.shape, F32)
    dva[...] = jnp.zeros(dva.shape, F32)

    def block(i, carry):
        first = i * QB
        lo, hi = key_range(bounds, first, QB)
        key_lo, key_hi = row_bounds(bounds, first + lax.broadcasted_iota(jnp.int32, (1, QB), 1))
        rq = pl.ds(pl.multiple_of(first, QB), QB)
        dqt[...] = jnp.zeros(dqt.shape, F32)
        cols = [slice(h * HD, (h + 1) * HD) for h in range(heads)]

        def body(start, size):
            rk = pl.ds(pl.multiple_of(start, UNIT), size)
            key_pos = start + lax.broadcasted_iota(jnp.int32, (size, QB), 0)
            allowed = (key_pos >= key_lo) & (key_pos < key_hi)
            scores = [mm_t(k[rk, c], q[rq, c]) for c in cols]
            dprobs = [mm_t(v[rk, c], do[rq, c]) for c in cols]
            probs = []
            dscores = []
            for h in range(heads):
                p = jnp.where(allowed, jnp.exp2(scores[h] * SCALE2 - lse[h : h + 1, rq]), 0.0)
                probs.append(p.astype(BF))
                dscores.append((p * (dprobs[h] - delta[h : h + 1, rq])).astype(BF))
            for h, c in enumerate(cols):
                dva[rk, c] += mm(probs[h], do[rq, c])
                dka[rk, c] += mm(dscores[h], q[rq, c])
                dqt[c, :] += mm(kt[c, rk], dscores[h])

        over_keys(lo, hi, KB_BACK, body)
        dq_o[rq, :] = (dqt[...] * SCALE).T.astype(BF)
        return carry

    lax.fori_loop(0, rows // QB, block, 0)
    padding = lax.broadcasted_iota(jnp.int32, (rows, 1), 0) >= bounds[-1][2]
    dk_o[...] = (dka[...] * SCALE).astype(BF)
    dv_o[...] = (dva[...] + jnp.where(padding, do[...].astype(F32), 0.0)).astype(BF)


def backward(ctx, qry, tok, q, k, kt, v, do, lse, delta):
    rows, width = tok.shape
    struct = jax.ShapeDtypeStruct
    whole = full((rows, width))
    spec = pltpu.PrefetchScalarGridSpec(
        num_scalar_prefetch=2,
        grid=(1,),
        in_specs=[whole, whole, whole, full((width, rows)), whole, whole, full((8, rows)), full((8, rows))],
        out_specs=[whole] * 3,
        scratch_shapes=[
            pltpu.VMEM((width, QB), F32),
            pltpu.VMEM((rows, width), F32),
            pltpu.VMEM((rows, width), F32),
        ],
    )
    return pl.pallas_call(
        functools.partial(backward_kernel, rows, HEADS),
        grid_spec=spec,
        out_shape=[struct((rows, width), BF)] * 3,
        compiler_params=pltpu.CompilerParams(vmem_limit_bytes=34 << 20),
        cost_estimate=pl.CostEstimate(flops=30 * 10**9, bytes_accessed=20 << 20, transcendentals=8 << 20),
        name="attention_backward",
    )(ctx, qry, tok, q, k, kt, v, do, lse, delta)


def input_grad_kernel(ds, dq, dk, dv, wq, wk, wv, o):
    total = ds[...] + mm_t(dq[...], wq[...]) + mm_t(dk[...], wk[...]) + mm_t(dv[...], wv[...])
    o[...] = total.astype(BF)


def input_gradient(ds, dq, dk, dv, wq, wk, wv):
    rows, width = ds.shape
    row = pl.BlockSpec((ROWS, width), lambda i: (i, 0))
    square = pl.BlockSpec((width, width), lambda i: (0, 0))
    return pl.pallas_call(
        input_grad_kernel,
        grid=(rows // ROWS,),
        in_specs=[row] * 4 + [square] * 3,
        out_specs=row,
        out_shape=jax.ShapeDtypeStruct((rows, width), BF),
        compiler_params=pltpu.CompilerParams(vmem_limit_bytes=16 << 20),
        cost_estimate=LIGHT,
        name="input_gradient",
    )(ds, dq, dk, dv, wq, wk, wv)


def projection_kernel(core, tok, dq, dk, dv, vec, keep_o, small, *rest):
    sends, acc = rest[:-1], rest[-1]
    i = pl.program_id(0)

    @pl.when(i == 0)
    def _():
        acc[...] = jnp.zeros(acc.shape, F32)
        small[0:8, :] = vec[...]
        small[8:, :] = jnp.zeros((small.shape[0] - 8, small.shape[1]), F32)

    t = tok[...]
    width = t.shape[1]
    for n, g in enumerate((dq, dk, dv)):
        value = t_mm(t, g[...])
        for r in range(0, width, PIECE):
            half, at = divmod(n * width + r, acc.shape[1])
            acc[half, at : at + PIECE, :] += value[r : r + PIECE]
    small[8:9, :] += jnp.sum(dq[...].astype(F32), axis=0, keepdims=True)
    small[9:10, :] += jnp.sum(dv[...].astype(F32), axis=0, keepdims=True)

    @pl.when(i == pl.num_programs(0) - 1)
    def _():
        keep_o[...] = acc[core[0]]
        for n, send in enumerate(sends):
            send[...] = acc[1 - core[0], n * SEND : (n + 1) * SEND, :]


def projection_gradients(core, tok, dq, dk, dv, vec):
    rows, width = tok.shape
    half = 3 * width // 2
    struct = jax.ShapeDtypeStruct
    row = pl.BlockSpec((2 * ROWS, width), lambda i, *_: (i, 0))
    spec = pltpu.PrefetchScalarGridSpec(
        num_scalar_prefetch=1,
        grid=(rows // (2 * ROWS),),
        in_specs=[row] * 4 + [full((8, width))],
        out_specs=[full((half, width)), full((SMALL, width))] + [full((SEND, width))] * (half // SEND),
        scratch_shapes=[pltpu.VMEM((2, half, width), F32)],
    )
    return pl.pallas_call(
        projection_kernel,
        grid_spec=spec,
        out_shape=[
            struct((half, width), F32),
            struct((SMALL, width), F32),
        ]
        + [struct((SEND, width), F32)] * (half // SEND),
        compiler_params=pltpu.CompilerParams(vmem_limit_bytes=32 << 20),
        cost_estimate=LIGHT,
        name="projection_gradients",
    )(core, tok, dq, dk, dv, vec)


def split_kernel(where, *refs):
    for n in range(4):
        refs[8 + n][...] = refs[n][0] + refs[4 + n][0]


def add_and_split(where, x, got):
    rows, cols = x.shape[0] // 4, x.shape[1]
    step = rows // 2 if rows % 16 == 0 else rows
    ins = [pl.BlockSpec((1, step, cols), lambda i, w, n=n: (w[n], i, 0)) for n in range(4)]
    spec = pltpu.PrefetchScalarGridSpec(
        num_scalar_prefetch=1,
        grid=(rows // step,),
        in_specs=ins + ins,
        out_specs=[pl.BlockSpec((step, cols), lambda i, w: (i, 0))] * 4,
    )
    return pl.pallas_call(
        split_kernel,
        grid_spec=spec,
        out_shape=[jax.ShapeDtypeStruct((rows, cols), F32)] * 4,
        compiler_params=pltpu.CompilerParams(vmem_limit_bytes=32 << 20),
        name="add_and_split",
    )(where, *[x.reshape(4, rows, cols)] * 4, *[got.reshape(4, rows, cols)] * 4)


def split_small_kernel(where, x, small, got_small, *rest):
    gots, outs, total = rest[:-5], rest[-5:-1], rest[-1]
    rows = x.shape[0] // 4
    for n, got in enumerate(gots):
        at = slice(n * SEND, (n + 1) * SEND)
        total[at, :] = x[at, :] + got[...]
    for n in range(4):
        outs[n][:rows, :] = total[pl.ds(pl.multiple_of(where[n] * rows, 8), rows), :]
        outs[n][rows:, :] = small[...] + got_small[...]


def add_and_split_small(where, x, small, got_small, *gots):
    rows, cols = x.shape[0] // 4, x.shape[1]
    whole = pl.BlockSpec(memory_space=pltpu.VMEM)
    return pl.pallas_call(
        split_small_kernel,
        in_specs=[pl.BlockSpec(memory_space=pltpu.SMEM)] + [whole] * (3 + len(gots)),
        out_specs=[whole] * 4,
        out_shape=[jax.ShapeDtypeStruct((rows + small.shape[0], cols), F32)] * 4,
        scratch_shapes=[pltpu.VMEM(x.shape, F32)],
        compiler_params=pltpu.CompilerParams(vmem_limit_bytes=16 << 20),
        name="add_and_split_small",
    )(where, x, small, got_small, *gots)


def unpack_kernel(places, piece, first, count, results, order, *refs):
    sources, outs = refs[:count], refs[count + results : -3]
    held, in_sem, out_sem = refs[-3:]

    def loads(n):
        return pltpu.make_async_copy(sources[n], held.at[n], in_sem.at[n])

    def copies(n, p):
        made = []
        for start, count, out, row, col in places:
            if start // piece == p:
                to = outs[out].at[pl.ds(row, count), pl.ds(col, held.shape[2])]
                from_ = held.at[n, pl.ds(start % piece, count)]
                made.append(pltpu.make_async_copy(from_, to, out_sem.at[n, len(made)]))
        return made

    for n in range(count):
        loads(n).start()
    for action in ("start", "wait"):
        for n in range(count):
            if action == "start":
                loads(n).wait()
            for p in range(4):

                @pl.when(order[first + n] == p)
                def _(n=n, p=p):
                    for c in copies(n, p):
                        c.start() if action == "start" else c.wait()


def unpack(places, shapes, order, sources, first=0, results=()):
    anywhere = pl.BlockSpec(memory_space=pl.ANY)
    count = len(sources)
    piece = sources[0].shape[0]
    places = cut(places, piece)
    most = max(sum(p[0] // piece == n for p in places) for n in range(4))
    return pl.pallas_call(
        functools.partial(unpack_kernel, places, piece, first, count, len(results)),
        in_specs=[pl.BlockSpec(memory_space=pltpu.SMEM)] + [anywhere] * (count + len(results)),
        out_specs=[anywhere] * len(shapes),
        out_shape=[jax.ShapeDtypeStruct(s, F32) for s in shapes],
        scratch_shapes=[
            pltpu.VMEM((count,) + sources[0].shape, F32),
            pltpu.SemaphoreType.DMA((count,)),
            pltpu.SemaphoreType.DMA((count, most)),
        ],
        input_output_aliases={1 + count + n: n for n in range(len(results))},
        compiler_params=pltpu.CompilerParams(vmem_limit_bytes=24 << 20),
        name="unpack",
    )(order, *sources, *results)


def swap_pairs(sizes, mask):
    dp, dq = sizes
    return [(p * dq + q, p * dq + (q ^ mask[p % 2])) for p in range(dp) for q in range(dq)]


class Ring:
    def __init__(self, sizes):
        dp, dq = sizes
        self.sizes = sizes
        self.core = lax.axis_index("dp") & 1
        me = lax.axis_index("dq")
        first, second = me & 1, (me >> 1) & 1
        self.low = jnp.where(self.core == 0, first, second)
        self.high = jnp.where(self.core == 0, second, first)
        place = 2 * self.high + self.low
        turned = [place ^ jnp.where(self.core == 0, a, b) for a, b in ((0, 0), (1, 2), (2, 1), (3, 3))]
        self.where = jnp.stack(turned).astype(jnp.int32)
        mine, other = 2 * self.core, 2 - 2 * self.core
        high = jnp.where(self.core == 0, first, second)
        self.order = jnp.stack(
            [mine + self.high, mine + 1 - self.high, other + high, other + 1 - high]
        ).astype(jnp.int32)
        bits = list(range(2, dq.bit_length() - 1))
        swapped = bits[1::-1] + bits[2:]
        self.far = [swap_pairs(sizes, (1 << a, 1 << b)) for a, b in zip(bits, swapped)]
        self.outer = [[(p, p ^ (1 << b)) for p in range(dp)] for b in range(1, dp.bit_length() - 1)]

    def core_start(self, send):
        return lax.ppermute(send, "dp", [(p, p ^ 1) for p in range(self.sizes[0])])

    def plane_start(self, sends):
        return [
            lax.ppermute(s, ("dp", "dq"), swap_pairs(self.sizes, (m, m))) for m, s in zip((1, 2, 3), sends)
        ]

    def plane_end(self, own, got):
        return (own + got[0]) + (got[1] + got[2])

    def far_start(self, x, n):
        return lax.ppermute(x, ("dp", "dq"), self.far[n])

    def rest(self, x):
        for pairs in self.far[2:]:
            x = x + lax.ppermute(x, ("dp", "dq"), pairs)
        for pairs in self.outer:
            x = x + lax.ppermute(x, "dp", pairs)
        return x

    def back_start(self, x, n):
        return lax.ppermute(x, ("dp", "dq"), swap_pairs(self.sizes, ((1, 2), (2, 1))[n]))

    def back_end(self, x, got, n):
        bit = (self.low, self.high)[n]
        return jnp.where(bit == 0, jnp.concatenate([x, got]), jnp.concatenate([got, x]))


def in_hbm(x):
    return pltpu.with_memory_space_constraint(x, pltpu.HBM)


def tie(*groups):
    return lax.optimization_barrier(groups)


def local(
    sizes, tokens, out_grad, context_len, query_count, w_query, w_key, w_value, b_query, b_value, w_out, b_out,
    norm1_gain, norm1_bias, w_hidden, b_hidden, w_back, b_back, norm2_gain, norm2_bias,
):
    width = tokens.shape[1]
    ff = w_hidden.shape[1]
    ring = Ring(sizes)
    tokens, out_grad, w_query, w_key, w_value, w_out, w_hidden, w_back = [
        pltpu.with_memory_space_constraint(x, pltpu.HBM)
        for x in (tokens, out_grad, w_query, w_key, w_value, w_out, w_hidden, w_back)
    ]
    core = ring.core.reshape(1).astype(jnp.int32)
    q, k, v, kt, att, lse = forward(
        context_len, query_count, tokens, w_query, w_key, w_value, b_query, b_value
    )
    output, ds, dbr, keep, send, vec = middle(
        core, context_len, query_count, tokens, out_grad, in_hbm(att), w_out, b_out, norm1_gain, norm1_bias,
        w_hidden, b_hidden, w_back, b_back, norm2_gain, norm2_bias,
    )
    got = ring.core_start(send)
    send, att, dbr = tie(send, att, dbr)
    datt, delta = attended_grad(att, dbr, w_out)
    got, datt, delta = tie(got, datt, delta)
    one, *sends = add_and_split(ring.where, keep, got)
    got_one = ring.plane_start(sends)
    one, ins = tie(one, (context_len, query_count, tokens, q, k, kt, v, datt, lse, delta))
    dq, dk, dv = backward(*ins)
    one, got_one, dq, dk, dv = tie(one, got_one, dq, dk, dv)
    one = ring.plane_end(one, got_one)
    got_one = ring.far_start(one, 0)
    one, dq, dk, dv = tie(one, dq, dk, dv)
    keep, small, *sends = projection_gradients(core, tokens, dq, dk, dv, vec)
    got = [ring.core_start(s) for s in [small] + sends]
    one = one + got_one
    middle_row = one.shape[0] // 2
    got_one = [ring.far_start(x, 1) for x in (one[:middle_row], one[middle_row:])]
    two, *sends = add_and_split_small(ring.where, keep, small, *got)
    got_two = ring.plane_start(sends)
    one, two, sends, dq, dk, dv, ds = tie(one, two, sends, dq, dk, dv, ds)
    input_grad = input_gradient(in_hbm(ds), dq, dk, dv, w_query, w_key, w_value)
    one, got_one, two, got_two, input_grad = tie(one, got_one, two, got_two, input_grad)
    one = ring.rest(one + jnp.concatenate(got_one))
    got_one = ring.back_start(one, 0)
    two = ring.plane_end(two, got_two)
    got_two = ring.far_start(two, 0)
    one, got_one, two, got_two = tie(one, got_one, two, got_two)
    one = ring.back_end(one, got_one, 0)
    got_one = ring.back_start(one, 1)
    home_one = ring.core_start(one)
    two = two + got_two
    got_two = ring.far_start(two, 1)
    one, two, got_two = tie(one, two, got_two)
    two = ring.rest(two + got_two)
    small = two[-SMALL:]
    two = two[:-SMALL]
    vectors = [small[n] for n in (8, 9, 0, 1, 2)] + [small[3:5].reshape(-1)] + [small[n] for n in (5, 6, 7)]
    got_two = ring.back_start(two, 0)
    one, got_one, home_one, two, got_two = tie(one, got_one, home_one, two, got_two)
    two = ring.back_end(two, got_two, 0)
    got_two = ring.back_start(two, 1)
    home_two = ring.core_start(two)
    last_one = ring.core_start(got_one)
    places = [(0, ff, 0, 0, 0)]
    places += [(ff + n * width, width, 1, 0, n * width) for n in range(ff // width)]
    places += [(2 * ff, width, 2, 0, 0)]
    shapes = [(ff, width), (width, ff), (width, width)]
    gwb, gwh, gwo = unpack(
        places, shapes, ring.order, [in_hbm(x) for x in (one, got_one, home_one, last_one)]
    )
    two, got_two, home_two, gwb, gwh, gwo, vectors = tie(two, got_two, home_two, gwb, gwh, gwo, vectors)
    places = [(n * width, width, n, 0, 0) for n in range(3)]
    last_two = ring.core_start(got_two)
    shapes = [(width, width)] * 3
    squares = unpack(places, shapes, ring.order, (two, got_two, home_two))
    gq, gk, gv = unpack(places, shapes, ring.order, (last_two,), 3, squares)
    return (
        output,
        input_grad,
        gq,
        gk,
        gv,
        vectors[0],
        vectors[1],
        gwo,
        vectors[2],
        vectors[3],
        vectors[4],
        gwh,
        vectors[5],
        gwb,
        vectors[6],
        vectors[7],
        vectors[8],
    )


def cut(places, piece):
    out = []
    for start, rows, to, row, col in places:
        at = start
        while at < start + rows:
            end = min((at // piece + 1) * piece, start + rows)
            out.append((at, end - at, to, row + at - start, col))
            at = end
    return out


def solution(mesh):
    sizes = (mesh.shape["dp"], mesh.shape["dq"])
    return jax.shard_map(
        functools.partial(local, sizes),
        mesh=mesh,
        in_specs=(
            P(("dp", "dq"), None),
            P(("dp", "dq"), None),
            P(("dp", "dq"), None),
            P(("dp", "dq"), None),
            P(),
            P(),
            P(),
            P(),
            P(),
            P(),
            P(),
            P(),
            P(),
            P(),
            P(),
            P(),
            P(),
            P(),
            P(),
        ),
        out_specs=(
            P(("dp", "dq"), None),
            P(("dp", "dq"), None),
            P(),
            P(),
            P(),
            P(),
            P(),
            P(),
            P(),
            P(),
            P(),
            P(),
            P(),
            P(),
            P(),
            P(),
            P(),
        ),
        check_vma=False,
    )
```

```python
import functools
import math

import jax
import jax.experimental.pallas as pl
import jax.experimental.pallas.tpu as pltpu
import jax.numpy as jnp
from jax import lax
from jax.sharding import PartitionSpec as P

HEADS = 4
HD = 128
SLOTS = 8
EPS = 1e-5
SCALE = 1.0 / math.sqrt(HD)
SCALE2 = SCALE * math.log2(math.e)
NEG = -1e30
F32 = jnp.float32
BF = jnp.bfloat16
ROWS = 512
QF = 512
QB = 256
KB = 1024
KB_BACK = 1024
UNIT = 128
PROJ = 1024
ATT = 2
PIECE = 256
LIGHT = pl.CostEstimate(flops=1, bytes_accessed=1, transcendentals=0)
SMALL = 16
SEND = 128


def mm(a, b):
    return jnp.dot(a, b, preferred_element_type=F32)


def mm_t(a, b):
    return lax.dot_general(a, b, (((1,), (1,)), ((), ())), preferred_element_type=F32)


def t_mm(a, b):
    return lax.dot_general(a, b, (((0,), (0,)), ((), ())), preferred_element_type=F32)


def slot_bounds(ctx, qry):
    out = []
    start = jnp.int32(0)
    for t in range(SLOTS):
        c = ctx[0, t]
        end = start + c + qry[0, t]
        out.append((start, start + c, end))
        start = end
    return out


def key_range(bounds, first, rows):
    lo = jnp.int32(1 << 30)
    hi = jnp.int32(0)
    for start, ctx_end, end in bounds:
        hit = (start < first + rows) & (end > first) & (end > start)
        lo = jnp.where(hit, jnp.minimum(lo, start), lo)
        hi = jnp.where(hit, jnp.maximum(hi, ctx_end), hi)
    return lo, hi


def row_bounds(bounds, pos):
    lo = jnp.zeros(pos.shape, jnp.int32)
    hi = jnp.zeros(pos.shape, jnp.int32)
    for start, ctx_end, end in bounds:
        inside = (pos >= start) & (pos < end)
        lo = jnp.where(inside, start, lo)
        hi = jnp.where(inside, ctx_end, hi)
    return lo, hi


def over_keys(lo, hi, most, body):
    start = lo // UNIT * UNIT
    units = jnp.maximum((hi - start + UNIT - 1) // UNIT, 0)
    whole = units // (most // UNIT)

    def step(j, carry):
        body(start + j * most, most)
        return carry

    lax.fori_loop(0, whole, step, 0)
    done = whole * (most // UNIT)
    size = most // 2
    while size >= UNIT:
        take = (units - done) // (size // UNIT)
        pl.when(take > 0)(functools.partial(body, start + done * UNIT, size))
        done = done + take * (size // UNIT)
        size //= 2


def full(shape):
    return pl.BlockSpec(shape, lambda i, *_: (0,) * len(shape), pipeline_mode=pl.Buffered(1))


def forward_kernel(
    rows, ctx, qry, tok, wq, wk, wv, bq, bv, q_o, k_o, v_o, kt_o, att_o, lse_o, qs, ks, vt, mx, sm, acc, sc
):
    i = pl.program_id(0)
    proj_steps = rows // PROJ

    @pl.when(i < proj_steps)
    def _():
        t = tok[...]
        r = pl.ds(pl.multiple_of(i * PROJ, PROJ), PROJ)
        q = (mm(t, wq[...]) + bq[...]).astype(BF)
        qs[r, :] = q
        q_o[...] = q
        k = mm(t, wk[...]).astype(BF)
        ks[r, :] = k
        k_o[...] = k
        kt_o[...] = k.T
        v = (mm(t, wv[...]) + bv[...]).astype(BF)
        v_o[...] = v
        vt[:, r] = v.T

    def attend(n, carry):
        first = (i - proj_steps) * (ATT * QF) + n * QF
        bounds = slot_bounds(ctx, qry)
        lo, hi = key_range(bounds, first, QF)
        key_lo, key_hi = row_bounds(bounds, first + lax.broadcasted_iota(jnp.int32, (1, QF), 1))
        rq = pl.ds(pl.multiple_of(first, QF), QF)
        mx[...] = jnp.full(mx.shape, NEG, F32)
        sm[...] = jnp.zeros(sm.shape, F32)
        acc[...] = jnp.zeros(acc.shape, F32)
        cols = [slice(h * HD, (h + 1) * HD) for h in range(HEADS)]
        parts = [slice(h * 8, (h + 1) * 8) for h in range(HEADS)]

        def score_pass(start, size):
            rk = pl.ds(pl.multiple_of(start, UNIT), size)
            key_pos = start + lax.broadcasted_iota(jnp.int32, (size, QF), 0)
            allowed = (key_pos >= key_lo) & (key_pos < key_hi)
            raw = [mm_t(ks[rk, c], qs[rq, c]) for c in cols]
            for h, part in enumerate(parts):
                s = jnp.where(allowed, raw[h], NEG)
                sc[h, rk, :] = s
                mx[part, :] = jnp.maximum(mx[part, :], jnp.max(s.reshape(size // 8, 8, QF), axis=0))

        over_keys(lo, hi, KB, score_pass)
        peak = [jnp.max(mx[part, :], axis=0, keepdims=True) * SCALE2 for part in parts]

        def value_pass(start, size):
            rk = pl.ds(pl.multiple_of(start, UNIT), size)
            probs = []
            for h, part in enumerate(parts):
                p = jnp.exp2(sc[h, rk, :] * SCALE2 - peak[h])
                sm[part, :] = sm[part, :] + jnp.sum(p.reshape(size // 8, 8, QF), axis=0)
                probs.append(p.astype(BF))
            for h, c in enumerate(cols):
                acc[c, :] = acc[c, :] + mm(vt[c, rk], probs[h])

        over_keys(lo, hi, KB, value_pass)
        here = pl.ds(pl.multiple_of(n * QF, QF), QF)
        padding = key_hi == 0
        own_values = vt[:, rq]
        for h, (c, part) in enumerate(zip(cols, parts)):
            total = jnp.sum(sm[part, :], axis=0, keepdims=True)
            o = jnp.where(padding, own_values[c, :].astype(F32), acc[c, :] * (1.0 / total))
            att_o[here, c] = o.T.astype(BF)
            lse_o[h : h + 1, here] = peak[h] + jnp.log2(total)
        return carry

    @pl.when(i >= proj_steps)
    def _():
        lax.fori_loop(0, ATT, attend, 0)


def forward(ctx, qry, tok, wq, wk, wv, bq, bv):
    rows, width = tok.shape
    ps, qn = rows // PROJ, rows // (ATT * QF)
    struct = jax.ShapeDtypeStruct
    proj = pl.BlockSpec((PROJ, width), lambda i, *_: (jnp.minimum(i, ps - 1), 0))
    proj_t = pl.BlockSpec((width, PROJ), lambda i, *_: (0, jnp.minimum(i, ps - 1)))
    att = pl.BlockSpec((ATT * QF, width), lambda i, *_: (jnp.maximum(i - ps, 0), 0))
    att_t = pl.BlockSpec((8, ATT * QF), lambda i, *_: (0, jnp.maximum(i - ps, 0)))
    spec = pltpu.PrefetchScalarGridSpec(
        num_scalar_prefetch=2,
        grid=(ps + qn,),
        in_specs=[proj] + [full((width, width))] * 3 + [full((1, width))] * 2,
        out_specs=[proj] * 3 + [proj_t, att, att_t],
        scratch_shapes=[
            pltpu.VMEM((rows, width), BF),
            pltpu.VMEM((rows, width), BF),
            pltpu.VMEM((width, rows), BF),
            pltpu.VMEM((8 * HEADS, QF), F32),
            pltpu.VMEM((8 * HEADS, QF), F32),
            pltpu.VMEM((width, QF), F32),
            pltpu.VMEM((HEADS, rows, QF), F32),
        ],
    )
    return pl.pallas_call(
        functools.partial(forward_kernel, rows),
        grid_spec=spec,
        out_shape=[pltpu.HBM((rows, width), BF)] * 3
        + [pltpu.HBM((width, rows), BF), pltpu.HBM((rows, width), BF), pltpu.HBM((8, rows), F32)],
        compiler_params=pltpu.CompilerParams(vmem_limit_bytes=58 << 20),
        name="attention_forward",
    )(ctx, qry, tok, wq, wk, wv, bq[None], bv[None])


def middle_kernel(
    core, ctx, qry, tok, og, att, w_out, b_out, g1, b1, w_h, b_h, w_b, b_b, g2, b2,
    out_o, dsum_o, dbr_o, keep_o, send_o, vec, pack,
):
    i = pl.program_id(0)
    total = slot_bounds(ctx, qry)[-1][2]
    width = tok.shape[1]
    ff = w_h.shape[1]
    count = 2
    sub = ROWS // count
    rows = [slice(n * sub, (n + 1) * sub) for n in range(count)]

    @pl.when(i == 0)
    def _():
        pack[...] = jnp.zeros(pack.shape, F32)
        vec[...] = jnp.zeros(vec.shape, F32)

    def add(row, value):
        for r in range(0, value.shape[0], PIECE):
            half, at = divmod(row + r, pack.shape[1])
            pack[half, at : at + PIECE, :] += value[r : r + PIECE]

    def mean(x):
        return jnp.mean(x, axis=1, keepdims=True)

    def each(f, *lists):
        return [f(*xs) for xs in zip(*lists)]

    def split(pairs):
        return [list(xs) for xs in zip(*pairs)]

    def cols(lists):
        return sum(jnp.sum(x.astype(F32), axis=0, keepdims=True) for x in lists)

    def first_norm(r, branch):
        x1 = tok[r, :].astype(F32) + (branch + b_out[...])
        xc1 = x1 - mean(x1)
        r1 = lax.rsqrt(mean(xc1 * xc1) + EPS)
        xh1 = xc1 * r1
        n1 = xh1 * g1[...] + b1[...]
        return r1, xh1, n1, n1.astype(BF)

    def gelu(hp):
        hp = hp + b_h[...]
        cdf = 0.5 * (1.0 + lax.erf(hp * (1.0 / math.sqrt(2.0))))
        slope = cdf + hp * (jnp.exp(-0.5 * hp * hp) * (1.0 / math.sqrt(2.0 * math.pi)))
        return (hp * cdf).astype(BF), slope

    def second_norm(r, n1, ffn):
        row = i * ROWS + r.start + lax.broadcasted_iota(jnp.int32, (sub, 1), 0)
        valid = (row < total).astype(F32)
        x2 = n1 + (ffn + b_b[...])
        xc2 = x2 - mean(x2)
        r2 = lax.rsqrt(mean(xc2 * xc2) + EPS)
        xh2 = xc2 * r2
        out_o[r, :] = ((xh2 * g2[...] + b2[...]) * valid).astype(BF)
        dy = og[r, :].astype(F32) * valid
        dx = dy * g2[...]
        d2 = r2 * (dx - mean(dx) - xh2 * mean(dx * xh2))
        dg2 = jnp.sum(dy * xh2, axis=0, keepdims=True)
        return d2, d2.astype(BF), dg2, jnp.sum(dy, axis=0, keepdims=True)

    def first_norm_back(r, r1, xh1, d2, dhn):
        dn = d2 + dhn
        dx1 = dn * g1[...]
        ds = r1 * (dx1 - mean(dx1) - xh1 * mean(dx1 * xh1))
        dsum_o[r, :] = ds
        dbr = ds.astype(BF)
        dbr_o[r, :] = dbr
        dg1 = jnp.sum(dn * xh1, axis=0, keepdims=True)
        return dbr, dg1, jnp.sum(dn, axis=0, keepdims=True)

    branch = [mm(att[r, :], w_out[...]) for r in rows]
    r1, xh1, n1, nl = split(each(first_norm, rows, branch))
    act, slope = split(each(gelu, [mm(x, w_h[...]) for x in nl]))
    ffn = [mm(x, w_b[...]) for x in act]
    d2, df, dg2, db2 = split(each(second_norm, rows, n1, ffn))
    dact = [mm_t(x, w_b[...]) for x in df]
    add(0, t_mm(jnp.concatenate(act), jnp.concatenate(df)))
    dh = each(lambda x, s: (x * s).astype(BF), dact, slope)
    dhn = [mm_t(x, w_h[...]) for x in dh]
    nl, dh_all = jnp.concatenate(nl), jnp.concatenate(dh)
    for n in range(ff // width):
        add(ff + n * width, t_mm(nl, dh_all[:, n * width : (n + 1) * width]))
    dbr, dg1, db1 = split(each(first_norm_back, rows, r1, xh1, d2, dhn))
    add(2 * ff, t_mm(att[...], jnp.concatenate(dbr)))
    dbo, dbh, dbb = cols(dbr), cols(dh), cols(df)
    dg1, db1, dg2, db2 = cols(dg1), cols(db1), cols(dg2), cols(db2)
    for n, v in enumerate((dbo, dg1, db1, dbh[:, :width], dbh[:, width:], dbb, dg2, db2)):
        vec[n : n + 1, :] += v

    @pl.when(i == pl.num_programs(0) - 1)
    def _():
        keep_o[...] = pack[core[0]]
        send_o[...] = pack[1 - core[0]]


def middle(core, ctx, qry, tok, og, att, w_out, b_out, g1, b1, w_h, b_h, w_b, b_b, g2, b2):
    rows, width = tok.shape
    ff = w_h.shape[1]
    half = ff + width // 2
    struct = jax.ShapeDtypeStruct
    row = pl.BlockSpec((ROWS, width), lambda i, *_: (i, 0))
    vec = full((1, width))
    spec = pltpu.PrefetchScalarGridSpec(
        num_scalar_prefetch=3,
        grid=(rows // ROWS,),
        in_specs=[row] * 3
        + [full((width, width)), vec, vec, vec, full((width, ff)), full((1, ff)), full((ff, width)), vec, vec, vec],
        out_specs=[row] * 3
        + [full((half, width)), full((half, width)), full((8, width))],
        scratch_shapes=[pltpu.VMEM((2, half, width), F32)],
    )
    return pl.pallas_call(
        middle_kernel,
        grid_spec=spec,
        out_shape=[
            pltpu.HBM((rows, width), BF),
            pltpu.HBM((rows, width), F32),
            struct((rows, width), BF),
            struct((half, width), F32),
            struct((half, width), F32),
            struct((8, width), F32),
        ],
        compiler_params=pltpu.CompilerParams(vmem_limit_bytes=40 << 20),
        name="ffn_and_norms",
    )(
        core, ctx, qry, tok, og, att, w_out, b_out[None], g1[None], b1[None], w_h, b_h[None], w_b, b_b[None],
        g2[None], b2[None],
    )


def attended_grad_kernel(att, dbr, w_out, datt_o, delta_o):
    da = mm_t(dbr[...], w_out[...]).astype(BF)
    datt_o[...] = da
    prod = att[...].astype(F32) * da.astype(F32)
    heads = [jnp.sum(prod[:, h * HD : (h + 1) * HD], axis=1, keepdims=True) for h in range(HEADS)]
    rest = jnp.zeros((prod.shape[0], HD - HEADS), F32)
    delta_o[...] = jnp.concatenate(heads + [rest], axis=1).T[:8]


def attended_grad(att, dbr, w_out):
    rows, width = att.shape
    row = pl.BlockSpec((2 * ROWS, width), lambda i: (i, 0))
    return pl.pallas_call(
        attended_grad_kernel,
        grid=(rows // (2 * ROWS),),
        in_specs=[row, row, full((width, width))],
        out_specs=[row, pl.BlockSpec((8, 2 * ROWS), lambda i: (0, i))],
        out_shape=[pltpu.HBM((rows, width), BF), pltpu.HBM((8, rows), F32)],
        compiler_params=pltpu.CompilerParams(vmem_limit_bytes=20 << 20),
        cost_estimate=LIGHT,
        name="attended_gradient",
    )(att, dbr, w_out)


def backward_kernel(
    rows, heads, ctx, qry, q, k, kt, v, do, lse, delta, dq_o, dk_o, dv_o, dqt, dka, dva
):
    width = heads * HD
    bounds = slot_bounds(ctx, qry)

    dka[...] = jnp.zeros(dka.shape, F32)
    dva[...] = jnp.zeros(dva.shape, F32)

    def block(i, carry):
        first = i * QB
        lo, hi = key_range(bounds, first, QB)
        key_lo, key_hi = row_bounds(bounds, first + lax.broadcasted_iota(jnp.int32, (1, QB), 1))
        rq = pl.ds(pl.multiple_of(first, QB), QB)
        dqt[...] = jnp.zeros(dqt.shape, F32)
        cols = [slice(h * HD, (h + 1) * HD) for h in range(heads)]

        def body(start, size):
            rk = pl.ds(pl.multiple_of(start, UNIT), size)
            key_pos = start + lax.broadcasted_iota(jnp.int32, (size, QB), 0)
            allowed = (key_pos >= key_lo) & (key_pos < key_hi)
            scores = [mm_t(k[rk, c], q[rq, c]) for c in cols]
            dprobs = [mm_t(v[rk, c], do[rq, c]) for c in cols]
            probs = []
            dscores = []
            for h in range(heads):
                p = jnp.where(allowed, jnp.exp2(scores[h] * SCALE2 - lse[h : h + 1, rq]), 0.0)
                probs.append(p.astype(BF))
                dscores.append((p * (dprobs[h] - delta[h : h + 1, rq])).astype(BF))
            for h, c in enumerate(cols):
                dva[rk, c] += mm(probs[h], do[rq, c])
                dka[rk, c] += mm(dscores[h], q[rq, c])
                dqt[c, :] += mm(kt[c, rk], dscores[h])

        over_keys(lo, hi, KB_BACK, body)
        dq_o[rq, :] = (dqt[...] * SCALE).T.astype(BF)
        return carry

    lax.fori_loop(0, rows // QB, block, 0)
    padding = lax.broadcasted_iota(jnp.int32, (rows, 1), 0) >= bounds[-1][2]
    dk_o[...] = (dka[...] * SCALE).astype(BF)
    dv_o[...] = (dva[...] + jnp.where(padding, do[...].astype(F32), 0.0)).astype(BF)


def backward(ctx, qry, q, k, kt, v, do, lse, delta):
    rows, width = q.shape
    struct = jax.ShapeDtypeStruct
    whole = full((rows, width))
    spec = pltpu.PrefetchScalarGridSpec(
        num_scalar_prefetch=2,
        grid=(1,),
        in_specs=[whole, whole, full((width, rows)), whole, whole, full((8, rows)), full((8, rows))],
        out_specs=[whole] * 3,
        scratch_shapes=[
            pltpu.VMEM((width, QB), F32),
            pltpu.VMEM((rows, width), F32),
            pltpu.VMEM((rows, width), F32),
        ],
    )
    return pl.pallas_call(
        functools.partial(backward_kernel, rows, HEADS),
        grid_spec=spec,
        out_shape=[struct((rows, width), BF)] * 3,
        compiler_params=pltpu.CompilerParams(vmem_limit_bytes=34 << 20),
        cost_estimate=pl.CostEstimate(flops=30 * 10**9, bytes_accessed=20 << 20, transcendentals=8 << 20),
        name="attention_backward",
    )(ctx, qry, q, k, kt, v, do, lse, delta)


def input_grad_kernel(ds, dq, dk, dv, wq, wk, wv, o):
    total = ds[...] + mm_t(dq[...], wq[...]) + mm_t(dk[...], wk[...]) + mm_t(dv[...], wv[...])
    o[...] = total.astype(BF)


def input_gradient(ds, dq, dk, dv, wq, wk, wv):
    rows, width = ds.shape
    row = pl.BlockSpec((ROWS, width), lambda i: (i, 0))
    square = pl.BlockSpec((width, width), lambda i: (0, 0))
    return pl.pallas_call(
        input_grad_kernel,
        grid=(rows // ROWS,),
        in_specs=[row] * 4 + [square] * 3,
        out_specs=row,
        out_shape=jax.ShapeDtypeStruct((rows, width), BF),
        compiler_params=pltpu.CompilerParams(vmem_limit_bytes=16 << 20),
        cost_estimate=LIGHT,
        name="input_gradient",
    )(ds, dq, dk, dv, wq, wk, wv)


def projection_kernel(core, tok, dq, dk, dv, vec, keep_o, small, *rest):
    sends, acc = rest[:-1], rest[-1]
    i = pl.program_id(0)

    @pl.when(i == 0)
    def _():
        acc[...] = jnp.zeros(acc.shape, F32)
        small[0:8, :] = vec[...]
        small[8:, :] = jnp.zeros((small.shape[0] - 8, small.shape[1]), F32)

    t = tok[...]
    width = t.shape[1]
    for n, g in enumerate((dq, dk, dv)):
        value = t_mm(t, g[...])
        for r in range(0, width, PIECE):
            half, at = divmod(n * width + r, acc.shape[1])
            acc[half, at : at + PIECE, :] += value[r : r + PIECE]
    small[8:9, :] += jnp.sum(dq[...].astype(F32), axis=0, keepdims=True)
    small[9:10, :] += jnp.sum(dv[...].astype(F32), axis=0, keepdims=True)

    @pl.when(i == pl.num_programs(0) - 1)
    def _():
        keep_o[...] = acc[core[0]]
        for n, send in enumerate(sends):
            send[...] = acc[1 - core[0], n * SEND : (n + 1) * SEND, :]


def projection_gradients(core, tok, dq, dk, dv, vec):
    rows, width = tok.shape
    half = 3 * width // 2
    struct = jax.ShapeDtypeStruct
    row = pl.BlockSpec((2 * ROWS, width), lambda i, *_: (i, 0))
    spec = pltpu.PrefetchScalarGridSpec(
        num_scalar_prefetch=1,
        grid=(rows // (2 * ROWS),),
        in_specs=[row] * 4 + [full((8, width))],
        out_specs=[full((half, width)), full((SMALL, width))] + [full((SEND, width))] * (half // SEND),
        scratch_shapes=[pltpu.VMEM((2, half, width), F32)],
    )
    return pl.pallas_call(
        projection_kernel,
        grid_spec=spec,
        out_shape=[
            struct((half, width), F32),
            struct((SMALL, width), F32),
        ]
        + [struct((SEND, width), F32)] * (half // SEND),
        compiler_params=pltpu.CompilerParams(vmem_limit_bytes=32 << 20),
        cost_estimate=LIGHT,
        name="projection_gradients",
    )(core, tok, dq, dk, dv, vec)


def split_kernel(where, *refs):
    for n in range(4):
        refs[8 + n][...] = refs[n][0] + refs[4 + n][0]


def add_and_split(where, x, got):
    rows, cols = x.shape[0] // 4, x.shape[1]
    step = rows // 2 if rows % 16 == 0 else rows
    ins = [pl.BlockSpec((1, step, cols), lambda i, w, n=n: (w[n], i, 0)) for n in range(4)]
    spec = pltpu.PrefetchScalarGridSpec(
        num_scalar_prefetch=1,
        grid=(rows // step,),
        in_specs=ins + ins,
        out_specs=[pl.BlockSpec((step, cols), lambda i, w: (i, 0))] * 4,
    )
    return pl.pallas_call(
        split_kernel,
        grid_spec=spec,
        out_shape=[jax.ShapeDtypeStruct((rows, cols), F32)] * 4,
        compiler_params=pltpu.CompilerParams(vmem_limit_bytes=32 << 20),
        name="add_and_split",
    )(where, *[x.reshape(4, rows, cols)] * 4, *[got.reshape(4, rows, cols)] * 4)


def split_small_kernel(where, x, small, got_small, *rest):
    gots, outs, total = rest[:-5], rest[-5:-1], rest[-1]
    rows = x.shape[0] // 4
    for n, got in enumerate(gots):
        at = slice(n * SEND, (n + 1) * SEND)
        total[at, :] = x[at, :] + got[...]
    for n in range(4):
        outs[n][:rows, :] = total[pl.ds(pl.multiple_of(where[n] * rows, 8), rows), :]
        outs[n][rows:, :] = small[...] + got_small[...]


def add_and_split_small(where, x, small, got_small, *gots):
    rows, cols = x.shape[0] // 4, x.shape[1]
    whole = pl.BlockSpec(memory_space=pltpu.VMEM)
    return pl.pallas_call(
        split_small_kernel,
        in_specs=[pl.BlockSpec(memory_space=pltpu.SMEM)] + [whole] * (3 + len(gots)),
        out_specs=[whole] * 4,
        out_shape=[jax.ShapeDtypeStruct((rows + small.shape[0], cols), F32)] * 4,
        scratch_shapes=[pltpu.VMEM(x.shape, F32)],
        compiler_params=pltpu.CompilerParams(vmem_limit_bytes=16 << 20),
        name="add_and_split_small",
    )(where, x, small, got_small, *gots)


def unpack_kernel(places, piece, first, count, results, order, *refs):
    sources, outs = refs[:count], refs[count + results : -3]
    held, in_sem, out_sem = refs[-3:]

    def loads(n):
        return pltpu.make_async_copy(sources[n], held.at[n], in_sem.at[n])

    def copies(n, p):
        made = []
        for start, count, out, row, col in places:
            if start // piece == p:
                to = outs[out].at[pl.ds(row, count), pl.ds(col, held.shape[2])]
                from_ = held.at[n, pl.ds(start % piece, count)]
                made.append(pltpu.make_async_copy(from_, to, out_sem.at[n, len(made)]))
        return made

    for n in range(count):
        loads(n).start()
    for action in ("start", "wait"):
        for n in range(count):
            if action == "start":
                loads(n).wait()
            for p in range(4):

                @pl.when(order[first + n] == p)
                def _(n=n, p=p):
                    for c in copies(n, p):
                        c.start() if action == "start" else c.wait()


def unpack(places, shapes, order, sources, first=0, results=()):
    anywhere = pl.BlockSpec(memory_space=pl.ANY)
    count = len(sources)
    piece = sources[0].shape[0]
    places = cut(places, piece)
    most = max(sum(p[0] // piece == n for p in places) for n in range(4))
    return pl.pallas_call(
        functools.partial(unpack_kernel, places, piece, first, count, len(results)),
        in_specs=[pl.BlockSpec(memory_space=pltpu.SMEM)] + [anywhere] * (count + len(results)),
        out_specs=[anywhere] * len(shapes),
        out_shape=[jax.ShapeDtypeStruct(s, F32) for s in shapes],
        scratch_shapes=[
            pltpu.VMEM((count,) + sources[0].shape, F32),
            pltpu.SemaphoreType.DMA((count,)),
            pltpu.SemaphoreType.DMA((count, most)),
        ],
        input_output_aliases={1 + count + n: n for n in range(len(results))},
        compiler_params=pltpu.CompilerParams(vmem_limit_bytes=24 << 20),
        name="unpack",
    )(order, *sources, *results)


def swap_pairs(sizes, mask):
    dp, dq = sizes
    return [(p * dq + q, p * dq + (q ^ mask[p % 2])) for p in range(dp) for q in range(dq)]


class Ring:
    def __init__(self, sizes):
        dp, dq = sizes
        self.sizes = sizes
        self.core = lax.axis_index("dp") & 1
        me = lax.axis_index("dq")
        first, second = me & 1, (me >> 1) & 1
        self.low = jnp.where(self.core == 0, first, second)
        self.high = jnp.where(self.core == 0, second, first)
        place = 2 * self.high + self.low
        turned = [place ^ jnp.where(self.core == 0, a, b) for a, b in ((0, 0), (1, 2), (2, 1), (3, 3))]
        self.where = jnp.stack(turned).astype(jnp.int32)
        mine, other = 2 * self.core, 2 - 2 * self.core
        high = jnp.where(self.core == 0, first, second)
        self.order = jnp.stack(
            [mine + self.high, mine + 1 - self.high, other + high, other + 1 - high]
        ).astype(jnp.int32)
        bits = list(range(2, dq.bit_length() - 1))
        swapped = bits[1::-1] + bits[2:]
        self.far = [swap_pairs(sizes, (1 << a, 1 << b)) for a, b in zip(bits, swapped)]
        self.outer = [[(p, p ^ (1 << b)) for p in range(dp)] for b in range(1, dp.bit_length() - 1)]

    def core_start(self, send):
        return lax.ppermute(send, "dp", [(p, p ^ 1) for p in range(self.sizes[0])])

    def plane_start(self, sends):
        return [
            lax.ppermute(s, ("dp", "dq"), swap_pairs(self.sizes, (m, m))) for m, s in zip((1, 2, 3), sends)
        ]

    def plane_end(self, own, got):
        return (own + got[0]) + (got[1] + got[2])

    def far_start(self, x, n):
        return lax.ppermute(x, ("dp", "dq"), self.far[n])

    def rest(self, x):
        for pairs in self.far[2:]:
            x = x + lax.ppermute(x, ("dp", "dq"), pairs)
        for pairs in self.outer:
            x = x + lax.ppermute(x, "dp", pairs)
        return x

    def back_start(self, x, n):
        return lax.ppermute(x, ("dp", "dq"), swap_pairs(self.sizes, ((1, 2), (2, 1))[n]))

    def back_end(self, x, got, n):
        bit = (self.low, self.high)[n]
        return jnp.where(bit == 0, jnp.concatenate([x, got]), jnp.concatenate([got, x]))


def in_hbm(x):
    return pltpu.with_memory_space_constraint(x, pltpu.HBM)


def tie(*groups):
    return lax.optimization_barrier(groups)


def local(
    sizes, tokens, out_grad, context_len, query_count, w_query, w_key, w_value, b_query, b_value, w_out, b_out,
    norm1_gain, norm1_bias, w_hidden, b_hidden, w_back, b_back, norm2_gain, norm2_bias,
):
    width = tokens.shape[1]
    ff = w_hidden.shape[1]
    ring = Ring(sizes)
    rows_of_tokens = tokens
    tokens, out_grad, w_query, w_key, w_value, w_hidden, w_back = [
        in_hbm(x) for x in (tokens, out_grad, w_query, w_key, w_value, w_hidden, w_back)
    ]
    core = ring.core.reshape(1).astype(jnp.int32)
    q, k, v, kt, att, lse = forward(
        context_len, query_count, tokens, w_query, w_key, w_value, b_query, b_value
    )
    output, ds, dbr, keep, send, vec = middle(
        core, context_len, query_count, tokens, out_grad, in_hbm(att), w_out, b_out, norm1_gain, norm1_bias,
        w_hidden, b_hidden, w_back, b_back, norm2_gain, norm2_bias,
    )
    got = ring.core_start(send)
    send, att, dbr = tie(send, att, dbr)
    datt, delta = attended_grad(att, dbr, w_out)
    got, datt, delta = tie(got, datt, delta)
    one, *sends = add_and_split(ring.where, keep, got)
    got_one = ring.plane_start(sends)
    one, ins = tie(one, (context_len, query_count, q, k, kt, v, datt, lse, delta))
    dq, dk, dv = backward(*ins)
    one, got_one, dq, dk, dv = tie(one, got_one, dq, dk, dv)
    one = ring.plane_end(one, got_one)
    got_one = ring.far_start(one, 0)
    one, dq, dk, dv = tie(one, dq, dk, dv)
    keep, small, *sends = projection_gradients(core, rows_of_tokens, dq, dk, dv, vec)
    got = [ring.core_start(s) for s in [small] + sends]
    one = one + got_one
    middle_row = one.shape[0] // 2
    got_one = [ring.far_start(x, 1) for x in (one[:middle_row], one[middle_row:])]
    two, *sends = add_and_split_small(ring.where, keep, small, *got)
    got_two = ring.plane_start(sends)
    one, two, sends, dq, dk, dv, ds = tie(one, two, sends, dq, dk, dv, ds)
    input_grad = input_gradient(in_hbm(ds), dq, dk, dv, w_query, w_key, w_value)
    one, got_one, two, got_two, input_grad = tie(one, got_one, two, got_two, input_grad)
    one = ring.rest(one + jnp.concatenate(got_one))
    got_one = ring.back_start(one, 0)
    two = ring.plane_end(two, got_two)
    got_two = ring.far_start(two, 0)
    one, got_one, two, got_two = tie(one, got_one, two, got_two)
    one = ring.back_end(one, got_one, 0)
    got_one = ring.back_start(one, 1)
    home_one = ring.core_start(one)
    two = two + got_two
    got_two = ring.far_start(two, 1)
    one, two, got_two = tie(one, two, got_two)
    two = ring.rest(two + got_two)
    small = two[-SMALL:]
    two = two[:-SMALL]
    vectors = [small[n] for n in (8, 9, 0, 1, 2)] + [small[3:5].reshape(-1)] + [small[n] for n in (5, 6, 7)]
    got_two = ring.back_start(two, 0)
    one, got_one, home_one, two, got_two = tie(one, got_one, home_one, two, got_two)
    two = ring.back_end(two, got_two, 0)
    got_two = ring.back_start(two, 1)
    home_two = ring.core_start(two)
    last_one = ring.core_start(got_one)
    places = [(0, ff, 0, 0, 0)]
    places += [(ff + n * width, width, 1, 0, n * width) for n in range(ff // width)]
    places += [(2 * ff, width, 2, 0, 0)]
    shapes = [(ff, width), (width, ff), (width, width)]
    gwb, gwh, gwo = unpack(
        places, shapes, ring.order, [in_hbm(x) for x in (one, got_one, home_one, last_one)]
    )
    two, got_two, home_two, gwb, gwh, gwo, vectors = tie(two, got_two, home_two, gwb, gwh, gwo, vectors)
    places = [(n * width, width, n, 0, 0) for n in range(3)]
    last_two = ring.core_start(got_two)
    shapes = [(width, width)] * 3
    squares = unpack(places, shapes, ring.order, (two, got_two, home_two))
    gq, gk, gv = unpack(places, shapes, ring.order, (last_two,), 3, squares)
    return (
        output,
        input_grad,
        gq,
        gk,
        gv,
        vectors[0],
        vectors[1],
        gwo,
        vectors[2],
        vectors[3],
        vectors[4],
        gwh,
        vectors[5],
        gwb,
        vectors[6],
        vectors[7],
        vectors[8],
    )


def cut(places, piece):
    out = []
    for start, rows, to, row, col in places:
        at = start
        while at < start + rows:
            end = min((at // piece + 1) * piece, start + rows)
            out.append((at, end - at, to, row + at - start, col))
            at = end
    return out


def solution(mesh):
    sizes = (mesh.shape["dp"], mesh.shape["dq"])
    return jax.shard_map(
        functools.partial(local, sizes),
        mesh=mesh,
        in_specs=(
            P(("dp", "dq"), None),
            P(("dp", "dq"), None),
            P(("dp", "dq"), None),
            P(("dp", "dq"), None),
            P(),
            P(),
            P(),
            P(),
            P(),
            P(),
            P(),
            P(),
            P(),
            P(),
            P(),
            P(),
            P(),
            P(),
            P(),
        ),
        out_specs=(
            P(("dp", "dq"), None),
            P(("dp", "dq"), None),
            P(),
            P(),
            P(),
            P(),
            P(),
            P(),
            P(),
            P(),
            P(),
            P(),
            P(),
            P(),
            P(),
            P(),
            P(),
        ),
        check_vma=False,
    )
```

```python
import functools
import math

import jax
import jax.experimental.pallas as pl
import jax.experimental.pallas.tpu as pltpu
import jax.numpy as jnp
from jax import lax
from jax.sharding import PartitionSpec as P

HEADS = 4
HD = 128
SLOTS = 8
EPS = 1e-5
SCALE = 1.0 / math.sqrt(HD)
SCALE2 = SCALE * math.log2(math.e)
NEG = -1e30
F32 = jnp.float32
BF = jnp.bfloat16
ROWS = 512
QF = 512
QB = 256
KB = 1024
KB_BACK = 1024
UNIT = 128
PROJ = 1024
ATT = 2
PIECE = 256
LIGHT = pl.CostEstimate(flops=1, bytes_accessed=1, transcendentals=0)
SMALL = 16
SEND = 128


def mm(a, b):
    return jnp.dot(a, b, preferred_element_type=F32)


def mm_t(a, b):
    return lax.dot_general(a, b, (((1,), (1,)), ((), ())), preferred_element_type=F32)


def t_mm(a, b):
    return lax.dot_general(a, b, (((0,), (0,)), ((), ())), preferred_element_type=F32)


def slot_bounds(ctx, qry):
    out = []
    start = jnp.int32(0)
    for t in range(SLOTS):
        c = ctx[0, t]
        end = start + c + qry[0, t]
        out.append((start, start + c, end))
        start = end
    return out


def key_range(bounds, first, rows):
    lo = jnp.int32(1 << 30)
    hi = jnp.int32(0)
    for start, ctx_end, end in bounds:
        hit = (start < first + rows) & (end > first) & (end > start)
        lo = jnp.where(hit, jnp.minimum(lo, start), lo)
        hi = jnp.where(hit, jnp.maximum(hi, ctx_end), hi)
    return lo, hi


def row_bounds(bounds, pos):
    lo = jnp.zeros(pos.shape, jnp.int32)
    hi = jnp.zeros(pos.shape, jnp.int32)
    for start, ctx_end, end in bounds:
        inside = (pos >= start) & (pos < end)
        lo = jnp.where(inside, start, lo)
        hi = jnp.where(inside, ctx_end, hi)
    return lo, hi


def over_keys(lo, hi, most, body):
    start = lo // UNIT * UNIT
    units = jnp.maximum((hi - start + UNIT - 1) // UNIT, 0)
    whole = units // (most // UNIT)

    def step(j, carry):
        body(start + j * most, most)
        return carry

    lax.fori_loop(0, whole, step, 0)
    done = whole * (most // UNIT)
    size = most // 2
    while size >= UNIT:
        take = (units - done) // (size // UNIT)
        pl.when(take > 0)(functools.partial(body, start + done * UNIT, size))
        done = done + take * (size // UNIT)
        size //= 2


def full(shape):
    return pl.BlockSpec(shape, lambda i, *_: (0,) * len(shape), pipeline_mode=pl.Buffered(1))


def forward_kernel(
    rows, ctx, qry, tok, wq, wk, wv, bq, bv, q_o, k_o, v_o, kt_o, att_o, lse_o, qs, ks, vt, mx, sm, acc, sc
):
    i = pl.program_id(0)
    proj_steps = rows // PROJ

    @pl.when(i < proj_steps)
    def _():
        t = tok[...]
        r = pl.ds(pl.multiple_of(i * PROJ, PROJ), PROJ)
        q = (mm(t, wq[...]) + bq[...]).astype(BF)
        qs[r, :] = q
        q_o[...] = q
        k = mm(t, wk[...]).astype(BF)
        ks[r, :] = k
        k_o[...] = k
        kt_o[...] = k.T
        v = (mm(t, wv[...]) + bv[...]).astype(BF)
        v_o[...] = v
        vt[:, r] = v.T

    def attend(n, carry):
        first = (i - proj_steps) * (ATT * QF) + n * QF
        bounds = slot_bounds(ctx, qry)
        lo, hi = key_range(bounds, first, QF)
        key_lo, key_hi = row_bounds(bounds, first + lax.broadcasted_iota(jnp.int32, (1, QF), 1))
        rq = pl.ds(pl.multiple_of(first, QF), QF)
        mx[...] = jnp.full(mx.shape, NEG, F32)
        sm[...] = jnp.zeros(sm.shape, F32)
        acc[...] = jnp.zeros(acc.shape, F32)
        cols = [slice(h * HD, (h + 1) * HD) for h in range(HEADS)]
        parts = [slice(h * 8, (h + 1) * 8) for h in range(HEADS)]

        def score_pass(start, size):
            rk = pl.ds(pl.multiple_of(start, UNIT), size)
            key_pos = start + lax.broadcasted_iota(jnp.int32, (size, QF), 0)
            allowed = (key_pos >= key_lo) & (key_pos < key_hi)
            raw = [mm_t(ks[rk, c], qs[rq, c]) for c in cols]
            for h, part in enumerate(parts):
                s = jnp.where(allowed, raw[h], NEG)
                sc[h, rk, :] = s
                mx[part, :] = jnp.maximum(mx[part, :], jnp.max(s.reshape(size // 8, 8, QF), axis=0))

        over_keys(lo, hi, KB, score_pass)
        peak = [jnp.max(mx[part, :], axis=0, keepdims=True) * SCALE2 for part in parts]

        def value_pass(start, size):
            rk = pl.ds(pl.multiple_of(start, UNIT), size)
            probs = []
            for h, part in enumerate(parts):
                p = jnp.exp2(sc[h, rk, :] * SCALE2 - peak[h])
                sm[part, :] = sm[part, :] + jnp.sum(p.reshape(size // 8, 8, QF), axis=0)
                probs.append(p.astype(BF))
            for h, c in enumerate(cols):
                acc[c, :] = acc[c, :] + mm(vt[c, rk], probs[h])

        over_keys(lo, hi, KB, value_pass)
        here = pl.ds(pl.multiple_of(n * QF, QF), QF)
        padding = key_hi == 0
        own_values = vt[:, rq]
        for h, (c, part) in enumerate(zip(cols, parts)):
            total = jnp.sum(sm[part, :], axis=0, keepdims=True)
            o = jnp.where(padding, own_values[c, :].astype(F32), acc[c, :] * (1.0 / total))
            att_o[here, c] = o.T.astype(BF)
            lse_o[h : h + 1, here] = peak[h] + jnp.log2(total)
        return carry

    @pl.when(i >= proj_steps)
    def _():
        lax.fori_loop(0, ATT, attend, 0)


def forward(ctx, qry, tok, wq, wk, wv, bq, bv):
    rows, width = tok.shape
    ps, qn = rows // PROJ, rows // (ATT * QF)
    struct = jax.ShapeDtypeStruct
    proj = pl.BlockSpec((PROJ, width), lambda i, *_: (jnp.minimum(i, ps - 1), 0))
    proj_t = pl.BlockSpec((width, PROJ), lambda i, *_: (0, jnp.minimum(i, ps - 1)))
    att = pl.BlockSpec((ATT * QF, width), lambda i, *_: (jnp.maximum(i - ps, 0), 0))
    att_t = pl.BlockSpec((8, ATT * QF), lambda i, *_: (0, jnp.maximum(i - ps, 0)))
    spec = pltpu.PrefetchScalarGridSpec(
        num_scalar_prefetch=2,
        grid=(ps + qn,),
        in_specs=[proj] + [full((width, width))] * 3 + [full((1, width))] * 2,
        out_specs=[proj] * 3 + [proj_t, att, att_t],
        scratch_shapes=[
            pltpu.VMEM((rows, width), BF),
            pltpu.VMEM((rows, width), BF),
            pltpu.VMEM((width, rows), BF),
            pltpu.VMEM((8 * HEADS, QF), F32),
            pltpu.VMEM((8 * HEADS, QF), F32),
            pltpu.VMEM((width, QF), F32),
            pltpu.VMEM((HEADS, rows, QF), F32),
        ],
    )
    return pl.pallas_call(
        functools.partial(forward_kernel, rows),
        grid_spec=spec,
        out_shape=[pltpu.HBM((rows, width), BF)] * 3
        + [pltpu.HBM((width, rows), BF), pltpu.HBM((rows, width), BF), pltpu.HBM((8, rows), F32)],
        compiler_params=pltpu.CompilerParams(vmem_limit_bytes=58 << 20),
        name="attention_forward",
    )(ctx, qry, tok, wq, wk, wv, bq[None], bv[None])


def middle_kernel(
    core, ctx, qry, tok, og, att, w_out, b_out, g1, b1, w_h, b_h, w_b, b_b, g2, b2,
    out_o, dsum_o, dbr_o, keep_o, send_o, vec, pack,
):
    i = pl.program_id(0)
    total = slot_bounds(ctx, qry)[-1][2]
    width = tok.shape[1]
    ff = w_h.shape[1]
    count = 2
    sub = ROWS // count
    rows = [slice(n * sub, (n + 1) * sub) for n in range(count)]

    @pl.when(i == 0)
    def _():
        pack[...] = jnp.zeros(pack.shape, F32)
        vec[...] = jnp.zeros(vec.shape, F32)

    def add(row, value):
        for r in range(0, value.shape[0], PIECE):
            half, at = divmod(row + r, pack.shape[1])
            pack[half, at : at + PIECE, :] += value[r : r + PIECE]

    def mean(x):
        return jnp.mean(x, axis=1, keepdims=True)

    def each(f, *lists):
        return [f(*xs) for xs in zip(*lists)]

    def split(pairs):
        return [list(xs) for xs in zip(*pairs)]

    def cols(lists):
        return sum(jnp.sum(x.astype(F32), axis=0, keepdims=True) for x in lists)

    def first_norm(r, branch):
        x1 = tok[r, :].astype(F32) + (branch + b_out[...])
        xc1 = x1 - mean(x1)
        r1 = lax.rsqrt(mean(xc1 * xc1) + EPS)
        xh1 = xc1 * r1
        n1 = xh1 * g1[...] + b1[...]
        return r1, xh1, n1, n1.astype(BF)

    def gelu(hp):
        hp = hp + b_h[...]
        cdf = 0.5 * (1.0 + lax.erf(hp * (1.0 / math.sqrt(2.0))))
        slope = cdf + hp * (jnp.exp(-0.5 * hp * hp) * (1.0 / math.sqrt(2.0 * math.pi)))
        return (hp * cdf).astype(BF), slope

    def second_norm(r, n1, ffn):
        row = i * ROWS + r.start + lax.broadcasted_iota(jnp.int32, (sub, 1), 0)
        valid = (row < total).astype(F32)
        x2 = n1 + (ffn + b_b[...])
        xc2 = x2 - mean(x2)
        r2 = lax.rsqrt(mean(xc2 * xc2) + EPS)
        xh2 = xc2 * r2
        out_o[r, :] = ((xh2 * g2[...] + b2[...]) * valid).astype(BF)
        dy = og[r, :].astype(F32) * valid
        dx = dy * g2[...]
        d2 = r2 * (dx - mean(dx) - xh2 * mean(dx * xh2))
        dg2 = jnp.sum(dy * xh2, axis=0, keepdims=True)
        return d2, d2.astype(BF), dg2, jnp.sum(dy, axis=0, keepdims=True)

    def first_norm_back(r, r1, xh1, d2, dhn):
        dn = d2 + dhn
        dx1 = dn * g1[...]
        ds = r1 * (dx1 - mean(dx1) - xh1 * mean(dx1 * xh1))
        dsum_o[r, :] = ds
        dbr = ds.astype(BF)
        dbr_o[r, :] = dbr
        dg1 = jnp.sum(dn * xh1, axis=0, keepdims=True)
        return dbr, dg1, jnp.sum(dn, axis=0, keepdims=True)

    branch = [mm(att[r, :], w_out[...]) for r in rows]
    r1, xh1, n1, nl = split(each(first_norm, rows, branch))
    act, slope = split(each(gelu, [mm(x, w_h[...]) for x in nl]))
    ffn = [mm(x, w_b[...]) for x in act]
    d2, df, dg2, db2 = split(each(second_norm, rows, n1, ffn))
    dact = [mm_t(x, w_b[...]) for x in df]
    add(0, t_mm(jnp.concatenate(act), jnp.concatenate(df)))
    dh = each(lambda x, s: (x * s).astype(BF), dact, slope)
    dhn = [mm_t(x, w_h[...]) for x in dh]
    nl, dh_all = jnp.concatenate(nl), jnp.concatenate(dh)
    for n in range(ff // width):
        add(ff + n * width, t_mm(nl, dh_all[:, n * width : (n + 1) * width]))
    dbr, dg1, db1 = split(each(first_norm_back, rows, r1, xh1, d2, dhn))
    add(2 * ff, t_mm(att[...], jnp.concatenate(dbr)))
    dbo, dbh, dbb = cols(dbr), cols(dh), cols(df)
    dg1, db1, dg2, db2 = cols(dg1), cols(db1), cols(dg2), cols(db2)
    for n, v in enumerate((dbo, dg1, db1, dbh[:, :width], dbh[:, width:], dbb, dg2, db2)):
        vec[n : n + 1, :] += v

    @pl.when(i == pl.num_programs(0) - 1)
    def _():
        keep_o[...] = pack[core[0]]
        send_o[...] = pack[1 - core[0]]


def middle(core, ctx, qry, tok, og, att, w_out, b_out, g1, b1, w_h, b_h, w_b, b_b, g2, b2):
    rows, width = tok.shape
    ff = w_h.shape[1]
    half = ff + width // 2
    struct = jax.ShapeDtypeStruct
    row = pl.BlockSpec((ROWS, width), lambda i, *_: (i, 0))
    vec = full((1, width))
    spec = pltpu.PrefetchScalarGridSpec(
        num_scalar_prefetch=3,
        grid=(rows // ROWS,),
        in_specs=[row] * 3
        + [full((width, width)), vec, vec, vec, full((width, ff)), full((1, ff)), full((ff, width)), vec, vec, vec],
        out_specs=[row] * 3
        + [full((half, width)), full((half, width)), full((8, width))],
        scratch_shapes=[pltpu.VMEM((2, half, width), F32)],
    )
    return pl.pallas_call(
        middle_kernel,
        grid_spec=spec,
        out_shape=[
            pltpu.HBM((rows, width), BF),
            pltpu.HBM((rows, width), F32),
            struct((rows, width), BF),
            struct((half, width), F32),
            struct((half, width), F32),
            struct((8, width), F32),
        ],
        compiler_params=pltpu.CompilerParams(vmem_limit_bytes=40 << 20),
        name="ffn_and_norms",
    )(
        core, ctx, qry, tok, og, att, w_out, b_out[None], g1[None], b1[None], w_h, b_h[None], w_b, b_b[None],
        g2[None], b2[None],
    )


def attended_grad_kernel(att, dbr, w_out, datt_o, delta_o):
    da = mm_t(dbr[...], w_out[...]).astype(BF)
    datt_o[...] = da
    prod = att[...].astype(F32) * da.astype(F32)
    heads = [jnp.sum(prod[:, h * HD : (h + 1) * HD], axis=1, keepdims=True) for h in range(HEADS)]
    rest = jnp.zeros((prod.shape[0], HD - HEADS), F32)
    delta_o[...] = jnp.concatenate(heads + [rest], axis=1).T[:8]


def attended_grad(att, dbr, w_out):
    rows, width = att.shape
    row = pl.BlockSpec((2 * ROWS, width), lambda i: (i, 0))
    return pl.pallas_call(
        attended_grad_kernel,
        grid=(rows // (2 * ROWS),),
        in_specs=[row, row, full((width, width))],
        out_specs=[row, pl.BlockSpec((8, 2 * ROWS), lambda i: (0, i))],
        out_shape=[pltpu.HBM((rows, width), BF), pltpu.HBM((8, rows), F32)],
        compiler_params=pltpu.CompilerParams(vmem_limit_bytes=20 << 20),
        cost_estimate=LIGHT,
        name="attended_gradient",
    )(att, dbr, w_out)


def backward_kernel(
    rows, heads, ctx, qry, q, k, kt, v, do, lse, delta, dq_o, dk_o, dv_o, dqt, dka, dva
):
    width = heads * HD
    bounds = slot_bounds(ctx, qry)

    dka[...] = jnp.zeros(dka.shape, F32)
    dva[...] = jnp.zeros(dva.shape, F32)

    def block(i, carry):
        first = i * QB
        lo, hi = key_range(bounds, first, QB)
        key_lo, key_hi = row_bounds(bounds, first + lax.broadcasted_iota(jnp.int32, (1, QB), 1))
        rq = pl.ds(pl.multiple_of(first, QB), QB)
        dqt[...] = jnp.zeros(dqt.shape, F32)
        cols = [slice(h * HD, (h + 1) * HD) for h in range(heads)]

        def body(start, size):
            rk = pl.ds(pl.multiple_of(start, UNIT), size)
            key_pos = start + lax.broadcasted_iota(jnp.int32, (size, QB), 0)
            allowed = (key_pos >= key_lo) & (key_pos < key_hi)
            scores = [mm_t(k[rk, c], q[rq, c]) for c in cols]
            dprobs = [mm_t(v[rk, c], do[rq, c]) for c in cols]
            probs = []
            dscores = []
            for h in range(heads):
                p = jnp.where(allowed, jnp.exp2(scores[h] * SCALE2 - lse[h : h + 1, rq]), 0.0)
                probs.append(p.astype(BF))
                dscores.append((p * (dprobs[h] - delta[h : h + 1, rq])).astype(BF))
            for h, c in enumerate(cols):
                dva[rk, c] += mm(probs[h], do[rq, c])
                dka[rk, c] += mm(dscores[h], q[rq, c])
                dqt[c, :] += mm(kt[c, rk], dscores[h])

        over_keys(lo, hi, KB_BACK, body)
        dq_o[rq, :] = (dqt[...] * SCALE).T.astype(BF)
        return carry

    lax.fori_loop(0, rows // QB, block, 0)
    padding = lax.broadcasted_iota(jnp.int32, (rows, 1), 0) >= bounds[-1][2]
    dk_o[...] = (dka[...] * SCALE).astype(BF)
    dv_o[...] = (dva[...] + jnp.where(padding, do[...].astype(F32), 0.0)).astype(BF)


def backward(ctx, qry, q, k, kt, v, do, lse, delta):
    rows, width = q.shape
    struct = jax.ShapeDtypeStruct
    whole = full((rows, width))
    spec = pltpu.PrefetchScalarGridSpec(
        num_scalar_prefetch=2,
        grid=(1,),
        in_specs=[whole, whole, full((width, rows)), whole, whole, full((8, rows)), full((8, rows))],
        out_specs=[whole] * 3,
        scratch_shapes=[
            pltpu.VMEM((width, QB), F32),
            pltpu.VMEM((rows, width), F32),
            pltpu.VMEM((rows, width), F32),
        ],
    )
    return pl.pallas_call(
        functools.partial(backward_kernel, rows, HEADS),
        grid_spec=spec,
        out_shape=[struct((rows, width), BF)] * 3,
        compiler_params=pltpu.CompilerParams(vmem_limit_bytes=31 << 20),
        cost_estimate=pl.CostEstimate(flops=30 * 10**9, bytes_accessed=20 << 20, transcendentals=8 << 20),
        name="attention_backward",
    )(ctx, qry, q, k, kt, v, do, lse, delta)


def input_grad_kernel(ds, dq, dk, dv, wq, wk, wv, o):
    total = ds[...] + mm_t(dq[...], wq[...]) + mm_t(dk[...], wk[...]) + mm_t(dv[...], wv[...])
    o[...] = total.astype(BF)


def input_gradient(ds, dq, dk, dv, wq, wk, wv):
    rows, width = ds.shape
    row = pl.BlockSpec((ROWS, width), lambda i: (i, 0))
    square = pl.BlockSpec((width, width), lambda i: (0, 0))
    return pl.pallas_call(
        input_grad_kernel,
        grid=(rows // ROWS,),
        in_specs=[row] * 4 + [square] * 3,
        out_specs=row,
        out_shape=jax.ShapeDtypeStruct((rows, width), BF),
        compiler_params=pltpu.CompilerParams(vmem_limit_bytes=16 << 20),
        cost_estimate=LIGHT,
        name="input_gradient",
    )(ds, dq, dk, dv, wq, wk, wv)


def projection_kernel(core, tok, dq, dk, dv, vec, keep_o, small, *rest):
    sends, acc = rest[:-1], rest[-1]
    i = pl.program_id(0)

    @pl.when(i == 0)
    def _():
        acc[...] = jnp.zeros(acc.shape, F32)
        small[0:8, :] = vec[...]
        small[8:, :] = jnp.zeros((small.shape[0] - 8, small.shape[1]), F32)

    t = tok[...]
    width = t.shape[1]
    for n, g in enumerate((dq, dk, dv)):
        value = t_mm(t, g[...])
        for r in range(0, width, PIECE):
            half, at = divmod(n * width + r, acc.shape[1])
            acc[half, at : at + PIECE, :] += value[r : r + PIECE]
    small[8:9, :] += jnp.sum(dq[...].astype(F32), axis=0, keepdims=True)
    small[9:10, :] += jnp.sum(dv[...].astype(F32), axis=0, keepdims=True)

    @pl.when(i == pl.num_programs(0) - 1)
    def _():
        keep_o[...] = acc[core[0]]
        for n, send in enumerate(sends):
            send[...] = acc[1 - core[0], n * SEND : (n + 1) * SEND, :]


def projection_gradients(core, tok, dq, dk, dv, vec):
    rows, width = tok.shape
    half = 3 * width // 2
    struct = jax.ShapeDtypeStruct
    row = pl.BlockSpec((2 * ROWS, width), lambda i, *_: (i, 0))
    spec = pltpu.PrefetchScalarGridSpec(
        num_scalar_prefetch=1,
        grid=(rows // (2 * ROWS),),
        in_specs=[row] * 4 + [full((8, width))],
        out_specs=[full((half, width)), full((SMALL, width))] + [full((SEND, width))] * (half // SEND),
        scratch_shapes=[pltpu.VMEM((2, half, width), F32)],
    )
    return pl.pallas_call(
        projection_kernel,
        grid_spec=spec,
        out_shape=[
            struct((half, width), F32),
            struct((SMALL, width), F32),
        ]
        + [struct((SEND, width), F32)] * (half // SEND),
        compiler_params=pltpu.CompilerParams(vmem_limit_bytes=32 << 20),
        cost_estimate=LIGHT,
        name="projection_gradients",
    )(core, tok, dq, dk, dv, vec)


def split_kernel(where, *refs):
    for n in range(4):
        refs[8 + n][...] = refs[n][0] + refs[4 + n][0]


def add_and_split(where, x, got):
    rows, cols = x.shape[0] // 4, x.shape[1]
    step = rows // 2 if rows % 16 == 0 else rows
    ins = [pl.BlockSpec((1, step, cols), lambda i, w, n=n: (w[n], i, 0)) for n in range(4)]
    spec = pltpu.PrefetchScalarGridSpec(
        num_scalar_prefetch=1,
        grid=(rows // step,),
        in_specs=ins + ins,
        out_specs=[pl.BlockSpec((step, cols), lambda i, w: (i, 0))] * 4,
    )
    return pl.pallas_call(
        split_kernel,
        grid_spec=spec,
        out_shape=[jax.ShapeDtypeStruct((rows, cols), F32)] * 4,
        compiler_params=pltpu.CompilerParams(vmem_limit_bytes=32 << 20),
        name="add_and_split",
    )(where, *[x.reshape(4, rows, cols)] * 4, *[got.reshape(4, rows, cols)] * 4)


def split_small_kernel(where, x, small, got_small, *rest):
    gots, outs, total = rest[:-5], rest[-5:-1], rest[-1]
    rows = x.shape[0] // 4
    for n, got in enumerate(gots):
        at = slice(n * SEND, (n + 1) * SEND)
        total[at, :] = x[at, :] + got[...]
    for n in range(4):
        outs[n][:rows, :] = total[pl.ds(pl.multiple_of(where[n] * rows, 8), rows), :]
        outs[n][rows:, :] = small[...] + got_small[...]


def add_and_split_small(where, x, small, got_small, *gots):
    rows, cols = x.shape[0] // 4, x.shape[1]
    whole = pl.BlockSpec(memory_space=pltpu.VMEM)
    return pl.pallas_call(
        split_small_kernel,
        in_specs=[pl.BlockSpec(memory_space=pltpu.SMEM)] + [whole] * (3 + len(gots)),
        out_specs=[whole] * 4,
        out_shape=[jax.ShapeDtypeStruct((rows + small.shape[0], cols), F32)] * 4,
        scratch_shapes=[pltpu.VMEM(x.shape, F32)],
        compiler_params=pltpu.CompilerParams(vmem_limit_bytes=16 << 20),
        name="add_and_split_small",
    )(where, x, small, got_small, *gots)


def unpack_kernel(places, piece, first, count, results, order, *refs):
    sources, outs = refs[:count], refs[count + results : -3]
    held, in_sem, out_sem = refs[-3:]

    def loads(n):
        return pltpu.make_async_copy(sources[n], held.at[n], in_sem.at[n])

    def copies(n, p):
        made = []
        for start, count, out, row, col in places:
            if start // piece == p:
                to = outs[out].at[pl.ds(row, count), pl.ds(col, held.shape[2])]
                from_ = held.at[n, pl.ds(start % piece, count)]
                made.append(pltpu.make_async_copy(from_, to, out_sem.at[n, len(made)]))
        return made

    for n in range(count):
        loads(n).start()
    for action in ("start", "wait"):
        for n in range(count):
            if action == "start":
                loads(n).wait()
            for p in range(4):

                @pl.when(order[first + n] == p)
                def _(n=n, p=p):
                    for c in copies(n, p):
                        c.start() if action == "start" else c.wait()


def unpack(places, shapes, order, sources, first=0, results=()):
    anywhere = pl.BlockSpec(memory_space=pl.ANY)
    count = len(sources)
    piece = sources[0].shape[0]
    places = cut(places, piece)
    most = max(sum(p[0] // piece == n for p in places) for n in range(4))
    return pl.pallas_call(
        functools.partial(unpack_kernel, places, piece, first, count, len(results)),
        in_specs=[pl.BlockSpec(memory_space=pltpu.SMEM)] + [anywhere] * (count + len(results)),
        out_specs=[anywhere] * len(shapes),
        out_shape=[jax.ShapeDtypeStruct(s, F32) for s in shapes],
        scratch_shapes=[
            pltpu.VMEM((count,) + sources[0].shape, F32),
            pltpu.SemaphoreType.DMA((count,)),
            pltpu.SemaphoreType.DMA((count, most)),
        ],
        input_output_aliases={1 + count + n: n for n in range(len(results))},
        compiler_params=pltpu.CompilerParams(vmem_limit_bytes=24 << 20),
        name="unpack",
    )(order, *sources, *results)


def swap_pairs(sizes, mask):
    dp, dq = sizes
    return [(p * dq + q, p * dq + (q ^ mask[p % 2])) for p in range(dp) for q in range(dq)]


class Ring:
    def __init__(self, sizes):
        dp, dq = sizes
        self.sizes = sizes
        self.core = lax.axis_index("dp") & 1
        me = lax.axis_index("dq")
        first, second = me & 1, (me >> 1) & 1
        self.low = jnp.where(self.core == 0, first, second)
        self.high = jnp.where(self.core == 0, second, first)
        place = 2 * self.high + self.low
        turned = [place ^ jnp.where(self.core == 0, a, b) for a, b in ((0, 0), (1, 2), (2, 1), (3, 3))]
        self.where = jnp.stack(turned).astype(jnp.int32)
        mine, other = 2 * self.core, 2 - 2 * self.core
        high = jnp.where(self.core == 0, first, second)
        self.order = jnp.stack(
            [mine + self.high, mine + 1 - self.high, other + high, other + 1 - high]
        ).astype(jnp.int32)
        bits = list(range(2, dq.bit_length() - 1))
        swapped = bits[1::-1] + bits[2:]
        self.far = [swap_pairs(sizes, (1 << a, 1 << b)) for a, b in zip(bits, swapped)]
        self.outer = [[(p, p ^ (1 << b)) for p in range(dp)] for b in range(1, dp.bit_length() - 1)]

    def core_start(self, send):
        return lax.ppermute(send, "dp", [(p, p ^ 1) for p in range(self.sizes[0])])

    def plane_start(self, sends):
        return [
            lax.ppermute(s, ("dp", "dq"), swap_pairs(self.sizes, (m, m))) for m, s in zip((1, 2, 3), sends)
        ]

    def plane_end(self, own, got):
        return (own + got[0]) + (got[1] + got[2])

    def far_start(self, x, n):
        return lax.ppermute(x, ("dp", "dq"), self.far[n])

    def rest(self, x):
        for pairs in self.far[2:]:
            x = x + lax.ppermute(x, ("dp", "dq"), pairs)
        for pairs in self.outer:
            x = x + lax.ppermute(x, "dp", pairs)
        return x

    def back_start(self, x, n):
        return lax.ppermute(x, ("dp", "dq"), swap_pairs(self.sizes, ((1, 2), (2, 1))[n]))

    def back_end(self, x, got, n):
        bit = (self.low, self.high)[n]
        return jnp.where(bit == 0, jnp.concatenate([x, got]), jnp.concatenate([got, x]))


def in_hbm(x):
    return pltpu.with_memory_space_constraint(x, pltpu.HBM)


def tie(*groups):
    return lax.optimization_barrier(groups)


def local(
    sizes, tokens, out_grad, context_len, query_count, w_query, w_key, w_value, b_query, b_value, w_out, b_out,
    norm1_gain, norm1_bias, w_hidden, b_hidden, w_back, b_back, norm2_gain, norm2_bias,
):
    width = tokens.shape[1]
    ff = w_hidden.shape[1]
    ring = Ring(sizes)
    rows_of_tokens = tokens
    tokens, out_grad, w_query, w_key, w_value, w_hidden, w_back = [
        in_hbm(x) for x in (tokens, out_grad, w_query, w_key, w_value, w_hidden, w_back)
    ]
    core = ring.core.reshape(1).astype(jnp.int32)
    q, k, v, kt, att, lse = forward(
        context_len, query_count, tokens, w_query, w_key, w_value, b_query, b_value
    )
    output, ds, dbr, keep, send, vec = middle(
        core, context_len, query_count, tokens, out_grad, in_hbm(att), w_out, b_out, norm1_gain, norm1_bias,
        w_hidden, b_hidden, w_back, b_back, norm2_gain, norm2_bias,
    )
    got = ring.core_start(send)
    send, att, dbr = tie(send, att, dbr)
    datt, delta = attended_grad(att, dbr, w_out)
    got, datt, delta = tie(got, datt, delta)
    one, *sends = add_and_split(ring.where, keep, got)
    got_one = ring.plane_start(sends)
    one, ins = tie(one, (context_len, query_count, q, k, kt, v, datt, lse, delta))
    dq, dk, dv = backward(*ins)
    one, got_one, dq, dk, dv = tie(one, got_one, dq, dk, dv)
    one = ring.plane_end(one, got_one)
    got_one = ring.far_start(one, 0)
    one, dq, dk, dv = tie(one, dq, dk, dv)
    keep, small, *sends = projection_gradients(core, rows_of_tokens, dq, dk, dv, vec)
    got = [ring.core_start(s) for s in [small] + sends]
    one = one + got_one
    middle_row = one.shape[0] // 2
    got_one = [ring.far_start(x, 1) for x in (one[:middle_row], one[middle_row:])]
    two, *sends = add_and_split_small(ring.where, keep, small, *got)
    got_two = ring.plane_start(sends)
    one, two, sends, dq, dk, dv, ds = tie(one, two, sends, dq, dk, dv, ds)
    input_grad = input_gradient(in_hbm(ds), dq, dk, dv, w_query, w_key, w_value)
    one, got_one, two, got_two, input_grad = tie(one, got_one, two, got_two, input_grad)
    one = ring.rest(one + jnp.concatenate(got_one))
    got_one = ring.back_start(one, 0)
    two = ring.plane_end(two, got_two)
    got_two = ring.far_start(two, 0)
    one, got_one, two, got_two = tie(one, got_one, two, got_two)
    one = ring.back_end(one, got_one, 0)
    got_one = ring.back_start(one, 1)
    home_one = ring.core_start(one)
    two = two + got_two
    got_two = ring.far_start(two, 1)
    one, two, got_two = tie(one, two, got_two)
    two = ring.rest(two + got_two)
    small = two[-SMALL:]
    two = two[:-SMALL]
    vectors = [small[n] for n in (8, 9, 0, 1, 2)] + [small[3:5].reshape(-1)] + [small[n] for n in (5, 6, 7)]
    got_two = ring.back_start(two, 0)
    one, got_one, home_one, two, got_two = tie(one, got_one, home_one, two, got_two)
    two = ring.back_end(two, got_two, 0)
    got_two = ring.back_start(two, 1)
    home_two = ring.core_start(two)
    last_one = ring.core_start(got_one)
    places = [(0, ff, 0, 0, 0)]
    places += [(ff + n * width, width, 1, 0, n * width) for n in range(ff // width)]
    places += [(2 * ff, width, 2, 0, 0)]
    shapes = [(ff, width), (width, ff), (width, width)]
    gwb, gwh, gwo = unpack(
        places, shapes, ring.order, [in_hbm(x) for x in (one, got_one, home_one, last_one)]
    )
    two, got_two, home_two, gwb, gwh, gwo, vectors = tie(two, got_two, home_two, gwb, gwh, gwo, vectors)
    places = [(n * width, width, n, 0, 0) for n in range(3)]
    last_two = ring.core_start(got_two)
    shapes = [(width, width)] * 3
    squares = unpack(places, shapes, ring.order, (two, got_two, home_two))
    gq, gk, gv = unpack(places, shapes, ring.order, (last_two,), 3, squares)
    return (
        output,
        input_grad,
        gq,
        gk,
        gv,
        vectors[0],
        vectors[1],
        gwo,
        vectors[2],
        vectors[3],
        vectors[4],
        gwh,
        vectors[5],
        gwb,
        vectors[6],
        vectors[7],
        vectors[8],
    )


def cut(places, piece):
    out = []
    for start, rows, to, row, col in places:
        at = start
        while at < start + rows:
            end = min((at // piece + 1) * piece, start + rows)
            out.append((at, end - at, to, row + at - start, col))
            at = end
    return out


def solution(mesh):
    sizes = (mesh.shape["dp"], mesh.shape["dq"])
    return jax.shard_map(
        functools.partial(local, sizes),
        mesh=mesh,
        in_specs=(
            P(("dp", "dq"), None),
            P(("dp", "dq"), None),
            P(("dp", "dq"), None),
            P(("dp", "dq"), None),
            P(),
            P(),
            P(),
            P(),
            P(),
            P(),
            P(),
            P(),
            P(),
            P(),
            P(),
            P(),
            P(),
            P(),
            P(),
        ),
        out_specs=(
            P(("dp", "dq"), None),
            P(("dp", "dq"), None),
            P(),
            P(),
            P(),
            P(),
            P(),
            P(),
            P(),
            P(),
            P(),
            P(),
            P(),
            P(),
            P(),
            P(),
            P(),
        ),
        check_vma=False,
    )
```
